128 devices in a mesh: dp: 8 (over x, z_lo), seq: 16 (over y, z_hi, core).
Axes of the slice: x: 4, y: 4, z: 4 (z_hi: 2, z_lo: 2; z = z_hi * 2 + z_lo), core: 2. Of those that a mesh axis runs over, the one named last changes fastest.
Arguments:
- tokens: bfloat16 [8, 2048, 2048], P('dp', 'seq'), may hold values from -6 to 6
- cotangent: bfloat16 [8, 2048, 2048], P('dp', 'seq'), may hold values from -6 to 6
- w_qkv: float32 [2048, 2560], P(('dp', 'seq')), may hold values from -0.21875 to 0.21875
- w_out: float32 [2048, 2048], P(('dp', 'seq')), may hold values from -0.125 to 0.125
- w_gate_up: float32 [2048, 11264], P(('dp', 'seq')), may hold values from -0.125 to 0.125
- w_down_t: float32 [2048, 5632], P(('dp', 'seq')), may hold values from -0.078125 to 0.078125
- gains: float32 [2048, 2], P(('dp', 'seq')), may hold values from 0.5 to 1.5
- first_qkv: float32 [2048, 2560], P(('dp', 'seq')), may hold values from -224 to 224
- second_qkv: float32 [2048, 2560], P(('dp', 'seq')), may hold values from 819.2 to 16384
- first_out: float32 [2048, 2048], P(('dp', 'seq')), may hold values from -112 to 112
- second_out: float32 [2048, 2048], P(('dp', 'seq')), may hold values from 819.2 to 6553.6
- first_gate_up: float32 [2048, 11264], P(('dp', 'seq')), may hold values from -56 to 56
- second_gate_up: float32 [2048, 11264], P(('dp', 'seq')), may hold values from 163.84 to 1310.72
- first_down: float32 [2048, 5632], P(('dp', 'seq')), may hold values from -56 to 56
- second_down: float32 [2048, 5632], P(('dp', 'seq')), may hold values from 163.84 to 1310.72
- first_gains: float32 [2048, 2], P(('dp', 'seq')), may hold values from -112 to 112
- second_gains: float32 [2048, 2], P(('dp', 'seq')), may hold values from 819.2 to 6553.6
Outputs:
- block_out: bfloat16 [8, 2048, 2048], P('dp', 'seq')
- d_tokens: bfloat16 [8, 2048, 2048], P('dp', 'seq')
- new_first_qkv: float32 [2048, 2560], P(('dp', 'seq'))
- new_second_qkv: float32 [2048, 2560], P(('dp', 'seq'))
- new_w_qkv: float32 [2048, 2560], P(('dp', 'seq'))
- new_first_out: float32 [2048, 2048], P(('dp', 'seq'))
- new_second_out: float32 [2048, 2048], P(('dp', 'seq'))
- new_w_out: float32 [2048, 2048], P(('dp', 'seq'))
- new_first_gate_up: float32 [2048, 11264], P(('dp', 'seq'))
- new_second_gate_up: float32 [2048, 11264], P(('dp', 'seq'))
- new_w_gate_up: float32 [2048, 11264], P(('dp', 'seq'))
- new_first_down: float32 [2048, 5632], P(('dp', 'seq'))
- new_second_down: float32 [2048, 5632], P(('dp', 'seq'))
- new_w_down: float32 [2048, 5632], P(('dp', 'seq'))
- new_first_gains: float32 [2048, 2], P(('dp', 'seq'))
- new_second_gains: float32 [2048, 2], P(('dp', 'seq'))
- new_gains: float32 [2048, 2], P(('dp', 'seq'))
The draws below stay inside these ranges and needn't reach their ends.
All inputs are finite; a program needn't handle non-finite values.
Results may differ from the reference program's by a relative error of at most 0.034.
Values may be sent and summed in bfloat16 or wider, within the bound.
A program may use at most 320 MiB of HBM per device.

```python
import math
import jax
import jax.numpy as jnp
from jax import lax

D = 2048
HEADS = 32
KV_HEADS = 4
HEAD = 64
FF = 5632
STEP = 10
SEQS = 8
LENGTH = 2048
TOKENS = 16384


def block_scale(own_key, shape, cuts, low, high):
    def one(dim, shards_of):
        steps = jax.random.uniform(jax.random.fold_in(jax.random.fold_in(own_key, 6), dim), (shards_of,), jnp.float32, low / len(cuts), high / len(cuts))
        return jnp.repeat(jnp.exp(steps), shape[dim] // shards_of).reshape((-1,) + (1,) * (len(shape) - dim - 1))

    loudness = one(*cuts[0])
    for cut in cuts[1:]:
        loudness = loudness * one(*cut)
    return loudness


def centred(rng, shape, spread, bound, cuts=(), held_as=jnp.bfloat16):
    array = jax.random.normal(rng, shape, jnp.float32) * spread
    if len(cuts) > 0:
        array = block_scale(rng, shape, cuts, -0.22, 0.18) * array
    return jnp.clip(array, min=-bound, max=bound).astype(held_as)


def setup_inputs(seed: int = 0) -> dict:
    streams_of = jax.random.split(jax.random.key(seed), 18)
    return {
        "tokens": centred(streams_of[0], (SEQS, LENGTH, D), 1.0, 6.0, ((0, 8), (1, 16))),
        "cotangent": centred(streams_of[1], (SEQS, LENGTH, D), 1.0, 6.0, ((0, 8), (1, 16))),
        "w_qkv": centred(streams_of[2], (D, D + 2 * KV_HEADS * HEAD), (D * 2 // 5) ** -0.5, 0.21875, ((0, 128),), jnp.float32),
        "w_out": centred(streams_of[3], (D, D), D ** -0.5, 0.125, ((0, 128),), jnp.float32),
        "w_gate_up": centred(streams_of[4], (D, 2 * FF), D ** -0.5, 0.125, ((0, 128),), jnp.float32),
        "w_down_t": centred(streams_of[5], (D, FF), FF ** -0.5, 0.078125, ((0, 128),), jnp.float32),
        "gains": jnp.clip(1.0 + 0.1 * jax.random.normal(streams_of[6], (D, 2), jnp.float32), 0.5, 1.5),
        "first_qkv": centred(streams_of[7], (D, D + 2 * KV_HEADS * HEAD), (0.3 * TOKENS ** 0.5), 224.0, ((0, 128),), jnp.float32),
        "second_qkv": jnp.clip(jnp.exp(math.log(16384.0) - 2.9957323 * jax.random.uniform(streams_of[8], (D, D + 2 * KV_HEADS * HEAD), jnp.float32) ** block_scale(streams_of[8], (D, D + 2 * KV_HEADS * HEAD), ((0, 128),), -0.2, 0.2)), 819.2, 16384.0),
        "first_out": centred(streams_of[9], (D, D), (0.15 * TOKENS ** 0.5), 112.0, ((0, 128),), jnp.float32),
        "second_out": jnp.clip(jnp.exp(math.log(6553.6) - 2.0794415 * jax.random.uniform(streams_of[10], (D, D), jnp.float32) ** block_scale(streams_of[10], (D, D), ((0, 128),), -0.2, 0.2)), 819.2, 6553.6),
        "first_gate_up": centred(streams_of[11], (D, 2 * FF), (0.07 * TOKENS ** 0.5), 56.0, ((0, 128),), jnp.float32),
        "second_gate_up": jnp.clip(jnp.exp(math.log(1310.72) - 2.0794415 * jax.random.uniform(streams_of[12], (D, 2 * FF), jnp.float32) ** block_scale(streams_of[12], (D, 2 * FF), ((0, 128),), -0.2, 0.2)), 163.84, 1310.72),
        "first_down": centred(streams_of[13], (D, FF), (0.07 * TOKENS ** 0.5), 56.0, ((0, 128),), jnp.float32),
        "second_down": jnp.clip(jnp.exp(math.log(1310.72) - 2.0794415 * jax.random.uniform(streams_of[14], (D, FF), jnp.float32) ** block_scale(streams_of[14], (D, FF), ((0, 128),), -0.2, 0.2)), 163.84, 1310.72),
        "first_gains": centred(streams_of[15], (D, 2), (0.15 * TOKENS ** 0.5), 112.0, ((0, 128),), jnp.float32),
        "second_gains": jnp.clip(jnp.exp(math.log(6553.6) - 2.0794415 * jax.random.uniform(streams_of[16], (D, 2), jnp.float32) ** block_scale(streams_of[16], (D, 2), ((0, 128),), -0.2, 0.2)), 819.2, 6553.6),
    }


@jax.custom_vjp
def low(v):
    return lax.optimization_barrier(v.astype(jnp.bfloat16)).astype(jnp.float32)

@jax.custom_vjp
def low_back(v):
    return v

def low_keep(v):
    return (low(v), None)

def low_pass(kept, grad):
    return (grad,)

def back_keep(v):
    return (v, None)

def back_low(kept, grad):
    return (low(grad),)
low.defvjp(low_keep, low_pass)
low_back.defvjp(back_keep, back_low)
norm_eps = 1e-05
rope_base = 10000.0
mask_fill = -1e+30
beta_one = 0.9
beta_two = 0.95
adam_eps = 1e-08
decay_rate = 0.1
rate_matrix = 0.08
rate_gain = 0.8

def product(left_side, right_side):
    return jnp.dot(left_side, right_side, precision=lax.Precision.HIGHEST, preferred_element_type=jnp.float32)

def rope_tables(length):
    half_width = HEAD // 2
    frequency = jnp.exp(jnp.arange(half_width, dtype=jnp.float32) * (-2.0 * math.log(rope_base) / HEAD))
    angles = jnp.arange(length, dtype=jnp.float32)[:, None] * frequency[None, :]
    angles = jnp.concatenate([angles, angles], axis=1)
    return (jnp.cos(angles), jnp.sin(angles))

def rotate(values, cos_table, sin_table):
    half_width = values.shape[-1] // 2
    turned = jnp.concatenate([-values[..., half_width:], values[..., :half_width]], axis=-1)
    return values * cos_table + turned * sin_table

def rms_scale(values, gain_col):
    return values * lax.rsqrt(lax.optimization_barrier(jnp.mean(values * values, axis=-1, keepdims=True)) + norm_eps) * gain_col

def attention(queries, keys_rot, values):
    length = queries.shape[0]
    group_size = HEADS // KV_HEADS
    key_heads = jnp.repeat(keys_rot, group_size, axis=1)
    value_heads = jnp.repeat(values, group_size, axis=1)
    block_rows = min(512, length)
    score_scale = HEAD ** (-0.5)
    key_pos = jnp.arange(length, dtype=jnp.int32)

    def one_block(offset):
        query_block = lax.dynamic_slice_in_dim(queries, offset, block_rows, 0)
        scores = jnp.einsum('bhe,lhe->hbl', query_block, key_heads, precision=lax.Precision.HIGHEST) * score_scale
        scores = low_back(scores)
        query_pos = offset + jnp.arange(block_rows, dtype=jnp.int32)
        scores = jnp.where(key_pos[None, None, :] <= query_pos[None, :, None], scores, mask_fill)
        totals = jax.nn.logsumexp(scores, axis=-1, keepdims=True)
        attn_probs = low(jnp.exp(scores - totals))
        return jnp.einsum('hbl,lhe->bhe', attn_probs, value_heads, precision=lax.Precision.HIGHEST)
    offsets = jnp.arange(length // block_rows, dtype=jnp.int32) * block_rows
    blocks = lax.map(jax.checkpoint(one_block), offsets)
    return blocks.reshape(length, HEADS * HEAD)

def layer(inputs, w_qkv, w_out, w_gate_up, w_down_t, gains):
    length = inputs.shape[0]
    kv_width = KV_HEADS * HEAD
    gain_low = low(gains)
    acts_in = low(rms_scale(inputs, gain_low[:, 0]))
    qkv_rows = low(low_back(product(acts_in, low(w_qkv))))
    cos_table, sin_table = rope_tables(length)
    queries = qkv_rows[:, :D].reshape(length, HEADS, HEAD)
    key_part = qkv_rows[:, D:D + kv_width].reshape(length, KV_HEADS, HEAD)
    value_part = qkv_rows[:, D + kv_width:].reshape(length, KV_HEADS, HEAD)
    queries = low(rotate(queries, cos_table[:, None, :], sin_table[:, None, :]))
    key_part = low(rotate(key_part, cos_table[:, None, :], sin_table[:, None, :]))
    mixed_rows = low(low_back(attention(queries, key_part, value_part)))
    resid_mid = inputs + low_back(product(mixed_rows, low(w_out)))
    acts_mid = low(rms_scale(resid_mid, gain_low[:, 1]))
    gate_up = low_back(product(acts_mid, low(w_gate_up)))
    hidden = low(jax.nn.silu(gate_up[:, :FF]) * gate_up[:, FF:])
    return resid_mid + jnp.dot(hidden, low(w_down_t).T, precision=lax.Precision.HIGHEST, preferred_element_type=jnp.float32)

def adam(weight, gradient, first_moment, second, step_rate, decay_weight):
    first_new = beta_one * first_moment + (1.0 - beta_one) * gradient
    second_new = beta_two * second + (1.0 - beta_two) * gradient * gradient
    first_hat = first_new / (1.0 - beta_one ** STEP)
    second_hat = second_new / (1.0 - beta_two ** STEP)
    weight_new = weight - step_rate * (first_hat / (jnp.sqrt(second_hat) + adam_eps) + decay_weight * weight)
    return (first_new, second_new, weight_new)

def reference(tokens, cotangent, w_qkv, w_out, w_gate_up, w_down_t, gains, first_qkv, second_qkv, first_out, second_out, first_gate_up, second_gate_up, first_down, second_down, first_gains, second_gains):
    params = (w_qkv, w_out, w_gate_up, w_down_t, gains)

    def one_seq(carried, seq_pair):
        seq_in, seq_back = seq_pair
        result, pull_back = jax.vjp(layer, seq_in.astype(jnp.float32), *params)
        grads_all = pull_back(seq_back.astype(jnp.float32))
        summed = tuple((acc + new_grad for acc, new_grad in zip(carried, grads_all[1:])))
        return (summed, (result.astype(jnp.bfloat16), grads_all[0].astype(jnp.bfloat16)))
    zero_grads = tuple((jnp.zeros(weight.shape, jnp.float32) for weight in params))
    totals, (outputs, d_tok) = lax.scan(one_seq, zero_grads, (tokens, cotangent))
    first_q, second_q, weight_q = adam(w_qkv, totals[0], first_qkv, second_qkv, rate_matrix, decay_rate)
    first_o, second_o, weight_o = adam(w_out, totals[1], first_out, second_out, rate_matrix, decay_rate)
    first_g, second_g, weight_g = adam(w_gate_up, totals[2], first_gate_up, second_gate_up, rate_matrix, decay_rate)
    first_d, second_d, weight_d = adam(w_down_t, totals[3], first_down, second_down, rate_matrix, decay_rate)
    first_n, second_n, weight_n = adam(gains, totals[4], first_gains, second_gains, rate_gain, 0.0)
    return (outputs, d_tok, first_q, second_q, weight_q, first_o, second_o, weight_o, first_g, second_g, weight_g, first_d, second_d, weight_d, first_n, second_n, weight_n)
```

```python
import functools
import math

import jax
import jax.numpy as jnp
import numpy as np
from jax import lax
from jax.experimental import pallas as pl
from jax.experimental.pallas import tpu as pltpu
from jax.sharding import Mesh
from jax.sharding import PartitionSpec as P

D = 2048
HEAD = 64
FF = 5632
STEP = 10
SEG = FF // 8
QKV = 512

norm_eps = 1e-05
rope_base = 10000.0
mask_fill = -1e30
beta_one = 0.9
beta_two = 0.95
adam_eps = 1e-08
decay_rate = 0.1
rate_matrix = 0.08
rate_gain = 0.8

BF = jnp.bfloat16
F32 = jnp.float32
MESH = pl.DeviceIdType.MESH
ANY = pl.BlockSpec(memory_space=pl.ANY)
VM = pl.BlockSpec(memory_space=pltpu.VMEM)
VLIMIT = 56 * 2**20


def shaped(*shape, dtype=BF):
    return jax.ShapeDtypeStruct(shape, dtype)


class Place:
    def __init__(self):
        self.x, self.zlo, self.y = (lax.axis_index(a) for a in ("x", "zlo", "y"))
        self.zhi, self.core = lax.axis_index("zhi"), lax.axis_index("core")
        self.z = self.zhi * 2 + self.zlo
        self.t = self.y * 2 + self.core
        self.sib = {"core": 1 - self.core}
        self.right = {"y": lax.rem(self.y + 1, 4)}
        self.left = {"y": lax.rem(self.y + 3, 4)}
        self.zpart = {"zhi": 1 - self.zhi}

    def xs(self, step):
        return lax.rem(self.x + step, 4)

    def ys(self, step):
        return lax.rem(self.y + step, 4)

    def zs(self, step):
        z = lax.rem(self.z + step, 4)
        return lax.div(z, 2), lax.rem(z, 2)

    def xpeers(self):
        return [{"x": self.xs(i)} for i in (1, 2, 3)]

    def zpeers(self):
        out = []
        for i in (1, 2, 3):
            zhi, zlo = self.zs(i)
            out.append({"zhi": zhi, "zlo": zlo})
        return out

    def tpeers(self):
        return [
            {"y": self.ys(dy), "core": lax.rem(self.core + dc, 2)}
            for dy in range(4)
            for dc in range(2)
            if (dy, dc) != (0, 0)
        ]

    def plane(self):
        out = []
        for dx in range(4):
            for dz in range(4):
                for dc in range(2):
                    if (dx, dz, dc) != (0, 0, 0):
                        zhi, zlo = self.zs(dz)
                        out.append(
                            {"x": self.xs(dx), "zhi": zhi, "zlo": zlo, "core": lax.rem(self.core + dc, 2)}
                        )
        return out


def greet(peers):
    barrier = pltpu.get_barrier_semaphore()
    for peer in peers:
        pl.semaphore_signal(barrier, inc=1, device_id=peer, device_id_type=MESH)
    pl.semaphore_wait(barrier, len(peers))


class Net:
    def __init__(self, send, recv, local):
        self.send, self.recv, self.loc = send, recv, local
        self.n = 0
        self.m = 0

    def block(self, count):
        first = self.n
        self.n += count
        return first

    def make(self, src, dst, peer, at=None):
        if at is None:
            at = self.block(1)
        return pltpu.make_async_remote_copy(
            src, dst, self.send.at[at], self.recv.at[at], device_id=peer, device_id_type=MESH
        )

    def go(self, src, dst, peer, at=None):
        copy = self.make(src, dst, peer, at)
        copy.start()
        return copy

    def local(self, src, dst):
        copy = pltpu.make_async_copy(src, dst, self.loc.at[self.m])
        self.m += 1
        copy.start()
        return copy


def sems(remote, local):
    return [
        pltpu.SemaphoreType.DMA((remote,)),
        pltpu.SemaphoreType.DMA((remote,)),
        pltpu.SemaphoreType.DMA((max(local, 1),)),
    ]


class Gather:
    def __init__(self, net, pos, src, out):
        self.net, self.pos, self.src, self.out = net, pos, src, out

    def start(self):
        net, pos, src = self.net, self.pos, self.src
        mine = self.out.at[pos.t]
        lo, hi = pl.ds(0, 64), pl.ds(64, 64)
        self.own = net.local(src, mine)
        self.r = [net.go(src.at[lo], mine.at[lo], pos.right), None]
        self.l = [net.go(src.at[hi], mine.at[hi], pos.left), None]
        self.r[1] = net.go(src.at[hi], mine.at[hi], pos.right)
        self.l[1] = net.go(src.at[lo], mine.at[lo], pos.left)
        self.s = [net.go(src, mine, pos.sib)]

    def step(self):
        net, pos, out = self.net, self.pos, self.out
        lo, hi = pl.ds(0, 64), pl.ds(64, 64)
        from_left = out.at[pos.ys(3) * 2 + pos.core]
        from_right = out.at[pos.ys(1) * 2 + pos.core]
        self.r[0].wait_recv()
        self.r2 = net.go(from_left.at[lo], from_left.at[lo], pos.right)
        self.l[0].wait_recv()
        self.l2 = net.go(from_right.at[hi], from_right.at[hi], pos.left)
        self.r[1].wait_recv()
        self.s.append(net.go(from_left, from_left, pos.sib))
        self.l[1].wait_recv()
        self.s.append(net.go(from_right, from_right, pos.sib))

    def last(self):
        net, pos = self.net, self.pos
        far = self.out.at[pos.ys(2) * 2 + pos.core]
        lo, hi = pl.ds(0, 64), pl.ds(64, 64)
        self.r2.wait_recv()
        self.s.append(net.go(far.at[lo], far.at[lo], pos.sib))
        self.l2.wait_recv()
        self.s.append(net.go(far.at[hi], far.at[hi], pos.sib))

    def finish(self):
        for copy in self.r + self.l + [self.r2, self.l2]:
            copy.wait_send()
        for copy in self.s:
            copy.wait()
        self.own.wait()


GATHER_SEMS = 11


class Scatter:
    def __init__(self, net, pos, part, scratch):
        self.net, self.pos, self.part = net, pos, part
        self.sib, self.opp, self.nb, self.far, self.near = scratch

    def start(self):
        net, pos = self.net, self.pos
        self.c = {}
        for dy in (2, 1, 3, 0):
            self.c[dy] = net.go(
                self.part.at[pos.ys(dy) * 2 + 1 - pos.core], self.sib.at[dy], pos.sib
            )

    def _add(self, dst, dy, rows):
        pos = self.pos
        one = self.part[pos.ys(dy) * 2 + pos.core, rows].astype(F32)
        dst[rows] = (one + self.sib[dy, rows].astype(F32)).astype(BF)

    def step(self):
        net, pos = self.net, self.pos
        lo, hi = pl.ds(0, 64), pl.ds(64, 64)
        self.c[2].wait_recv()
        self._add(self.far, 2, lo)
        self.f0 = net.go(self.far.at[lo], self.opp.at[0], pos.right)
        self._add(self.far, 2, hi)
        self.f1 = net.go(self.far.at[hi], self.opp.at[1], pos.left)
        self.c[1].wait_recv()
        self._add(self.near.at[0], 1, hi)
        self.r1 = net.go(self.near.at[0, hi], self.nb.at[0, hi], pos.right)
        self.c[3].wait_recv()
        self._add(self.near.at[1], 3, lo)
        self.l0 = net.go(self.near.at[1, lo], self.nb.at[1, lo], pos.left)
        self._add(self.near.at[0], 1, lo)
        self._add(self.near.at[1], 3, hi)

    def last(self):
        net, pos = self.net, self.pos
        lo, hi = pl.ds(0, 64), pl.ds(64, 64)
        self.f0.wait_recv()
        self.near[0, lo] = (self.near[0, lo].astype(F32) + self.opp[0].astype(F32)).astype(BF)
        self.r0 = net.go(self.near.at[0, lo], self.nb.at[0, lo], pos.right)
        self.f1.wait_recv()
        self.near[1, hi] = (self.near[1, hi].astype(F32) + self.opp[1].astype(F32)).astype(BF)
        self.l1 = net.go(self.near.at[1, hi], self.nb.at[1, hi], pos.left)

    def arrive(self):
        for copy in (self.r1, self.l0, self.r0, self.l1, self.c[0]):
            copy.wait_recv()

    def total(self, rows):
        pos = self.pos
        out = self.part[pos.t, rows].astype(F32) + self.sib[0, rows].astype(F32)
        return out + self.nb[0, rows].astype(F32) + self.nb[1, rows].astype(F32)

    def finish(self):
        for copy in (self.f0, self.f1, self.r0, self.r1, self.l0, self.l1):
            copy.wait_send()
        for copy in self.c.values():
            copy.wait_send()


SCATTER_SEMS = 10


def scatter_scratch():
    return [
        pltpu.VMEM((4, 128, D), BF),
        pltpu.VMEM((2, 64, D), BF),
        pltpu.VMEM((2, 128, D), BF),
        pltpu.VMEM((128, D), BF),
        pltpu.VMEM((2, 128, D), BF),
    ]


def first_kernel(
    n_ref, wq_ref, wr_ref, nf_ref, wqf_ref, ra_ref, rb_ref, own_ref, send, recv, local
):
    pos, net = Place(), Net(send, recv, local)
    tpeers, xpeers, zpeers = pos.tpeers(), pos.xpeers(), pos.zpeers()
    greet(tpeers + xpeers + zpeers)
    x, y, zlo, zhi, core = pos.x, pos.y, pos.zlo, pos.zhi, pos.core
    low, high = pl.ds(0, 2), pl.ds(2, 2)

    small = []
    for peer in tpeers:
        t = peer["y"] * 2 + peer["core"]
        small.append(net.go(wq_ref.at[t], wqf_ref.at[x, zlo, y, zhi, core], peer))
    mine = net.local(wq_ref.at[pos.t], wqf_ref.at[x, zlo, y, zhi, core])
    gather = Gather(net, pos, n_ref, nf_ref)
    gather.start()
    large = []
    for peer in tpeers:
        t = peer["y"] * 2 + peer["core"]
        large.append(net.go(wr_ref.at[t], own_ref.at[:, y, core], peer))
    mine_large = net.local(wr_ref.at[pos.t], own_ref.at[:, y, core])

    mine.wait()
    for copy in small:
        copy.wait_recv()
    one = []
    for peer in xpeers:
        part = wqf_ref.at[x, zlo, low, zhi]
        one.append(net.go(part, part, peer))
    for peer in zpeers:
        part = wqf_ref.at[x, zlo, high, zhi]
        one.append(net.go(part, part, peer))

    gather.step()

    for copy in one:
        copy.wait_recv()
    two = []
    for peer in zpeers:
        part = wqf_ref.at[:, zlo, low, zhi]
        two.append(net.go(part, part, peer))
    for peer in xpeers:
        part = wqf_ref.at[x, :, high, :]
        two.append(net.go(part, part, peer))

    mine_large.wait()
    for copy in large:
        copy.wait_recv()
    three = []
    for peer in xpeers:
        three.append(net.go(own_ref.at[:, low], ra_ref.at[:, x], peer))
    for peer in zpeers:
        three.append(net.go(own_ref.at[:, high], rb_ref.at[:, zlo, :, zhi], peer))
    keep = [
        net.local(own_ref.at[:, low], ra_ref.at[:, x]),
        net.local(own_ref.at[:, high], rb_ref.at[:, zlo, :, zhi]),
    ]

    gather.last()
    gather.finish()
    for copy in small + large + one:
        copy.wait_send()
    for copy in two + three:
        copy.wait()
    for copy in keep:
        copy.wait()


def run_first(normed, wq_blocks, wr_blocks):
    return pl.pallas_call(
        first_kernel,
        out_shape=(
            shaped(8, 128, D),
            shaped(4, 2, 4, 2, 2, 16, QKV),
            shaped(3, 4, 2, 2, 16, SEG),
            shaped(3, 2, 2, 2, 2, 16, SEG),
        ),
        in_specs=[VM, ANY, ANY],
        out_specs=(VM, ANY, ANY, ANY),
        scratch_shapes=[pltpu.VMEM((3, 4, 2, 16, SEG), BF)] + sems(7 + 7 + 18 + GATHER_SEMS, 6),
        compiler_params=pltpu.CompilerParams(
            collective_id=0, has_side_effects=True, vmem_limit_bytes=VLIMIT
        ),
        name="first",
    )(normed, wq_blocks, wr_blocks)


def dot_nt(a, b):
    return lax.dot_general(a, b, (((1,), (1,)), ((), ())), preferred_element_type=F32)


def dot_tn(a, b):
    return lax.dot_general(a, b, (((0,), (0,)), ((), ())), preferred_element_type=F32)


def dot_nn(a, b):
    return lax.dot_general(a, b, (((1,), (0,)), ((), ())), preferred_element_type=F32)


def first_half_mask(shape):
    return (lax.broadcasted_iota(jnp.int32, shape, 1) & 63) < 32


def turn(u, cos, sin):
    rot = jnp.where(first_half_mask(u.shape), -pltpu.roll(u, 96, 1), pltpu.roll(u, 32, 1))
    return u * cos + rot * sin


def turn_back(u, cos, sin):
    v = u * sin
    rot = jnp.where(first_half_mask(u.shape), pltpu.roll(v, 96, 1), -pltpu.roll(v, 32, 1))
    return u * cos + rot


def lane_first(shape):
    return lax.broadcasted_iota(jnp.int32, shape, 1) < 64


def causal(zhi):
    key = lax.broadcasted_iota(jnp.int32, (512, 512), 0)
    query = (lax.broadcasted_iota(jnp.int32, (512, 512), 1) & 255) + zhi * 256
    return key <= query


class Spread:
    def __init__(self, net, pos, ra, rb, outs):
        self.net, self.pos, self.ra, self.rb, self.outs = net, pos, ra, rb, outs

    def start(self):
        net, pos = self.net, self.pos
        x, zlo, zhi = pos.x, pos.zlo, pos.zhi
        low, high = pl.ds(0, 2), pl.ds(2, 2)
        self.copies, self.keep = [], []
        for i, out in self.outs:
            part_a, part_b = out.at[:, zlo, low, zhi], out.at[x, :, high, :]
            src_a, src_b = self.ra.at[i], self.rb.at[i]
            for za, xb in zip(pos.zpeers(), pos.xpeers()):
                self.copies.append(net.go(src_a, part_a, za))
                self.copies.append(net.go(src_b, part_b, xb))
            self.keep += [net.local(src_a, part_a), net.local(src_b, part_b)]

    def finish(self):
        for copy in self.copies + self.keep:
            copy.wait()


class OutRows:
    def __init__(self, net, pos, src, out):
        self.net, self.pos, self.src, self.out = net, pos, src, out
        self.base = net.block(32)

    def _pairs(self):
        pos = self.pos
        for dx in range(4):
            for dz in range(4):
                yield dx, dz, pos.xs(dx), pos.zs(dz)

    def start(self):
        pos, net = self.pos, self.net
        half = lax.div(pos.x, 2)
        dst = self.out.at[lax.rem(pos.x, 2) * 2 + pos.zlo, pos.zhi, pos.core]
        for dx, dz, x, (zhi, zlo) in self._pairs():
            peer = {"x": x, "zhi": zhi, "zlo": zlo, "core": half}
            at = self.base + (dx * 4 + dz) * 2 + pos.core
            if (dx, dz) == (0, 0):

                @pl.when(half == pos.core)
                def _():
                    pltpu.make_async_copy(self.src, dst, net.loc.at[net.loc.shape[0] - 1]).start()

                @pl.when(half != pos.core)
                def _():
                    net.make(self.src, dst, peer, at).start()
            else:
                net.make(self.src, dst, peer, at).start()

    def finish(self):
        pos, net = self.pos, self.net
        half = lax.div(pos.x, 2)
        dst = self.out.at[lax.rem(pos.x, 2) * 2 + pos.zlo, pos.zhi, pos.core]
        for dx, dz, x, (zhi, zlo) in self._pairs():
            peer = {"x": x, "zhi": zhi, "zlo": zlo, "core": half}
            at = self.base + (dx * 4 + dz) * 2 + pos.core
            first = (dx, dz) == (0, 0)
            if first:

                @pl.when(half == pos.core)
                def _():
                    pltpu.make_async_copy(self.src, dst, net.loc.at[net.loc.shape[0] - 1]).wait()

                @pl.when(half != pos.core)
                def _():
                    net.make(self.src, dst, peer, at).wait_send()
            else:
                net.make(self.src, dst, peer, at).wait_send()
            back = lax.rem(pos.x + 4 - dx, 4)

            @pl.when(lax.div(back, 2) == pos.core)
            def _():
                for core in range(2):
                    slot = self.base + (dx * 4 + dz) * 2 + core
                    if first:

                        @pl.when(pos.core != core)
                        def _():
                            net.make(self.src, dst, peer, slot).wait_recv()
                    else:
                        net.make(self.src, dst, peer, slot).wait_recv()


def attend_kernel(
    qkv_ref, cos_ref, sin_ref, wout_ref, ra_ref, rb_ref, cot_ref,
    o_ref, lse_ref, q_ref, kv_ref, wg_ref, wu_ref, wd_ref, wo_ref, cotf_ref,
    k_ref, v_ref, send, recv, local,
):
    pos, net = Place(), Net(send, recv, local)
    zhi = pos.zhi
    greet(pos.plane() + [pos.right, pos.left])
    gather = Gather(net, pos, cot_ref, cotf_ref)
    spread = Spread(net, pos, ra_ref, rb_ref, [(2, wd_ref), (0, wg_ref), (1, wu_ref)])
    rows = OutRows(net, pos, wout_ref, wo_ref)

    swap = net.block(4)
    for j in range(4):
        r = pl.ds(j * 256, 256)
        cos, sin = cos_ref[r], sin_ref[r]
        for c in range(2):
            kv = qkv_ref[r, 256 + c * 128 : 384 + c * 128].astype(F32)
            mixed = jnp.where(lane_first(kv.shape), turn(kv, cos, sin), kv)
            kv_ref[j, zhi, :, c * 128 : (c + 1) * 128] = mixed.astype(BF)
        net.go(kv_ref.at[j, zhi], kv_ref.at[j, zhi], pos.zpart, swap + j)
    rows.start()
    spread.start()
    gather.start()
    for j in range(4):
        r = pl.ds(j * 256, 256)
        cos, sin = cos_ref[r], sin_ref[r]
        for c in range(2):
            q = turn(qkv_ref[r, c * 128 : (c + 1) * 128].astype(F32), cos, sin)
            q = q.astype(BF) * jnp.asarray(HEAD**-0.5, BF)
            q_ref[j, c, 0:256] = q[:, 0:64]
            q_ref[j, c, 256:512] = q[:, 64:128]

    def update(c, key_at, query, state, mask):
        top, norm, acc = state
        s = dot_nt(k_ref[c, key_at], query)
        if mask is not None:
            s = jnp.where(mask, s, mask_fill)
        new = jnp.maximum(top, jnp.max(s, axis=0, keepdims=True))
        p = jnp.exp(s - new)
        keep = jnp.exp(top - new)
        norm = norm * keep + jnp.sum(p, axis=0, keepdims=True)
        acc = acc * keep + dot_tn(v_ref[c, key_at], p.astype(BF))
        return new, norm, acc

    def block(qb, _):
        part = kv_ref.at[qb, zhi]
        net.make(part, part, pos.zpart, swap + qb).wait_recv()
        kv = kv_ref[qb].reshape(512, 256)
        for c in range(2):
            k_ref[c, qb] = kv[:, c * 128 : c * 128 + 64]
            v_ref[c, qb] = kv[:, c * 128 + 64 : c * 128 + 128]
        mask = causal(zhi)
        state = []
        for c in range(2):
            zero = (
                jnp.full((1, 512), mask_fill, F32),
                jnp.zeros((1, 512), F32),
                jnp.zeros((64, 512), F32),
            )
            state.append(update(c, qb, q_ref[qb, c], zero, mask))

        def more(j, held):
            return tuple(update(c, j, q_ref[qb, c], held[c], None) for c in range(2))

        state = lax.fori_loop(0, qb, more, tuple(state))
        for c in range(2):
            top, norm, acc = state[c]
            lse_ref[qb, c] = top + jnp.log(norm)
            out = (acc / norm).T
            pair = jnp.concatenate([out[0:256], out[256:512]], axis=1)
            o_ref[qb, :, c * 128 : (c + 1) * 128] = pair.astype(BF)
        return 0

    block(0, 0)
    gather.step()
    lax.fori_loop(1, 3, block, 0)
    gather.last()
    block(3, 0)
    gather.finish()
    spread.finish()
    rows.finish()
    for j in range(4):
        part = kv_ref.at[j, zhi]
        net.make(part, part, pos.zpart, swap + j).wait_send()


def run_attend(qkv, cos, sin, wout, ra, rb, cot):
    full = shaped(4, 2, 4, 2, 2, 16, SEG)
    return pl.pallas_call(
        attend_kernel,
        out_shape=(
            shaped(4, 256, 256),
            shaped(4, 2, 1, 512, dtype=F32),
            shaped(4, 2, 512, 64),
            shaped(4, 2, 256, 256),
            full,
            full,
            full,
            shaped(4, 2, 2, 16, D),
            shaped(8, 128, D),
        ),
        in_specs=[VM, VM, VM, ANY, ANY, ANY, ANY],
        out_specs=(VM, VM, VM, VM, ANY, ANY, ANY, ANY, ANY),
        scratch_shapes=[pltpu.VMEM((2, 4, 512, 64), BF), pltpu.VMEM((2, 4, 512, 64), BF)]
        + sems(4 + 18 + 32 + GATHER_SEMS, 9),
        compiler_params=pltpu.CompilerParams(
            collective_id=1, has_side_effects=True, vmem_limit_bytes=VLIMIT
        ),
        name="attend",
    )(qkv, cos, sin, wout, ra, rb, cot)


def mid_kernel(
    part_ref, tok_ref, resid_ref, full_ref, a, b, c, d, e, blk, send, recv, local
):
    pos, net = Place(), Net(send, recv, local)
    greet([pos.sib, pos.right, pos.left])
    sc = Scatter(net, pos, part_ref, (a, b, c, d, e))
    sc.start()
    sc.step()
    sc.last()
    sc.arrive()

    @pl.loop(0, 8)
    def _(i):
        rows = pl.ds(pl.multiple_of(i * 16, 16), 16)
        r = sc.total(rows) + tok_ref[rows].astype(F32)
        resid_ref[rows] = r
        inv = lax.rsqrt(jnp.mean(r * r, axis=-1, keepdims=True) + norm_eps)
        blk[rows] = (r * inv).astype(BF)

    gather = Gather(net, pos, blk, full_ref)
    gather.start()
    sc.finish()
    gather.step()
    gather.last()
    gather.finish()


def run_mid(part, tok):
    return pl.pallas_call(
        mid_kernel,
        out_shape=(shaped(128, D, dtype=F32), shaped(8, 128, D)),
        in_specs=[VM, VM],
        out_specs=(VM, VM),
        scratch_shapes=scatter_scratch()
        + [pltpu.VMEM((128, D), BF)]
        + sems(SCATTER_SEMS + GATHER_SEMS, 1),
        compiler_params=pltpu.CompilerParams(
            collective_id=2, has_side_effects=True, vmem_limit_bytes=VLIMIT
        ),
        name="mid",
    )(part, tok)


def norm_back(t, r, back):
    inv = lax.rsqrt(jnp.mean(r * r, axis=-1, keepdims=True) + norm_eps)
    normed = r * inv
    return back + inv * (t - normed * jnp.mean(t * normed, axis=-1, keepdims=True))


def back_kernel(
    part_ref, resid_ref, cot_ref, dmid_ref, full_ref, a, b, c, d, e, blk, send, recv, local
):
    pos, net = Place(), Net(send, recv, local)
    greet([pos.sib, pos.right, pos.left])
    sc = Scatter(net, pos, part_ref, (a, b, c, d, e))
    sc.start()
    sc.step()
    sc.last()
    sc.arrive()

    @pl.loop(0, 8)
    def _(i):
        rows = pl.ds(pl.multiple_of(i * 16, 16), 16)
        dmid = norm_back(sc.total(rows), resid_ref[rows], cot_ref[rows].astype(F32))
        dmid_ref[rows] = dmid
        blk[rows] = dmid.astype(BF)

    gather = Gather(net, pos, blk, full_ref)
    gather.start()
    sc.finish()
    gather.step()
    gather.last()
    gather.finish()


def run_back(part, resid, cot):
    return pl.pallas_call(
        back_kernel,
        out_shape=(shaped(128, D, dtype=F32), shaped(8, 128, D)),
        in_specs=[VM, VM, VM],
        out_specs=(VM, VM),
        scratch_shapes=scatter_scratch()
        + [pltpu.VMEM((128, D), BF)]
        + sems(SCATTER_SEMS + GATHER_SEMS, 1),
        compiler_params=pltpu.CompilerParams(
            collective_id=3, has_side_effects=True, vmem_limit_bytes=VLIMIT
        ),
        name="back",
    )(part, resid, cot)


class Fold:
    def __init__(self, net, pos, src, scratch):
        self.net, self.pos, self.src = net, pos, src
        self.ra, self.rb, self.sa, self.sb, self.ta, self.tb = scratch

    def start(self):
        net, pos, src = self.net, self.pos, self.src
        low, high = pl.ds(0, 2), pl.ds(2, 2)
        self.one = []
        for i, (za, xb) in enumerate(zip(pos.zpeers(), pos.xpeers())):
            self.one.append(net.go(src.at[:, za["zlo"], low, za["zhi"]], self.ra.at[i], za))
            self.one.append(net.go(src.at[xb["x"], :, high, :], self.rb.at[i], xb))
        self.keep = [
            net.local(src.at[:, pos.zlo, low, pos.zhi], self.sa),
            net.local(src.at[pos.x, :, high, :], self.sb),
        ]

    def step(self):
        net, pos = self.net, self.pos
        for copy in self.keep:
            copy.wait()
        for copy in self.one:
            copy.wait_recv()

        @pl.loop(0, 4)
        def _(i):
            for j in range(2):
                here = self.sa[i, j].astype(F32)
                for k in range(3):
                    here += self.ra[k, i, j].astype(F32)
                self.sa[i, j] = here.astype(BF)
            lo, hi = lax.div(i, 2), lax.rem(i, 2)
            for j in range(2):
                here = self.sb[lo, j, hi].astype(F32)
                for k in range(3):
                    here += self.rb[k, lo, j, hi].astype(F32)
                self.sb[lo, j, hi] = here.astype(BF)

        self.two = []
        for i, (za, xb) in enumerate(zip(pos.zpeers(), pos.xpeers())):
            self.two.append(net.go(self.sa.at[xb["x"]], self.ta.at[i], xb))
            self.two.append(net.go(self.sb.at[za["zlo"], :, za["zhi"]], self.tb.at[i], za))

    def finish(self, out):
        pos = self.pos
        for copy in self.two:
            copy.wait_recv()
        for j in range(2):
            here = self.sa[pos.x, j].astype(F32)
            for k in range(3):
                here += self.ta[k, j].astype(F32)
            out[j] = here.astype(BF)
            here = self.sb[pos.zlo, j, pos.zhi].astype(F32)
            for k in range(3):
                here += self.tb[k, j].astype(F32)
            out[2 + j] = here.astype(BF)
        for copy in self.one + self.two:
            copy.wait_send()


FOLD_SEMS = 12


def fold_scratch(cols):
    return [
        pltpu.VMEM((3, 4, 2, 2, 16, cols), BF),
        pltpu.VMEM((3, 2, 2, 2, 2, 16, cols), BF),
        pltpu.VMEM((4, 2, 2, 16, cols), BF),
        pltpu.VMEM((2, 2, 2, 2, 16, cols), BF),
        pltpu.VMEM((3, 2, 2, 16, cols), BF),
        pltpu.VMEM((3, 2, 2, 16, cols), BF),
    ]


class OutFold:
    def __init__(self, net, pos, src, land):
        self.net, self.pos, self.src, self.land = net, pos, src, land
        self.base = net.block(32)

    def _targets(self):
        for xh in range(2):
            for dz in range(4):
                for core in range(2):
                    yield xh, dz, core

    def _copy(self, xh, dz, core):
        pos, net = self.pos, self.net
        zhi, zlo = pos.zs(dz)
        x = pos.core * 2 + xh
        peer = {"x": x, "zhi": zhi, "zlo": zlo, "core": core}
        dx = lax.rem(pos.x + 4 - x, 4)
        src = self.src.at[xh * 2 + zlo, zhi, core]
        slot = dx * 4 + (4 - dz) % 4
        return peer, src, slot

    def start(self):
        pos, net = self.pos, self.net
        for n, (xh, dz, core) in enumerate(self._targets()):
            peer, src, slot = self._copy(xh, dz, core)

            def send(peer=peer, src=src, slot=slot, n=n):
                pltpu.make_async_remote_copy(
                    src, self.land.at[slot], net.send.at[self.base + n], net.recv.at[self.base + slot],
                    device_id=peer, device_id_type=MESH,
                ).start()

            if dz == 0:
                here = (pos.core * 2 + xh == pos.x) & (pos.core == core)

                @pl.when(here)
                def _(src=src):
                    pltpu.make_async_copy(src, self.land.at[0], net.loc.at[net.loc.shape[0] - 1]).start()

                @pl.when(jnp.logical_not(here))
                def _(send=send):
                    send()
            else:
                send()

    def finish(self, out):
        pos, net = self.pos, self.net
        for n, (xh, dz, core) in enumerate(self._targets()):
            peer, src, slot = self._copy(xh, dz, core)

            def sent(peer=peer, src=src, slot=slot, n=n):
                pltpu.make_async_remote_copy(
                    src, self.land.at[slot], net.send.at[self.base + n], net.recv.at[self.base + slot],
                    device_id=peer, device_id_type=MESH,
                ).wait_send()

            if dz == 0:
                here = (pos.core * 2 + xh == pos.x) & (pos.core == core)

                @pl.when(here)
                def _(src=src):
                    pltpu.make_async_copy(src, self.land.at[0], net.loc.at[net.loc.shape[0] - 1]).wait()

                @pl.when(jnp.logical_not(here))
                def _(sent=sent):
                    sent()
            else:
                sent()
        for slot in range(16):
            probe = pltpu.make_async_remote_copy(
                self.src.at[0, 0, 0], self.land.at[slot], net.send.at[self.base], net.recv.at[self.base + slot],
                device_id=pos.sib, device_id_type=MESH,
            )
            if slot == 0:

                @pl.when(lax.div(pos.x, 2) != pos.core)
                def _():
                    probe.wait_recv()
            else:
                probe.wait_recv()
        here = self.land[0].astype(F32)
        for slot in range(1, 16):
            here += self.land[slot].astype(F32)
        out[...] = here


def attend_back_kernel(
    q_ref, kv_ref, lse_ref, o_ref, do_ref, cos_ref, sin_ref, part_ref, resid_ref,
    gg_ref, gu_ref, gd_ref, go_ref,
    dqkv_ref, block_ref, fold_ref, fo_ref,
    k_ref, v_ref, do2_ref, delta_ref, dq_ref, dk_ref, dv_ref, send_ref, got_ref, mine_ref,
    *rest,
):
    pos = Place()
    folds, rest = rest[:18], rest[18:]
    land_ref, rest = rest[0], rest[1:]
    sc_scratch, rest = rest[:5], rest[5:]
    net = Net(*rest)
    zhi = pos.zhi
    greet(pos.plane() + [pos.right, pos.left])
    sc = Scatter(net, pos, part_ref, sc_scratch)
    fd = [Fold(net, pos, g, folds[i * 6 : i * 6 + 6]) for i, g in enumerate((gg_ref, gu_ref, gd_ref))]
    rows = OutFold(net, pos, go_ref, land_ref)
    for f in fd:
        f.start()
    sc.start()
    rows.start()

    for j in range(4):
        kv = kv_ref[j].reshape(512, 256)
        for c in range(2):
            k_ref[c, j] = kv[:, c * 128 : c * 128 + 64]
            v_ref[c, j] = kv[:, c * 128 + 64 : c * 128 + 128]
            cols = slice(c * 128, (c + 1) * 128)
            do = do_ref[j, :, cols]
            do2_ref[j, c, 0:256] = do[:, 0:64]
            do2_ref[j, c, 256:512] = do[:, 64:128]
            both = (do.astype(F32) * o_ref[j, :, cols].astype(F32)).T
            delta_ref[j, c] = jnp.concatenate(
                [
                    jnp.sum(both[0:64], axis=0, keepdims=True),
                    jnp.sum(both[64:128], axis=0, keepdims=True),
                ],
                axis=1,
            )
    dq_ref[...] = jnp.zeros_like(dq_ref)
    sc.step()

    swap = net.block(4)

    def pair(c, j, qb, mask):
        k, v, q, do = k_ref[c, j], v_ref[c, j], q_ref[qb, c], do2_ref[qb, c]
        p = jnp.exp(dot_nt(k, q) - lse_ref[qb, c])
        if mask is not None:
            p = jnp.where(mask, p, 0.0)
        ds = (p * (dot_nt(v, do) - delta_ref[qb, c])).astype(BF)
        dv = dot_nn(p.astype(BF), do)
        dk = dot_nn(ds, q)
        dq_ref[qb, c] += dot_tn(k, ds)
        return dk, dv

    def column(j, _):
        mask = causal(zhi)
        for c in range(2):
            dk, dv = pair(c, j, j, mask)
            dk_ref[c] = dk
            dv_ref[c] = dv

        def more(qb, _):
            for c in range(2):
                dk, dv = pair(c, j, qb, None)
                dk_ref[c] += dk
                dv_ref[c] += dv
            return 0

        lax.fori_loop(j + 1, 4, more, 0)
        both = jnp.concatenate([dk_ref[0], dv_ref[0], dk_ref[1], dv_ref[1]], axis=1)
        both = both.reshape(2, 256, 256)

        @pl.when(zhi == 0)
        def _():
            mine_ref[j] = both[0]
            send_ref[j] = both[1].astype(BF)

        @pl.when(zhi == 1)
        def _():
            mine_ref[j] = both[1]
            send_ref[j] = both[0].astype(BF)

        net.go(send_ref.at[j], got_ref.at[j], pos.zpart, swap + j)
        return 0

    column(0, 0)
    sc.last()
    for f in fd:
        f.step()
    lax.fori_loop(1, 4, column, 0)

    sc.arrive()

    @pl.loop(0, 8)
    def _(i):
        r = pl.ds(pl.multiple_of(i * 16, 16), 16)
        block_ref[r] = (sc.total(r) + resid_ref[r]).astype(BF)

    for j in range(4):
        r = pl.ds(j * 256, 256)
        cos, sin = cos_ref[r], sin_ref[r]
        for c in range(2):
            dq = dq_ref[j, c].T * HEAD**-0.5
            dq = jnp.concatenate([dq[0:256], dq[256:512]], axis=1)
            dqkv_ref[r, c * 128 : (c + 1) * 128] = turn_back(dq, cos, sin).astype(BF)
    for j in range(4):
        r = pl.ds(j * 256, 256)
        cos, sin = cos_ref[r], sin_ref[r]
        net.make(send_ref.at[j], got_ref.at[j], pos.zpart, swap + j).wait()
        for c in range(2):
            cols = slice(c * 128, (c + 1) * 128)
            dkv = mine_ref[j, :, cols] + got_ref[j, :, cols].astype(F32)
            dkv = jnp.where(lane_first(dkv.shape), turn_back(dkv, cos, sin), dkv)
            dqkv_ref[r, 256 + c * 128 : 384 + c * 128] = dkv.astype(BF)

    for i, f in enumerate(fd):
        f.finish(fold_ref.at[i])
    rows.finish(fo_ref)
    sc.finish()


def run_attend_back(q, kv, lse, o, do, cos, sin, part, resid, gg, gu, gd, go):
    return pl.pallas_call(
        attend_back_kernel,
        out_shape=(
            shaped(1024, QKV),
            shaped(128, D),
            shaped(3, 4, 2, 16, SEG),
            shaped(16, D, dtype=F32),
        ),
        in_specs=[VM] * 9 + [ANY] * 4,
        out_specs=(VM, VM, VM, VM),
        scratch_shapes=[
            pltpu.VMEM((2, 4, 512, 64), BF),
            pltpu.VMEM((2, 4, 512, 64), BF),
            pltpu.VMEM((4, 2, 512, 64), BF),
            pltpu.VMEM((4, 2, 1, 512), F32),
            pltpu.VMEM((4, 2, 64, 512), F32),
            pltpu.VMEM((2, 512, 64), F32),
            pltpu.VMEM((2, 512, 64), F32),
            pltpu.VMEM((4, 256, 256), BF),
            pltpu.VMEM((4, 256, 256), BF),
            pltpu.VMEM((4, 256, 256), F32),
        ]
        + fold_scratch(SEG) * 3
        + [pltpu.VMEM((16, 16, D), BF)]
        + scatter_scratch()
        + sems(4 + 3 * FOLD_SEMS + 32 + SCATTER_SEMS, 8),
        compiler_params=pltpu.CompilerParams(
            collective_id=4, has_side_effects=True, vmem_limit_bytes=VLIMIT
        ),
        name="attend_back",
    )(q, kv, lse, o, do, cos, sin, part, resid, gg, gu, gd, go)


def last_kernel(
    part_ref, tok_ref, dmid_ref, gq_ref, fold_ref, dtok_ref, outq_ref, outr_ref, sumq_ref, *rest
):
    pos = Place()
    fold_s, sc_scratch, rest = rest[:6], rest[6:11], rest[11:]
    net = Net(*rest)
    tpeers = pos.tpeers()
    greet(tpeers + pos.xpeers() + pos.zpeers())
    fd = Fold(net, pos, gq_ref, fold_s)
    sc = Scatter(net, pos, part_ref, sc_scratch)
    fd.start()
    sc.start()
    sc.step()
    ship = []
    for peer in tpeers:
        ship.append(net.go(fold_ref.at[:, peer["y"], peer["core"]], outr_ref.at[pos.t], peer))
    keep = [net.local(fold_ref.at[:, pos.y, pos.core], outr_ref.at[pos.t])]
    fd.step()
    sc.last()
    fd.finish(sumq_ref)
    for peer in tpeers:
        ship.append(net.go(sumq_ref.at[peer["y"], peer["core"]], outq_ref.at[pos.t], peer))
    keep.append(net.local(sumq_ref.at[pos.y, pos.core], outq_ref.at[pos.t]))
    sc.arrive()

    @pl.loop(0, 8)
    def _(i):
        rows = pl.ds(pl.multiple_of(i * 16, 16), 16)
        r = tok_ref[rows].astype(F32)
        dtok_ref[rows] = norm_back(sc.total(rows), r, dmid_ref[rows]).astype(BF)

    for copy in ship + keep:
        copy.wait()
    sc.finish()


def run_last(part, tok, dmid, gq, fold):
    return pl.pallas_call(
        last_kernel,
        out_shape=(shaped(128, D), shaped(8, 16, QKV), shaped(8, 3, 16, SEG)),
        in_specs=[VM, VM, VM, ANY, ANY],
        out_specs=(VM, ANY, ANY),
        scratch_shapes=[pltpu.VMEM((4, 2, 16, QKV), BF)]
        + fold_scratch(QKV)
        + scatter_scratch()
        + sems(FOLD_SEMS + SCATTER_SEMS + 14, 4),
        compiler_params=pltpu.CompilerParams(
            collective_id=5, has_side_effects=True, vmem_limit_bytes=VLIMIT
        ),
        name="last",
    )(part, tok, dmid, gq, fold)


def rope_tables():
    half = HEAD // 2
    freq = np.exp(np.arange(half, dtype=np.float32) * np.float32(-2.0 * math.log(rope_base) / HEAD))
    spots = np.arange(2048, dtype=np.float32).reshape(4, 2, 256).transpose(1, 0, 2).reshape(2, 1024)
    angles = (spots[:, :, None] * freq.astype(np.float32)).astype(np.float32)
    angles = np.concatenate([angles] * 4, axis=2)
    return np.cos(angles).astype(np.float32), np.sin(angles).astype(np.float32)


def adam(weight, gradient, first_moment, second, step_rate, decay_weight):
    first_new = beta_one * first_moment + (1.0 - beta_one) * gradient
    second_new = beta_two * second + (1.0 - beta_two) * gradient * gradient
    first_hat = first_new / (1.0 - beta_one**STEP)
    second_hat = second_new / (1.0 - beta_two**STEP)
    weight_new = weight - step_rate * (
        first_hat / (jnp.sqrt(second_hat) + adam_eps) + decay_weight * weight
    )
    return (first_new, second_new, weight_new)


def local(
    tokens, cotangent, w_qkv, w_out, w_gate_up, w_down_t, gains,
    first_qkv, second_qkv, first_out, second_out, first_gate_up, second_gate_up,
    first_down, second_down, first_gains, second_gains,
):
    tok, cot = tokens[0], cotangent[0]
    inputs = tok.astype(F32)
    inv = lax.rsqrt(jnp.mean(inputs * inputs, axis=-1, keepdims=True) + norm_eps)
    normed = (inputs * inv).astype(BF)

    gain = gains.astype(BF).astype(F32)
    low_qkv = w_qkv.astype(BF).astype(F32)
    low_gu = w_gate_up.astype(BF).astype(F32)
    qkv_g = (low_qkv * gain[:, 0:1]).astype(BF)
    gu_g = (low_gu * gain[:, 1:2]).astype(BF)
    q_cut = qkv_g[:, :D].reshape(16, 2, 4, 4, HEAD).transpose(3, 1, 0, 2, 4).reshape(4, 2, 16, 256)
    kv_cut = jnp.concatenate(
        [qkv_g[:, D : D + 256].reshape(16, 2, 2, HEAD), qkv_g[:, D + 256 :].reshape(16, 2, 2, HEAD)],
        axis=3,
    )
    kv_cut = kv_cut.transpose(1, 0, 2, 3).reshape(1, 2, 16, 256)
    wq_blocks = jnp.concatenate(
        [q_cut, jnp.broadcast_to(kv_cut, (4, 2, 16, 256))], axis=3
    ).reshape(8, 16, QKV)

    def cut(rows):
        return rows.reshape(16, 8, SEG).transpose(1, 0, 2)

    wr_blocks = jnp.stack(
        [cut(gu_g[:, :FF]), cut(gu_g[:, FF:]), cut(w_down_t.astype(BF))], axis=1
    )

    zhi = lax.axis_index("zhi")
    cos_all, sin_all = rope_tables()
    cos = lax.dynamic_index_in_dim(jnp.asarray(cos_all), zhi, 0, keepdims=False)
    sin = lax.dynamic_index_in_dim(jnp.asarray(sin_all), zhi, 0, keepdims=False)

    n_in, wq, ra, rb = run_first(normed, wq_blocks, wr_blocks)
    n_in, wq = n_in.reshape(1024, D), wq.reshape(D, QKV)
    qkv = dot_nn(n_in, wq).astype(BF)
    o, lse, q, kv, wg, wu, wd, wo, cotf = run_attend(qkv, cos, sin, w_out.astype(BF), ra, rb, cot)
    o_rows = o.reshape(1024, 256)
    wg, wu, wd = (w.reshape(D, SEG) for w in (wg, wu, wd))
    wo = wo.reshape(256, D)
    cotf = cotf.reshape(1024, D)
    part_o = dot_nn(o_rows, wo).astype(BF).reshape(8, 128, D)
    resid, n_mid = run_mid(part_o, tok)
    n_mid = n_mid.reshape(1024, D)
    gate, up = dot_nn(n_mid, wg), dot_nn(n_mid, wu)
    d_hidden = dot_nn(cotf, wd)
    sig = jax.nn.sigmoid(gate)
    silu = gate * sig
    hidden = (silu * up).astype(BF)
    d_gate = (d_hidden * up * sig * (1.0 + gate * (1.0 - sig))).astype(BF)
    d_up = (d_hidden * silu).astype(BF)
    part_m = (dot_nt(d_gate, wg) + dot_nt(d_up, wu)).astype(BF).reshape(8, 128, D)
    d_mid, d_attn = run_back(part_m, resid, cot)
    d_attn = d_attn.reshape(1024, D)
    part_b = dot_nt(hidden, wd).astype(BF).reshape(8, 128, D)
    gg, gu, gd = dot_tn(n_mid, d_gate), dot_tn(n_mid, d_up), dot_tn(cotf, hidden)
    gg, gu, gd = (g.astype(BF).reshape(4, 2, 4, 2, 2, 16, SEG) for g in (gg, gu, gd))
    d_o = dot_nt(d_attn, wo).astype(BF)
    go = dot_tn(o_rows, d_attn).astype(BF).reshape(4, 2, 2, 16, D)
    dqkv, block_out, fold, grad_out = run_attend_back(
        q, kv, lse, o, d_o.reshape(4, 256, 256), cos, sin, part_b, resid, gg, gu, gd, go
    )
    part_i = dot_nt(dqkv, wq).astype(BF).reshape(8, 128, D)
    gq = dot_tn(n_in, dqkv).astype(BF).reshape(4, 2, 4, 2, 2, 16, QKV)
    d_tokens, sum_q, sum_r = run_last(part_i, tok, d_mid, gq, fold)

    sum_q = sum_q.reshape(4, 2, 16, QKV).astype(F32)
    grad_q = sum_q[..., :256].reshape(4, 2, 16, 4, HEAD).transpose(2, 1, 3, 0, 4).reshape(16, D)
    grad_kv = jnp.sum(sum_q[..., 256:], axis=0).reshape(2, 16, 2, 2, HEAD)
    grad_kv = grad_kv.transpose(1, 3, 0, 2, 4).reshape(16, 512)
    raw_qkv = jnp.concatenate([grad_q, grad_kv], axis=1)
    sum_r = sum_r.astype(F32)
    raw_gu = sum_r[:, 0:2].transpose(2, 1, 0, 3).reshape(16, 2 * FF)
    grad_down = sum_r[:, 2].transpose(1, 0, 2).reshape(16, FF)
    grad_qkv = raw_qkv * gain[:, 0:1]
    grad_gu = raw_gu * gain[:, 1:2]
    grad_gains = jnp.stack(
        [jnp.sum(low_qkv * raw_qkv, axis=1), jnp.sum(low_gu * raw_gu, axis=1)], axis=1
    )

    first_q, second_q, weight_q = adam(w_qkv, grad_qkv, first_qkv, second_qkv, rate_matrix, decay_rate)
    first_o, second_o, weight_o = adam(w_out, grad_out, first_out, second_out, rate_matrix, decay_rate)
    first_g, second_g, weight_g = adam(
        w_gate_up, grad_gu, first_gate_up, second_gate_up, rate_matrix, decay_rate
    )
    first_d, second_d, weight_d = adam(
        w_down_t, grad_down, first_down, second_down, rate_matrix, decay_rate
    )
    first_n, second_n, weight_n = adam(gains, grad_gains, first_gains, second_gains, rate_gain, 0.0)
    return (
        block_out[None], d_tokens[None],
        first_q, second_q, weight_q, first_o, second_o, weight_o,
        first_g, second_g, weight_g, first_d, second_d, weight_d,
        first_n, second_n, weight_n,
    )


def solution(mesh):
    fine = Mesh(mesh.devices.reshape(4, 2, 4, 2, 2), ("x", "zlo", "y", "zhi", "core"))
    dp, seq = ("x", "zlo"), ("y", "zhi", "core")
    act, row = P(dp, seq, None), P(dp + seq, None)
    return jax.shard_map(
        local,
        mesh=fine,
        in_specs=(act, act) + (row,) * 15,
        out_specs=(act, act) + (row,) * 15,
        check_vma=False,
    )
```

```python
import functools
import math

import jax
import jax.numpy as jnp
import numpy as np
from jax import lax
from jax.experimental import pallas as pl
from jax.experimental.pallas import tpu as pltpu
from jax.sharding import Mesh
from jax.sharding import PartitionSpec as P

D = 2048
HEAD = 64
FF = 5632
STEP = 10
SEG = FF // 8
QKV = 512

norm_eps = 1e-05
rope_base = 10000.0
mask_fill = -1e30
beta_one = 0.9
beta_two = 0.95
adam_eps = 1e-08
decay_rate = 0.1
rate_matrix = 0.08
rate_gain = 0.8

BF = jnp.bfloat16
F32 = jnp.float32
MESH = pl.DeviceIdType.MESH
ANY = pl.BlockSpec(memory_space=pl.ANY)
VM = pl.BlockSpec(memory_space=pltpu.VMEM)
VLIMIT = 56 * 2**20


def shaped(*shape, dtype=BF):
    return jax.ShapeDtypeStruct(shape, dtype)


class Place:
    def __init__(self):
        self.x, self.zlo, self.y = (lax.axis_index(a) for a in ("x", "zlo", "y"))
        self.zhi, self.core = lax.axis_index("zhi"), lax.axis_index("core")
        self.z = self.zhi * 2 + self.zlo
        self.t = self.y * 2 + self.core
        self.sib = {"core": 1 - self.core}
        self.right = {"y": lax.rem(self.y + 1, 4)}
        self.left = {"y": lax.rem(self.y + 3, 4)}
        self.zpart = {"zhi": 1 - self.zhi}

    def xs(self, step):
        return lax.rem(self.x + step, 4)

    def ys(self, step):
        return lax.rem(self.y + step, 4)

    def zs(self, step):
        z = lax.rem(self.z + step, 4)
        return lax.div(z, 2), lax.rem(z, 2)

    def xpeers(self):
        return [{"x": self.xs(i)} for i in (1, 2, 3)]

    def zpeers(self):
        out = []
        for i in (1, 2, 3):
            zhi, zlo = self.zs(i)
            out.append({"zhi": zhi, "zlo": zlo})
        return out

    def tpeers(self):
        return [
            {"y": self.ys(dy), "core": lax.rem(self.core + dc, 2)}
            for dy in range(4)
            for dc in range(2)
            if (dy, dc) != (0, 0)
        ]

    def plane(self):
        out = []
        for dx in range(4):
            for dz in range(4):
                for dc in range(2):
                    if (dx, dz, dc) != (0, 0, 0):
                        zhi, zlo = self.zs(dz)
                        out.append(
                            {"x": self.xs(dx), "zhi": zhi, "zlo": zlo, "core": lax.rem(self.core + dc, 2)}
                        )
        return out


def greet(peers):
    barrier = pltpu.get_barrier_semaphore()
    for peer in peers:
        pl.semaphore_signal(barrier, inc=1, device_id=peer, device_id_type=MESH)
    pl.semaphore_wait(barrier, len(peers))


class Net:
    def __init__(self, send, recv, local):
        self.send, self.recv, self.loc = send, recv, local
        self.n = 0
        self.m = 0

    def block(self, count):
        first = self.n
        self.n += count
        return first

    def make(self, src, dst, peer, at=None):
        if at is None:
            at = self.block(1)
        return pltpu.make_async_remote_copy(
            src, dst, self.send.at[at], self.recv.at[at], device_id=peer, device_id_type=MESH
        )

    def go(self, src, dst, peer, at=None):
        copy = self.make(src, dst, peer, at)
        copy.start()
        return copy

    def local(self, src, dst):
        copy = pltpu.make_async_copy(src, dst, self.loc.at[self.m])
        self.m += 1
        copy.start()
        return copy


def sems(remote, local):
    return [
        pltpu.SemaphoreType.DMA((remote,)),
        pltpu.SemaphoreType.DMA((remote,)),
        pltpu.SemaphoreType.DMA((max(local, 1),)),
    ]


class Gather:
    def __init__(self, net, pos, src, out):
        self.net, self.pos, self.src, self.out = net, pos, src, out

    def start(self):
        net, pos, src = self.net, self.pos, self.src
        mine = self.out.at[pos.t]
        lo, hi = pl.ds(0, 64), pl.ds(64, 64)
        self.own = net.local(src, mine)
        self.r = [net.go(src.at[lo], mine.at[lo], pos.right), None]
        self.l = [net.go(src.at[hi], mine.at[hi], pos.left), None]
        self.r[1] = net.go(src.at[hi], mine.at[hi], pos.right)
        self.l[1] = net.go(src.at[lo], mine.at[lo], pos.left)
        self.s = [net.go(src, mine, pos.sib)]

    def step(self):
        net, pos, out = self.net, self.pos, self.out
        lo, hi = pl.ds(0, 64), pl.ds(64, 64)
        from_left = out.at[pos.ys(3) * 2 + pos.core]
        from_right = out.at[pos.ys(1) * 2 + pos.core]
        self.r[0].wait_recv()
        self.r2 = net.go(from_left.at[lo], from_left.at[lo], pos.right)
        self.l[0].wait_recv()
        self.l2 = net.go(from_right.at[hi], from_right.at[hi], pos.left)
        self.r[1].wait_recv()
        self.s.append(net.go(from_left, from_left, pos.sib))
        self.l[1].wait_recv()
        self.s.append(net.go(from_right, from_right, pos.sib))

    def last(self):
        net, pos = self.net, self.pos
        far = self.out.at[pos.ys(2) * 2 + pos.core]
        lo, hi = pl.ds(0, 64), pl.ds(64, 64)
        self.r2.wait_recv()
        self.s.append(net.go(far.at[lo], far.at[lo], pos.sib))
        self.l2.wait_recv()
        self.s.append(net.go(far.at[hi], far.at[hi], pos.sib))

    def finish(self):
        for copy in self.r + self.l + [self.r2, self.l2]:
            copy.wait_send()
        for copy in self.s:
            copy.wait()
        self.own.wait()


GATHER_SEMS = 11


class Scatter:
    def __init__(self, net, pos, part, scratch):
        self.net, self.pos, self.part = net, pos, part
        self.sib, self.opp, self.nb, self.far, self.near = scratch
        self.c = {}

    def _give(self, dy, fill):
        pos = self.pos
        y = pos.ys(dy)
        if fill is not None:
            fill(y)
        theirs = self.part.at[y, pl.ds((1 - pos.core) * 128, 128)]
        self.c[dy] = self.net.go(theirs, self.sib.at[dy], pos.sib)

    def _mine(self, dy, first, count):
        pos = self.pos
        rows = pl.ds(pl.multiple_of(pos.core * 128 + first, 16), count)
        return self.part[pos.ys(dy), rows].astype(F32) + self.sib[dy, pl.ds(first, count)].astype(F32)

    def start(self, fill=None):
        net, pos = self.net, self.pos
        lo, hi = pl.ds(0, 64), pl.ds(64, 64)
        self._give(2, fill)
        self._give(1, fill)
        self.c[2].wait_recv()
        self.far[lo] = self._mine(2, 0, 64).astype(BF)
        self.f0 = net.go(self.far.at[lo], self.opp.at[0], pos.right)
        self.far[hi] = self._mine(2, 64, 64).astype(BF)
        self.f1 = net.go(self.far.at[hi], self.opp.at[1], pos.left)
        self._give(3, fill)
        self.c[1].wait_recv()
        self.near[0, hi] = self._mine(1, 64, 64).astype(BF)
        self.r1 = net.go(self.near.at[0, hi], self.nb.at[0, hi], pos.right)
        self._give(0, fill)
        self.c[3].wait_recv()
        self.near[1, lo] = self._mine(3, 0, 64).astype(BF)
        self.l0 = net.go(self.near.at[1, lo], self.nb.at[1, lo], pos.left)
        self.near[0, lo] = self._mine(1, 0, 64).astype(BF)
        self.near[1, hi] = self._mine(3, 64, 64).astype(BF)

    def last(self):
        net, pos = self.net, self.pos
        lo, hi = pl.ds(0, 64), pl.ds(64, 64)
        self.f0.wait_recv()
        self.near[0, lo] = (self.near[0, lo].astype(F32) + self.opp[0].astype(F32)).astype(BF)
        self.r0 = net.go(self.near.at[0, lo], self.nb.at[0, lo], pos.right)
        self.f1.wait_recv()
        self.near[1, hi] = (self.near[1, hi].astype(F32) + self.opp[1].astype(F32)).astype(BF)
        self.l1 = net.go(self.near.at[1, hi], self.nb.at[1, hi], pos.left)

    def arrive(self):
        for copy in (self.r1, self.l0, self.r0, self.l1, self.c[0]):
            copy.wait_recv()

    def total(self, first):
        rows = pl.ds(first, 16)
        out = self._mine(0, first, 16)
        return out + self.nb[0, rows].astype(F32) + self.nb[1, rows].astype(F32)

    def finish(self):
        for copy in (self.f0, self.f1, self.r0, self.r1, self.l0, self.l1):
            copy.wait_send()
        for copy in self.c.values():
            copy.wait_send()


SCATTER_SEMS = 10


def scatter_scratch():
    return [
        pltpu.VMEM((4, 128, D), BF),
        pltpu.VMEM((2, 64, D), BF),
        pltpu.VMEM((2, 128, D), BF),
        pltpu.VMEM((128, D), BF),
        pltpu.VMEM((2, 128, D), BF),
    ]


class OutRows:
    def __init__(self, net, pos, src, out):
        self.net, self.pos, self.src, self.out = net, pos, src, out
        self.base = net.block(32)

    def _pairs(self):
        pos = self.pos
        for dx in range(4):
            for dz in range(4):
                yield dx, dz, pos.xs(dx), pos.zs(dz)

    def start(self):
        pos, net = self.pos, self.net
        half = lax.div(pos.x, 2)
        dst = self.out.at[lax.rem(pos.x, 2) * 2 + pos.zlo, pos.zhi, pos.core]
        for dx, dz, x, (zhi, zlo) in self._pairs():
            peer = {"x": x, "zhi": zhi, "zlo": zlo, "core": half}
            at = self.base + (dx * 4 + dz) * 2 + pos.core
            if (dx, dz) == (0, 0):

                @pl.when(half == pos.core)
                def _():
                    pltpu.make_async_copy(self.src, dst, net.loc.at[net.loc.shape[0] - 1]).start()

                @pl.when(half != pos.core)
                def _():
                    net.make(self.src, dst, peer, at).start()
            else:
                net.make(self.src, dst, peer, at).start()

    def finish(self):
        pos, net = self.pos, self.net
        half = lax.div(pos.x, 2)
        dst = self.out.at[lax.rem(pos.x, 2) * 2 + pos.zlo, pos.zhi, pos.core]
        for dx, dz, x, (zhi, zlo) in self._pairs():
            peer = {"x": x, "zhi": zhi, "zlo": zlo, "core": half}
            at = self.base + (dx * 4 + dz) * 2 + pos.core
            first = (dx, dz) == (0, 0)
            if first:

                @pl.when(half == pos.core)
                def _():
                    pltpu.make_async_copy(self.src, dst, net.loc.at[net.loc.shape[0] - 1]).wait()

                @pl.when(half != pos.core)
                def _():
                    net.make(self.src, dst, peer, at).wait_send()
            else:
                net.make(self.src, dst, peer, at).wait_send()
            back = lax.rem(pos.x + 4 - dx, 4)

            @pl.when(lax.div(back, 2) == pos.core)
            def _():
                for core in range(2):
                    slot = self.base + (dx * 4 + dz) * 2 + core
                    if first:

                        @pl.when(pos.core != core)
                        def _():
                            net.make(self.src, dst, peer, slot).wait_recv()
                    else:
                        net.make(self.src, dst, peer, slot).wait_recv()


def first_kernel(
    n_ref, wq_ref, wout_ref, qkv_ref, nf_ref, wqf_ref, wo_ref, send, recv, local
):
    pos, net = Place(), Net(send, recv, local)
    tpeers, xpeers, zpeers = pos.tpeers(), pos.xpeers(), pos.zpeers()
    greet(pos.plane() + tpeers[1:])
    x, y, zlo, zhi, core = pos.x, pos.y, pos.zlo, pos.zhi, pos.core
    low, high = pl.ds(0, 2), pl.ds(2, 2)

    small = []
    for peer in tpeers:
        t = peer["y"] * 2 + peer["core"]
        small.append(net.go(wq_ref.at[t], wqf_ref.at[x, zlo, y, zhi, core], peer))
    mine = net.local(wq_ref.at[pos.t], wqf_ref.at[x, zlo, y, zhi, core])
    gather = Gather(net, pos, n_ref, nf_ref)
    gather.start()
    rows = OutRows(net, pos, wout_ref, wo_ref)
    rows.start()

    mine.wait()
    for copy in small:
        copy.wait_recv()
    one = []
    for peer in xpeers:
        part = wqf_ref.at[x, zlo, low, zhi]
        one.append(net.go(part, part, peer))
    for peer in zpeers:
        part = wqf_ref.at[x, zlo, high, zhi]
        one.append(net.go(part, part, peer))

    for copy in one:
        copy.wait_recv()
    two = []
    for peer in zpeers:
        part = wqf_ref.at[:, zlo, low, zhi]
        two.append(net.go(part, part, peer))
    for peer in xpeers:
        part = wqf_ref.at[x, :, high, :]
        two.append(net.go(part, part, peer))

    gather.step()
    gather.last()
    for copy in small + one:
        copy.wait_send()
    for copy in two:
        copy.wait()
    gather.finish()

    @pl.loop(0, 4)
    def _(i):
        w = wqf_ref[...].reshape(D, QKV)
        a = nf_ref[pl.ds(i * 2, 2)].reshape(256, D)
        qkv_ref[pl.ds(pl.multiple_of(i * 256, 256), 256)] = dot_nn(a, w).astype(BF)

    rows.finish()


def run_first(normed, wq_blocks, wout):
    return pl.pallas_call(
        first_kernel,
        out_shape=(
            shaped(1024, QKV),
            shaped(8, 128, D),
            shaped(4, 2, 4, 2, 2, 16, QKV),
            shaped(4, 2, 2, 16, D),
        ),
        in_specs=[VM, VM, VM],
        out_specs=(VM, VM, VM, ANY),
        scratch_shapes=sems(7 + 12 + 32 + GATHER_SEMS, 3),
        compiler_params=pltpu.CompilerParams(
            collective_id=0, has_side_effects=True, vmem_limit_bytes=VLIMIT
        ),
        name="first",
    )(normed, wq_blocks, wout)


def dot_nt(a, b):
    return lax.dot_general(a, b, (((1,), (1,)), ((), ())), preferred_element_type=F32)


def dot_tn(a, b):
    return lax.dot_general(a, b, (((0,), (0,)), ((), ())), preferred_element_type=F32)


def dot_nn(a, b):
    return lax.dot_general(a, b, (((1,), (0,)), ((), ())), preferred_element_type=F32)


def first_half_mask(shape):
    return (lax.broadcasted_iota(jnp.int32, shape, 1) & 63) < 32


def turn(u, cos, sin):
    rot = jnp.where(first_half_mask(u.shape), -pltpu.roll(u, 96, 1), pltpu.roll(u, 32, 1))
    return u * cos + rot * sin


def turn_back(u, cos, sin):
    v = u * sin
    rot = jnp.where(first_half_mask(u.shape), pltpu.roll(v, 96, 1), -pltpu.roll(v, 32, 1))
    return u * cos + rot


def lane_first(shape):
    return lax.broadcasted_iota(jnp.int32, shape, 1) < 64


def causal(zhi):
    key = lax.broadcasted_iota(jnp.int32, (512, 512), 0)
    query = (lax.broadcasted_iota(jnp.int32, (512, 512), 1) & 255) + zhi * 256
    return key <= query


class Cross:
    def __init__(self, net, pos, src, own, ra, rb):
        self.net, self.pos, self.src, self.own, self.ra, self.rb = net, pos, src, own, ra, rb

    def start(self):
        net, pos = self.net, self.pos
        dst = self.own.at[:, pos.y, pos.core]
        self.one = []
        for peer in pos.tpeers():
            self.one.append(net.go(self.src.at[peer["y"] * 2 + peer["core"]], dst, peer))
        self.mine = net.local(self.src.at[pos.t], dst)

    def step(self):
        net, pos = self.net, self.pos
        self.mine.wait()
        for copy in self.one:
            copy.wait_recv()
        part_a, part_b = self.own.at[:, pl.ds(0, 2)], self.own.at[:, pl.ds(2, 2)]
        to_a, to_b = self.ra.at[:, pos.x], self.rb.at[:, pos.zlo, :, pos.zhi]
        self.two = []
        for xp, zp in zip(pos.xpeers(), pos.zpeers()):
            self.two.append(net.go(part_a, to_a, xp))
            self.two.append(net.go(part_b, to_b, zp))
        self.keep = [net.local(part_a, to_a), net.local(part_b, to_b)]

    def finish(self):
        for copy in self.one:
            copy.wait_send()
        for copy in self.two + self.keep:
            copy.wait()


class Spread:
    def __init__(self, net, pos, ra, rb, outs):
        self.net, self.pos, self.ra, self.rb, self.outs = net, pos, ra, rb, outs

    def start(self):
        net, pos = self.net, self.pos
        low, high = pl.ds(0, 2), pl.ds(2, 2)
        up_z, down_z = pos.zpeers()[0], pos.zpeers()[2]
        up_x, down_x = pos.xpeers()[0], pos.xpeers()[2]
        self.one, self.two, self.keep = [], [], []
        for i, out in self.outs:
            a = [(self.ra.at[i, h], out.at[h, pos.zlo, low, pos.zhi]) for h in (low, high)]
            b = [(self.rb.at[i, h], out.at[pos.x, h, high, :]) for h in (0, 1)]
            self.one.append(
                [net.go(*a[0], up_z), net.go(*a[1], down_z), net.go(*b[0], up_x), net.go(*b[1], down_x)]
                + [net.go(*a[1], up_z), net.go(*a[0], down_z), net.go(*b[1], up_x), net.go(*b[0], down_x)]
            )
            self.keep += [net.local(*c) for c in a + b]

    def step(self):
        net, pos = self.net, self.pos
        low, high = pl.ds(0, 2), pl.ds(2, 2)
        up_z, down_z = pos.zpeers()[0], pos.zpeers()[2]
        up_x, down_x = pos.xpeers()[0], pos.xpeers()[2]
        for (_, out), one in zip(self.outs, self.one):
            parts = (
                (out.at[low, down_z["zlo"], low, down_z["zhi"]], up_z),
                (out.at[high, up_z["zlo"], low, up_z["zhi"]], down_z),
                (out.at[down_x["x"], 0, high, :], up_x),
                (out.at[up_x["x"], 1, high, :], down_x),
            )
            for copy, (part, peer) in zip(one, parts):
                copy.wait_recv()
                self.two.append(net.go(part, part, peer))

    def finish(self):
        for one in self.one:
            for copy in one[:4]:
                copy.wait_send()
            for copy in one[4:]:
                copy.wait()
        for copy in self.two + self.keep:
            copy.wait()


SPREAD_SEMS = 36


def attend_kernel(
    qkv_ref, cos_ref, sin_ref, wr_ref, cot_ref,
    o_ref, lse_ref, q_ref, kv_ref, ra_ref, rb_ref, cotf_ref,
    k_ref, v_ref, own_ref, send, recv, local,
):
    pos, net = Place(), Net(send, recv, local)
    zhi = pos.zhi
    greet([pos.zpart] + pos.tpeers() + pos.xpeers() + pos.zpeers()[0:3:2])
    gather = Gather(net, pos, cot_ref, cotf_ref)
    cross = Cross(net, pos, wr_ref, own_ref, ra_ref, rb_ref)

    swap = net.block(4)
    for j in range(4):
        r = pl.ds(j * 256, 256)
        cos, sin = cos_ref[r], sin_ref[r]
        for c in range(2):
            kv = qkv_ref[r, 256 + c * 128 : 384 + c * 128].astype(F32)
            mixed = jnp.where(lane_first(kv.shape), turn(kv, cos, sin), kv)
            kv_ref[j, zhi, :, c * 128 : (c + 1) * 128] = mixed.astype(BF)
        net.go(kv_ref.at[j, zhi], kv_ref.at[j, zhi], pos.zpart, swap + j)
    cross.start()
    gather.start()
    for j in range(4):
        r = pl.ds(j * 256, 256)
        cos, sin = cos_ref[r], sin_ref[r]
        for c in range(2):
            q = turn(qkv_ref[r, c * 128 : (c + 1) * 128].astype(F32), cos, sin)
            q = q.astype(BF) * jnp.asarray(HEAD**-0.5, BF)
            q_ref[j, c, 0:256] = q[:, 0:64]
            q_ref[j, c, 256:512] = q[:, 64:128]

    def update(c, key_at, query, state, mask):
        top, norm, acc = state
        s = dot_nt(k_ref[c, key_at], query)
        if mask is not None:
            s = jnp.where(mask, s, mask_fill)
        new = jnp.maximum(top, jnp.max(s, axis=0, keepdims=True))
        p = jnp.exp(s - new)
        keep = jnp.exp(top - new)
        norm = norm * keep + jnp.sum(p, axis=0, keepdims=True)
        acc = acc * keep + dot_tn(v_ref[c, key_at], p.astype(BF))
        return new, norm, acc

    def block(qb, _):
        part = kv_ref.at[qb, zhi]
        net.make(part, part, pos.zpart, swap + qb).wait_recv()
        kv = kv_ref[qb].reshape(512, 256)
        for c in range(2):
            k_ref[c, qb] = kv[:, c * 128 : c * 128 + 64]
            v_ref[c, qb] = kv[:, c * 128 + 64 : c * 128 + 128]
        mask = causal(zhi)
        state = []
        for c in range(2):
            zero = (
                jnp.full((1, 512), mask_fill, F32),
                jnp.zeros((1, 512), F32),
                jnp.zeros((64, 512), F32),
            )
            state.append(update(c, qb, q_ref[qb, c], zero, mask))

        def more(j, held):
            return tuple(update(c, j, q_ref[qb, c], held[c], None) for c in range(2))

        state = lax.fori_loop(0, qb, more, tuple(state))
        for c in range(2):
            top, norm, acc = state[c]
            lse_ref[qb, c] = top + jnp.log(norm)
            out = (acc / norm).T
            pair = jnp.concatenate([out[0:256], out[256:512]], axis=1)
            o_ref[qb, :, c * 128 : (c + 1) * 128] = pair.astype(BF)
        return 0

    block(0, 0)
    cross.step()
    lax.fori_loop(1, 3, block, 0)
    gather.step()
    block(3, 0)
    gather.last()
    gather.finish()
    cross.finish()
    for j in range(4):
        part = kv_ref.at[j, zhi]
        net.make(part, part, pos.zpart, swap + j).wait_send()


def run_attend(qkv, cos, sin, wr_blocks, cot):
    return pl.pallas_call(
        attend_kernel,
        out_shape=(
            shaped(4, 256, 256),
            shaped(4, 2, 1, 512, dtype=F32),
            shaped(4, 2, 512, 64),
            shaped(4, 2, 256, 256),
            shaped(3, 4, 2, 2, 16, SEG),
            shaped(3, 2, 2, 2, 2, 16, SEG),
            shaped(8, 128, D),
        ),
        in_specs=[VM, VM, VM, VM, VM],
        out_specs=(VM, VM, VM, VM, ANY, ANY, ANY),
        scratch_shapes=[
            pltpu.VMEM((2, 4, 512, 64), BF),
            pltpu.VMEM((2, 4, 512, 64), BF),
            pltpu.VMEM((3, 4, 2, 16, SEG), BF),
        ]
        + sems(4 + 13 + GATHER_SEMS, 4),
        compiler_params=pltpu.CompilerParams(
            collective_id=1, has_side_effects=True, vmem_limit_bytes=VLIMIT
        ),
        name="attend",
    )(qkv, cos, sin, wr_blocks, cot)


class Fold:
    def __init__(self, net, pos, src, scratch, sums, scratch_two):
        self.net, self.pos, self.src = net, pos, src
        if scratch is not None:
            self.ra, self.rb = scratch
        self.sa, self.sb = sums
        if scratch_two is not None:
            self.ta, self.tb = scratch_two

    def start(self):
        net, pos, src = self.net, self.pos, self.src
        low, high = pl.ds(0, 2), pl.ds(2, 2)
        self.one = []
        for i, (za, xb) in enumerate(zip(pos.zpeers(), pos.xpeers())):
            self.one.append(net.go(src.at[:, za["zlo"], low, za["zhi"]], self.ra.at[i], za))
            self.one.append(net.go(src.at[xb["x"], :, high, :], self.rb.at[i], xb))
        self.keep = [
            net.local(src.at[:, pos.zlo, low, pos.zhi], self.sa),
            net.local(src.at[pos.x, :, high, :], self.sb),
        ]

    def add(self):
        for copy in self.keep:
            copy.wait()
        for copy in self.one:
            copy.wait_recv()

        @pl.loop(0, 4)
        def _(i):
            for j in range(2):
                here = self.sa[i, j].astype(F32)
                for k in range(3):
                    here += self.ra[k, i, j].astype(F32)
                self.sa[i, j] = here.astype(BF)
            lo, hi = lax.div(i, 2), lax.rem(i, 2)
            for j in range(2):
                here = self.sb[lo, j, hi].astype(F32)
                for k in range(3):
                    here += self.rb[k, lo, j, hi].astype(F32)
                self.sb[lo, j, hi] = here.astype(BF)

        for copy in self.one:
            copy.wait_send()

    def second(self):
        net, pos = self.net, self.pos
        self.two = []
        for i, (za, xb) in enumerate(zip(pos.zpeers(), pos.xpeers())):
            self.two.append(net.go(self.sa.at[xb["x"]], self.ta.at[i], xb))
            self.two.append(net.go(self.sb.at[za["zlo"], :, za["zhi"]], self.tb.at[i], za))

    def finish(self, out):
        pos = self.pos
        for copy in self.two:
            copy.wait_recv()
        for j in range(2):
            here = self.sa[pos.x, j].astype(F32)
            for k in range(3):
                here += self.ta[k, j].astype(F32)
            out[j] = here.astype(BF)
            here = self.sb[pos.zlo, j, pos.zhi].astype(F32)
            for k in range(3):
                here += self.tb[k, j].astype(F32)
            out[2 + j] = here.astype(BF)
        for copy in self.two:
            copy.wait_send()


FOLD_SEMS = 12


def fold_one(cols):
    return [pltpu.VMEM((3, 4, 2, 2, 16, cols), BF), pltpu.VMEM((3, 2, 2, 2, 2, 16, cols), BF)]


def fold_sums(cols):
    return [pltpu.VMEM((4, 2, 2, 16, cols), BF), pltpu.VMEM((2, 2, 2, 2, 16, cols), BF)]


def fold_two(cols):
    return [pltpu.VMEM((3, 2, 2, 16, cols), BF), pltpu.VMEM((3, 2, 2, 16, cols), BF)]


def mid_kernel(
    o_ref, wo_ref, tok_ref, ra_ref, rb_ref, resid_ref, full_ref, wg_ref, wu_ref, wd_ref,
    part_ref, a, b, c, d, e, blk, send, recv, local,
):
    pos, net = Place(), Net(send, recv, local)
    greet([pos.sib, pos.right, pos.left] + pos.xpeers() + pos.zpeers())
    sc = Scatter(net, pos, part_ref, (a, b, c, d, e))
    spread = Spread(net, pos, ra_ref, rb_ref, [(0, wg_ref), (1, wu_ref), (2, wd_ref)])
    spread.start()

    def fill(y):
        @pl.loop(0, 4)
        def _(i):
            cols = pl.ds(pl.multiple_of(i * 512, 512), 512)
            part_ref[y, :, cols] = dot_nn(o_ref[y], wo_ref[:, cols]).astype(BF)

    sc.start(fill)
    sc.last()
    sc.arrive()

    @pl.loop(0, 8)
    def _(i):
        first = pl.multiple_of(i * 16, 16)
        rows = pl.ds(first, 16)
        r = sc.total(first) + tok_ref[rows].astype(F32)
        resid_ref[rows] = r
        inv = lax.rsqrt(jnp.mean(r * r, axis=-1, keepdims=True) + norm_eps)
        blk[rows] = (r * inv).astype(BF)

    gather = Gather(net, pos, blk, full_ref)
    gather.start()
    sc.finish()
    spread.step()
    gather.step()
    gather.last()
    gather.finish()
    spread.finish()


def run_mid(o, wo, tok, ra, rb):
    full = shaped(4, 2, 4, 2, 2, 16, SEG)
    return pl.pallas_call(
        mid_kernel,
        out_shape=(shaped(128, D, dtype=F32), shaped(8, 128, D), full, full, full),
        in_specs=[VM, VM, VM, VM, VM],
        out_specs=(VM, ANY, ANY, ANY, ANY),
        scratch_shapes=[pltpu.VMEM((4, 256, D), BF)]
        + scatter_scratch()
        + [pltpu.VMEM((128, D), BF)]
        + sems(SCATTER_SEMS + GATHER_SEMS + SPREAD_SEMS, 13),
        compiler_params=pltpu.CompilerParams(
            collective_id=2, has_side_effects=True, vmem_limit_bytes=VLIMIT
        ),
        name="mid",
    )(o, wo, tok, ra, rb)


def norm_back(t, r, back):
    inv = lax.rsqrt(jnp.mean(r * r, axis=-1, keepdims=True) + norm_eps)
    normed = r * inv
    return back + inv * (t - normed * jnp.mean(t * normed, axis=-1, keepdims=True))


def back_kernel(
    wg_ref, wu_ref, wd_ref, nin_ref, cotin_ref, resid_ref, cot_ref,
    dmid_ref, full_ref, sa_ref, sb_ref, down_ref, gg_out, gu_out,
    part_ref, a, b, c, d, e, blk, n_ref, cotf_ref, dg_ref, du_ref, hid_ref, gd_ref, gg_ref, gu_ref, *rest,
):
    folds, rest = rest[:2], rest[2:]
    pos, net = Place(), Net(*rest)
    bring = {}
    for dy in (2, 1, 3, 0):
        rows = pl.ds(pl.multiple_of(pos.ys(dy) * 256, 256), 256)
        bring[dy] = [
            net.local(nin_ref.at[rows], n_ref.at[rows]),
            net.local(cotin_ref.at[rows], cotf_ref.at[rows]),
        ]
    greet([pos.sib, pos.right, pos.left] + pos.xpeers() + pos.zpeers())
    sc = Scatter(net, pos, part_ref, (a, b, c, d, e))
    fd = Fold(net, pos, gd_ref, folds, (sa_ref, sb_ref), None)
    order = iter((2, 1, 3, 0))

    def fill(y):
        for copy in bring[next(order)]:
            copy.wait()
        rows = pl.ds(pl.multiple_of(y * 256, 256), 256)
        gate, up = dot_nn(n_ref[rows], wg_ref[...]), dot_nn(n_ref[rows], wu_ref[...])
        d_hidden = dot_nn(cotf_ref[rows], wd_ref[...])
        sig = jax.nn.sigmoid(gate)
        silu = gate * sig
        hid_ref[rows] = (silu * up).astype(BF)
        dg_ref[rows] = (d_hidden * up * sig * (1.0 + gate * (1.0 - sig))).astype(BF)
        du_ref[rows] = (d_hidden * silu).astype(BF)

        @pl.loop(0, 4)
        def _(i):
            cols = pl.ds(pl.multiple_of(i * 512, 512), 512)
            both = dot_nt(dg_ref[rows], wg_ref[cols]) + dot_nt(du_ref[rows], wu_ref[cols])
            part_ref[y, :, cols] = both.astype(BF)

    def grad(left, right, out):
        @pl.loop(0, 8)
        def _(i):
            cols = pl.ds(pl.multiple_of(i * 256, 256), 256)
            g = dot_tn(left[:, cols], right[...]).astype(BF)
            out[lax.div(i, 2), lax.rem(i, 2)] = g.reshape(4, 2, 2, 16, SEG)

    sc.start(fill)
    sc.last()
    grad(cotf_ref, hid_ref, gd_ref)
    fd.start()
    sc.arrive()

    @pl.loop(0, 8)
    def _(i):
        first = pl.multiple_of(i * 16, 16)
        rows = pl.ds(first, 16)
        dmid = norm_back(sc.total(first), resid_ref[rows], cot_ref[rows].astype(F32))
        dmid_ref[rows] = dmid
        blk[rows] = dmid.astype(BF)

    gather = Gather(net, pos, blk, full_ref)
    gather.start()
    sc.finish()
    grad(n_ref, dg_ref, gg_ref)
    keep = [net.local(gg_ref, gg_out)]
    gather.step()
    grad(n_ref, du_ref, gu_ref)
    keep.append(net.local(gu_ref, gu_out))
    gather.last()

    @pl.loop(0, 4)
    def _(y):
        rows = pl.ds(pl.multiple_of(y * 256, 256), 256)

        @pl.loop(0, 4)
        def _(i):
            cols = pl.ds(pl.multiple_of(i * 512, 512), 512)
            down_ref[y, :, cols] = dot_nt(hid_ref[rows], wd_ref[cols]).astype(BF)

    fd.add()
    gather.finish()
    for copy in keep:
        copy.wait()


def run_back(wg, wu, wd, n, cotf, resid, cot):
    full = shaped(4, 2, 4, 2, 2, 16, SEG)
    return pl.pallas_call(
        back_kernel,
        out_shape=(
            shaped(128, D, dtype=F32),
            shaped(8, 128, D),
            shaped(4, 2, 2, 16, SEG),
            shaped(2, 2, 2, 2, 16, SEG),
            shaped(4, 256, D),
            full,
            full,
        ),
        in_specs=[VM] * 3 + [ANY] * 2 + [VM] * 2,
        out_specs=(VM, ANY, VM, VM, VM, ANY, ANY),
        scratch_shapes=[pltpu.VMEM((4, 256, D), BF)]
        + scatter_scratch()
        + [pltpu.VMEM((128, D), BF)]
        + [pltpu.VMEM((1024, D), BF)] * 2
        + [pltpu.VMEM((1024, SEG), BF)] * 3
        + [pltpu.VMEM((4, 2, 4, 2, 2, 16, SEG), BF)] * 3
        + fold_one(SEG)
        + sems(SCATTER_SEMS + GATHER_SEMS + 6, 13),
        compiler_params=pltpu.CompilerParams(
            collective_id=3, has_side_effects=True, vmem_limit_bytes=VLIMIT
        ),
        name="back",
    )(wg, wu, wd, n, cotf, resid, cot)


class OutFold:
    def __init__(self, net, pos, src, land):
        self.net, self.pos, self.src, self.land = net, pos, src, land
        self.base = net.block(32)

    def _targets(self):
        for xh in range(2):
            for dz in range(4):
                for core in range(2):
                    yield xh, dz, core

    def _copy(self, xh, dz, core):
        pos, net = self.pos, self.net
        zhi, zlo = pos.zs(dz)
        x = pos.core * 2 + xh
        peer = {"x": x, "zhi": zhi, "zlo": zlo, "core": core}
        dx = lax.rem(pos.x + 4 - x, 4)
        src = self.src.at[xh * 2 + zlo, zhi, core]
        slot = dx * 4 + (4 - dz) % 4
        return peer, src, slot

    def start(self):
        pos, net = self.pos, self.net
        for n, (xh, dz, core) in enumerate(self._targets()):
            peer, src, slot = self._copy(xh, dz, core)

            def send(peer=peer, src=src, slot=slot, n=n):
                pltpu.make_async_remote_copy(
                    src, self.land.at[slot], net.send.at[self.base + n], net.recv.at[self.base + slot],
                    device_id=peer, device_id_type=MESH,
                ).start()

            if dz == 0:
                here = (pos.core * 2 + xh == pos.x) & (pos.core == core)

                @pl.when(here)
                def _(src=src):
                    pltpu.make_async_copy(src, self.land.at[0], net.loc.at[net.loc.shape[0] - 1]).start()

                @pl.when(jnp.logical_not(here))
                def _(send=send):
                    send()
            else:
                send()

    def finish(self, out):
        pos, net = self.pos, self.net
        for n, (xh, dz, core) in enumerate(self._targets()):
            peer, src, slot = self._copy(xh, dz, core)

            def sent(peer=peer, src=src, slot=slot, n=n):
                pltpu.make_async_remote_copy(
                    src, self.land.at[slot], net.send.at[self.base + n], net.recv.at[self.base + slot],
                    device_id=peer, device_id_type=MESH,
                ).wait_send()

            if dz == 0:
                here = (pos.core * 2 + xh == pos.x) & (pos.core == core)

                @pl.when(here)
                def _(src=src):
                    pltpu.make_async_copy(src, self.land.at[0], net.loc.at[net.loc.shape[0] - 1]).wait()

                @pl.when(jnp.logical_not(here))
                def _(sent=sent):
                    sent()
            else:
                sent()
        for slot in range(16):
            probe = pltpu.make_async_remote_copy(
                self.src.at[0, 0, 0], self.land.at[slot], net.send.at[self.base], net.recv.at[self.base + slot],
                device_id=pos.sib, device_id_type=MESH,
            )
            if slot == 0:

                @pl.when(lax.div(pos.x, 2) != pos.core)
                def _():
                    probe.wait_recv()
            else:
                probe.wait_recv()
        here = self.land[0].astype(F32)
        for slot in range(1, 16):
            here += self.land[slot].astype(F32)
        out[...] = here


def attend_back_kernel(
    q_ref, kv_ref, lse_ref, o_ref, do_ref, cos_ref, sin_ref, part_ref, resid_ref,
    gg_ref, gu_ref, go_ref,
    dqkv_ref, block_ref, sga_ref, sgb_ref, sua_ref, sub_ref, fo_ref,
    k_ref, v_ref, do2_ref, delta_ref, dq_ref, dk_ref, dv_ref, send_ref, got_ref, mine_ref,
    *rest,
):
    pos = Place()
    folds, rest = rest[:4], rest[4:]
    land_ref, rest = rest[0], rest[1:]
    sc_scratch, rest = rest[:5], rest[5:]
    net = Net(*rest)
    zhi = pos.zhi
    greet(pos.plane() + [pos.right, pos.left])
    sc = Scatter(net, pos, part_ref, sc_scratch)
    fd = [
        Fold(net, pos, gg_ref, folds[0:2], (sga_ref, sgb_ref), None),
        Fold(net, pos, gu_ref, folds[2:4], (sua_ref, sub_ref), None),
    ]
    rows = OutFold(net, pos, go_ref, land_ref)
    sc.start()
    for f in fd:
        f.start()
    rows.start()

    for j in range(4):
        kv = kv_ref[j].reshape(512, 256)
        for c in range(2):
            k_ref[c, j] = kv[:, c * 128 : c * 128 + 64]
            v_ref[c, j] = kv[:, c * 128 + 64 : c * 128 + 128]
            cols = slice(c * 128, (c + 1) * 128)
            do = do_ref[j, :, cols]
            do2_ref[j, c, 0:256] = do[:, 0:64]
            do2_ref[j, c, 256:512] = do[:, 64:128]
            both = (do.astype(F32) * o_ref[j, :, cols].astype(F32)).T
            delta_ref[j, c] = jnp.concatenate(
                [
                    jnp.sum(both[0:64], axis=0, keepdims=True),
                    jnp.sum(both[64:128], axis=0, keepdims=True),
                ],
                axis=1,
            )
    dq_ref[...] = jnp.zeros_like(dq_ref)

    swap = net.block(4)

    def pair(c, j, qb, mask):
        k, v, q, do = k_ref[c, j], v_ref[c, j], q_ref[qb, c], do2_ref[qb, c]
        p = jnp.exp(dot_nt(k, q) - lse_ref[qb, c])
        if mask is not None:
            p = jnp.where(mask, p, 0.0)
        ds = (p * (dot_nt(v, do) - delta_ref[qb, c])).astype(BF)
        dv = dot_nn(p.astype(BF), do)
        dk = dot_nn(ds, q)
        dq_ref[qb, c] += dot_tn(k, ds)
        return dk, dv

    def column(j, _):
        mask = causal(zhi)
        for c in range(2):
            dk, dv = pair(c, j, j, mask)
            dk_ref[c] = dk
            dv_ref[c] = dv

        def more(qb, _):
            for c in range(2):
                dk, dv = pair(c, j, qb, None)
                dk_ref[c] += dk
                dv_ref[c] += dv
            return 0

        lax.fori_loop(j + 1, 4, more, 0)
        both = jnp.concatenate([dk_ref[0], dv_ref[0], dk_ref[1], dv_ref[1]], axis=1)
        both = both.reshape(2, 256, 256)

        @pl.when(zhi == 0)
        def _():
            mine_ref[j] = both[0]
            send_ref[j] = both[1].astype(BF)

        @pl.when(zhi == 1)
        def _():
            mine_ref[j] = both[1]
            send_ref[j] = both[0].astype(BF)

        net.go(send_ref.at[j], got_ref.at[j], pos.zpart, swap + j)
        return 0

    column(0, 0)
    sc.last()
    lax.fori_loop(1, 4, column, 0)

    sc.arrive()

    @pl.loop(0, 8)
    def _(i):
        first = pl.multiple_of(i * 16, 16)
        r = pl.ds(first, 16)
        block_ref[r] = (sc.total(first) + resid_ref[r]).astype(BF)

    for j in range(4):
        r = pl.ds(j * 256, 256)
        cos, sin = cos_ref[r], sin_ref[r]
        for c in range(2):
            dq = dq_ref[j, c].T * HEAD**-0.5
            dq = jnp.concatenate([dq[0:256], dq[256:512]], axis=1)
            dqkv_ref[r, c * 128 : (c + 1) * 128] = turn_back(dq, cos, sin).astype(BF)
    for j in range(4):
        r = pl.ds(j * 256, 256)
        cos, sin = cos_ref[r], sin_ref[r]
        net.make(send_ref.at[j], got_ref.at[j], pos.zpart, swap + j).wait()
        for c in range(2):
            cols = slice(c * 128, (c + 1) * 128)
            dkv = mine_ref[j, :, cols] + got_ref[j, :, cols].astype(F32)
            dkv = jnp.where(lane_first(dkv.shape), turn_back(dkv, cos, sin), dkv)
            dqkv_ref[r, 256 + c * 128 : 384 + c * 128] = dkv.astype(BF)

    for f in fd:
        f.add()
    rows.finish(fo_ref)
    sc.finish()


def run_attend_back(q, kv, lse, o, do, cos, sin, part, resid, gg, gu, go):
    sums = (shaped(4, 2, 2, 16, SEG), shaped(2, 2, 2, 2, 16, SEG)) * 2
    return pl.pallas_call(
        attend_back_kernel,
        out_shape=(
            shaped(1024, QKV),
            shaped(128, D),
            *sums,
            shaped(16, D, dtype=F32),
        ),
        in_specs=[VM] * 9 + [ANY] * 3,
        out_specs=(VM,) * 7,
        scratch_shapes=[
            pltpu.VMEM((2, 4, 512, 64), BF),
            pltpu.VMEM((2, 4, 512, 64), BF),
            pltpu.VMEM((4, 2, 512, 64), BF),
            pltpu.VMEM((4, 2, 1, 512), F32),
            pltpu.VMEM((4, 2, 64, 512), F32),
            pltpu.VMEM((2, 512, 64), F32),
            pltpu.VMEM((2, 512, 64), F32),
            pltpu.VMEM((4, 256, 256), BF),
            pltpu.VMEM((4, 256, 256), BF),
            pltpu.VMEM((4, 256, 256), F32),
        ]
        + fold_one(SEG) * 2
        + [pltpu.VMEM((16, 16, D), BF)]
        + scatter_scratch()
        + sems(4 + 12 + 32 + SCATTER_SEMS, 5),
        compiler_params=pltpu.CompilerParams(
            collective_id=4, has_side_effects=True, vmem_limit_bytes=VLIMIT
        ),
        name="attend_back",
    )(q, kv, lse, o, do, cos, sin, part, resid, gg, gu, go)


def last_kernel(
    dqkv_ref, wq_ref, n_ref, tok_ref, dmid_ref, sga_ref, sgb_ref, sua_ref, sub_ref, sda_ref, sdb_ref,
    dtok_ref, outq_ref, outr_ref,
    part_ref, gq_ref, sumq_ref, sumr_ref, *rest,
):
    pos = Place()
    fold_s, sc_scratch, rest = rest[:12], rest[12:17], rest[17:]
    net = Net(*rest)
    tpeers = pos.tpeers()
    greet(tpeers + pos.xpeers() + pos.zpeers())
    fd = Fold(net, pos, gq_ref, fold_s[0:2], fold_s[2:4], fold_s[4:6])
    others = [
        Fold(net, pos, None, None, (sga_ref, sgb_ref), fold_s[6:8]),
        Fold(net, pos, None, None, (sua_ref, sub_ref), fold_s[8:10]),
        Fold(net, pos, None, None, (sda_ref, sdb_ref), fold_s[10:12]),
    ]
    for f in others:
        f.second()
    sc = Scatter(net, pos, part_ref, sc_scratch)

    def fill(y):
        rows = pl.ds(pl.multiple_of(y * 256, 256), 256)

        @pl.loop(0, 4)
        def _(i):
            cols = pl.ds(pl.multiple_of(i * 512, 512), 512)
            part_ref[y, :, cols] = dot_nt(dqkv_ref[rows], wq_ref[cols]).astype(BF)

    sc.start(fill)

    @pl.loop(0, 8)
    def _(i):
        cols = pl.ds(pl.multiple_of(i * 256, 256), 256)
        g = dot_tn(n_ref[:, cols], dqkv_ref[...]).astype(BF)
        gq_ref[lax.div(i, 2), lax.rem(i, 2)] = g.reshape(4, 2, 2, 16, QKV)

    fd.start()
    for i, f in enumerate(others):
        f.finish(sumr_ref.at[i])
    ship = []
    for peer in tpeers:
        ship.append(net.go(sumr_ref.at[:, peer["y"], peer["core"]], outr_ref.at[pos.t], peer))
    keep = [net.local(sumr_ref.at[:, pos.y, pos.core], outr_ref.at[pos.t])]
    sc.last()
    fd.add()
    fd.second()
    fd.finish(sumq_ref)
    for peer in tpeers:
        ship.append(net.go(sumq_ref.at[peer["y"], peer["core"]], outq_ref.at[pos.t], peer))
    keep.append(net.local(sumq_ref.at[pos.y, pos.core], outq_ref.at[pos.t]))
    sc.arrive()

    @pl.loop(0, 8)
    def _(i):
        first = pl.multiple_of(i * 16, 16)
        rows = pl.ds(first, 16)
        r = tok_ref[rows].astype(F32)
        dtok_ref[rows] = norm_back(sc.total(first), r, dmid_ref[rows]).astype(BF)

    for copy in ship + keep:
        copy.wait()
    sc.finish()


def run_last(dqkv, wq, n, tok, dmid, sums):
    return pl.pallas_call(
        last_kernel,
        out_shape=(shaped(128, D), shaped(8, 16, QKV), shaped(8, 3, 16, SEG)),
        in_specs=[VM] * 11,
        out_specs=(VM, ANY, ANY),
        scratch_shapes=[
            pltpu.VMEM((4, 256, D), BF),
            pltpu.VMEM((4, 2, 4, 2, 2, 16, QKV), BF),
            pltpu.VMEM((4, 2, 16, QKV), BF),
            pltpu.VMEM((3, 4, 2, 16, SEG), BF),
        ]
        + fold_one(QKV)
        + fold_sums(QKV)
        + fold_two(QKV)
        + fold_two(SEG) * 3
        + scatter_scratch()
        + sems(FOLD_SEMS + 18 + SCATTER_SEMS + 14, 4),
        compiler_params=pltpu.CompilerParams(
            collective_id=5, has_side_effects=True, vmem_limit_bytes=VLIMIT
        ),
        name="last",
    )(dqkv, wq, n, tok, dmid, *sums)


def rope_tables():
    half = HEAD // 2
    freq = np.exp(np.arange(half, dtype=np.float32) * np.float32(-2.0 * math.log(rope_base) / HEAD))
    spots = np.arange(2048, dtype=np.float32).reshape(4, 2, 256).transpose(1, 0, 2).reshape(2, 1024)
    angles = (spots[:, :, None] * freq.astype(np.float32)).astype(np.float32)
    angles = np.concatenate([angles] * 4, axis=2)
    return np.cos(angles).astype(np.float32), np.sin(angles).astype(np.float32)


def adam(weight, gradient, first_moment, second, step_rate, decay_weight):
    first_new = beta_one * first_moment + (1.0 - beta_one) * gradient
    second_new = beta_two * second + (1.0 - beta_two) * gradient * gradient
    first_hat = first_new / (1.0 - beta_one**STEP)
    second_hat = second_new / (1.0 - beta_two**STEP)
    weight_new = weight - step_rate * (
        first_hat / (jnp.sqrt(second_hat) + adam_eps) + decay_weight * weight
    )
    return (first_new, second_new, weight_new)


def local(
    tokens, cotangent, w_qkv, w_out, w_gate_up, w_down_t, gains,
    first_qkv, second_qkv, first_out, second_out, first_gate_up, second_gate_up,
    first_down, second_down, first_gains, second_gains,
):
    tok, cot = tokens[0], cotangent[0]
    inputs = tok.astype(F32)
    inv = lax.rsqrt(jnp.mean(inputs * inputs, axis=-1, keepdims=True) + norm_eps)
    normed = (inputs * inv).astype(BF)

    gain = gains.astype(BF).astype(F32)
    low_qkv = w_qkv.astype(BF).astype(F32)
    low_gu = w_gate_up.astype(BF).astype(F32)
    qkv_g = (low_qkv * gain[:, 0:1]).astype(BF)
    gu_g = (low_gu * gain[:, 1:2]).astype(BF)
    q_cut = qkv_g[:, :D].reshape(16, 2, 4, 4, HEAD).transpose(3, 1, 0, 2, 4).reshape(4, 2, 16, 256)
    kv_cut = jnp.concatenate(
        [qkv_g[:, D : D + 256].reshape(16, 2, 2, HEAD), qkv_g[:, D + 256 :].reshape(16, 2, 2, HEAD)],
        axis=3,
    )
    kv_cut = kv_cut.transpose(1, 0, 2, 3).reshape(1, 2, 16, 256)
    wq_blocks = jnp.concatenate(
        [q_cut, jnp.broadcast_to(kv_cut, (4, 2, 16, 256))], axis=3
    ).reshape(8, 16, QKV)

    def cut(rows):
        return rows.reshape(16, 8, SEG).transpose(1, 0, 2)

    wr_blocks = jnp.stack(
        [cut(gu_g[:, :FF]), cut(gu_g[:, FF:]), cut(w_down_t.astype(BF))], axis=1
    )

    zhi = lax.axis_index("zhi")
    cos_all, sin_all = rope_tables()
    cos = lax.dynamic_index_in_dim(jnp.asarray(cos_all), zhi, 0, keepdims=False)
    sin = lax.dynamic_index_in_dim(jnp.asarray(sin_all), zhi, 0, keepdims=False)

    qkv, n_in, wq, wo = run_first(normed, wq_blocks, w_out.astype(BF))
    n_in, wq = n_in.reshape(1024, D), wq.reshape(D, QKV)
    o, lse, q, kv, ra, rb, cotf = run_attend(qkv, cos, sin, wr_blocks, cot)
    o_rows = o.reshape(1024, 256)
    wo = wo.reshape(256, D)
    cotf = cotf.reshape(1024, D)
    resid, n_mid, wg, wu, wd = run_mid(o, wo, tok, ra, rb)
    wg, wu, wd = (w.reshape(D, SEG) for w in (wg, wu, wd))
    n_mid = n_mid.reshape(1024, D)
    d_mid, d_attn, sda, sdb, part_b, gg, gu = run_back(wg, wu, wd, n_mid, cotf, resid, cot)
    d_attn = d_attn.reshape(1024, D)
    d_o = dot_nt(d_attn, wo).astype(BF)
    go = dot_tn(o_rows, d_attn).astype(BF).reshape(4, 2, 2, 16, D)
    dqkv, block_out, sga, sgb, sua, sub, grad_out = run_attend_back(
        q, kv, lse, o, d_o.reshape(4, 256, 256), cos, sin, part_b, resid, gg, gu, go
    )
    d_tokens, sum_q, sum_r = run_last(
        dqkv, wq, n_in, tok, d_mid, (sga, sgb, sua, sub, sda, sdb)
    )

    sum_q = sum_q.reshape(4, 2, 16, QKV).astype(F32)
    grad_q = sum_q[..., :256].reshape(4, 2, 16, 4, HEAD).transpose(2, 1, 3, 0, 4).reshape(16, D)
    grad_kv = jnp.sum(sum_q[..., 256:], axis=0).reshape(2, 16, 2, 2, HEAD)
    grad_kv = grad_kv.transpose(1, 3, 0, 2, 4).reshape(16, 512)
    raw_qkv = jnp.concatenate([grad_q, grad_kv], axis=1)
    sum_r = sum_r.astype(F32)
    raw_gu = sum_r[:, 0:2].transpose(2, 1, 0, 3).reshape(16, 2 * FF)
    grad_down = sum_r[:, 2].transpose(1, 0, 2).reshape(16, FF)
    grad_qkv = raw_qkv * gain[:, 0:1]
    grad_gu = raw_gu * gain[:, 1:2]
    grad_gains = jnp.stack(
        [jnp.sum(low_qkv * raw_qkv, axis=1), jnp.sum(low_gu * raw_gu, axis=1)], axis=1
    )

    first_q, second_q, weight_q = adam(w_qkv, grad_qkv, first_qkv, second_qkv, rate_matrix, decay_rate)
    first_o, second_o, weight_o = adam(w_out, grad_out, first_out, second_out, rate_matrix, decay_rate)
    first_g, second_g, weight_g = adam(
        w_gate_up, grad_gu, first_gate_up, second_gate_up, rate_matrix, decay_rate
    )
    first_d, second_d, weight_d = adam(
        w_down_t, grad_down, first_down, second_down, rate_matrix, decay_rate
    )
    first_n, second_n, weight_n = adam(gains, grad_gains, first_gains, second_gains, rate_gain, 0.0)
    return (
        block_out[None], d_tokens[None],
        first_q, second_q, weight_q, first_o, second_o, weight_o,
        first_g, second_g, weight_g, first_d, second_d, weight_d,
        first_n, second_n, weight_n,
    )


def solution(mesh):
    fine = Mesh(mesh.devices.reshape(4, 2, 4, 2, 2), ("x", "zlo", "y", "zhi", "core"))
    dp, seq = ("x", "zlo"), ("y", "zhi", "core")
    act, row = P(dp, seq, None), P(dp + seq, None)
    return jax.shard_map(
        local,
        mesh=fine,
        in_specs=(act, act) + (row,) * 15,
        out_specs=(act, act) + (row,) * 15,
        check_vma=False,
    )
```

```python
import functools
import math

import jax
import jax.numpy as jnp
import numpy as np
from jax import lax
from jax.experimental import pallas as pl
from jax.experimental.pallas import tpu as pltpu
from jax.sharding import Mesh
from jax.sharding import PartitionSpec as P

D = 2048
HEAD = 64
FF = 5632
STEP = 10
SEG = FF // 8
QKV = 512

norm_eps = 1e-05
rope_base = 10000.0
mask_fill = -1e30
beta_one = 0.9
beta_two = 0.95
adam_eps = 1e-08
decay_rate = 0.1
rate_matrix = 0.08
rate_gain = 0.8

BF = jnp.bfloat16
F32 = jnp.float32
MESH = pl.DeviceIdType.MESH
ANY = pl.BlockSpec(memory_space=pl.ANY)
VM = pl.BlockSpec(memory_space=pltpu.VMEM)
VLIMIT = 60 * 2**20


def shaped(*shape, dtype=BF):
    return jax.ShapeDtypeStruct(shape, dtype)


class Place:
    def __init__(self):
        self.x, self.zlo, self.y = (lax.axis_index(a) for a in ("x", "zlo", "y"))
        self.zhi, self.core = lax.axis_index("zhi"), lax.axis_index("core")
        self.z = self.zhi * 2 + self.zlo
        self.t = self.y * 2 + self.core
        self.sib = {"core": 1 - self.core}
        self.right = {"y": lax.rem(self.y + 1, 4)}
        self.left = {"y": lax.rem(self.y + 3, 4)}
        self.zpart = {"zhi": 1 - self.zhi}

    def xs(self, step):
        return lax.rem(self.x + step, 4)

    def ys(self, step):
        return lax.rem(self.y + step, 4)

    def zs(self, step):
        z = lax.rem(self.z + step, 4)
        return lax.div(z, 2), lax.rem(z, 2)

    def xpeers(self):
        return [{"x": self.xs(i)} for i in (1, 2, 3)]

    def zpeers(self):
        out = []
        for i in (1, 2, 3):
            zhi, zlo = self.zs(i)
            out.append({"zhi": zhi, "zlo": zlo})
        return out

    def tpeers(self):
        return [
            {"y": self.ys(dy), "core": lax.rem(self.core + dc, 2)}
            for dy in range(4)
            for dc in range(2)
            if (dy, dc) != (0, 0)
        ]


def greet(peers):
    barrier = pltpu.get_barrier_semaphore()
    for peer in peers:
        pl.semaphore_signal(barrier, inc=1, device_id=peer, device_id_type=MESH)
    pl.semaphore_wait(barrier, len(peers))


class Net:
    def __init__(self, send, recv, local):
        self.send, self.recv, self.loc = send, recv, local
        self.n = 0
        self.m = 0

    def block(self, count):
        first = self.n
        self.n += count
        return first

    def make(self, src, dst, peer, at=None):
        if at is None:
            at = self.block(1)
        return pltpu.make_async_remote_copy(
            src, dst, self.send.at[at], self.recv.at[at], device_id=peer, device_id_type=MESH
        )

    def go(self, src, dst, peer, at=None):
        copy = self.make(src, dst, peer, at)
        copy.start()
        return copy

    def local(self, src, dst):
        copy = pltpu.make_async_copy(src, dst, self.loc.at[self.m])
        self.m += 1
        copy.start()
        return copy


def sems(remote, local):
    return [
        pltpu.SemaphoreType.DMA((remote,)),
        pltpu.SemaphoreType.DMA((remote,)),
        pltpu.SemaphoreType.DMA((max(local, 1),)),
    ]


class Gather:
    def __init__(self, net, pos, src, out, base=0, rows=128):
        self.net, self.pos, self.src, self.out = net, pos, src, out
        self.all = pl.ds(base, rows)
        self.lo, self.hi = pl.ds(base, rows // 2), pl.ds(base + rows // 2, rows // 2)

    def start(self):
        net, pos, src, lo, hi = self.net, self.pos, self.src, self.lo, self.hi
        mine = self.out.at[pos.t]
        self.r = [net.go(src.at[lo], mine.at[lo], pos.right)]
        self.l = [net.go(src.at[hi], mine.at[hi], pos.left)]
        self.r.append(net.go(src.at[hi], mine.at[hi], pos.right))
        self.l.append(net.go(src.at[lo], mine.at[lo], pos.left))
        self.s = [net.go(src.at[self.all], mine.at[self.all], pos.sib)]
        self.own = net.local(src.at[self.all], mine.at[self.all])

    def step(self):
        net, pos, out, lo, hi = self.net, self.pos, self.out, self.lo, self.hi
        from_left = out.at[pos.ys(3) * 2 + pos.core]
        from_right = out.at[pos.ys(1) * 2 + pos.core]
        self.r[0].wait_recv()
        self.r2 = net.go(from_left.at[lo], from_left.at[lo], pos.right)
        self.l[0].wait_recv()
        self.l2 = net.go(from_right.at[hi], from_right.at[hi], pos.left)
        self.r[1].wait_recv()
        self.s.append(net.go(from_left.at[self.all], from_left.at[self.all], pos.sib))
        self.l[1].wait_recv()
        self.s.append(net.go(from_right.at[self.all], from_right.at[self.all], pos.sib))

    def last(self):
        net, pos, lo, hi = self.net, self.pos, self.lo, self.hi
        far = self.out.at[pos.ys(2) * 2 + pos.core]
        self.r2.wait_recv()
        self.s.append(net.go(far.at[lo], far.at[lo], pos.sib))
        self.l2.wait_recv()
        self.s.append(net.go(far.at[hi], far.at[hi], pos.sib))

    def have(self, *which):
        for i in which:
            self.s[i].wait_recv()
        if 0 in which:
            self.own.wait()

    def finish(self):
        for copy in self.r + self.l + [self.r2, self.l2] + self.s:
            copy.wait_send()


GATHER_SEMS = 11


class Scatter:
    def __init__(self, net, pos, part, scratch, base=0, rows=128):
        self.net, self.pos, self.part, self.base, self.rows = net, pos, part, base, rows
        self.lo, self.hi = pl.ds(0, rows // 2), pl.ds(rows // 2, rows // 2)
        self.sib, self.opp, self.nb, self.far_ref, self.near = scratch
        self.c = {}

    def give(self, dy):
        pos = self.pos
        rows = pl.ds(pl.multiple_of((1 - pos.core) * 128 + self.base, 16), self.rows)
        self.c[dy] = self.net.go(self.part.at[pos.ys(dy), rows], self.sib.at[dy], pos.sib)

    def _mine(self, dy, first, count):
        pos = self.pos
        rows = pl.ds(pl.multiple_of(pos.core * 128 + self.base + first, 16), count)
        return self.part[pos.ys(dy), rows].astype(F32) + self.sib[dy, pl.ds(first, count)].astype(F32)

    def far(self):
        net, pos, h = self.net, self.pos, self.rows // 2
        self.c[2].wait_recv()
        self.far_ref[self.lo] = self._mine(2, 0, h).astype(BF)
        self.f0 = net.go(self.far_ref.at[self.lo], self.opp.at[0], pos.right)
        self.far_ref[self.hi] = self._mine(2, h, h).astype(BF)
        self.f1 = net.go(self.far_ref.at[self.hi], self.opp.at[1], pos.left)

    def right(self):
        h = self.rows // 2
        self.c[1].wait_recv()
        self.near[0, self.hi] = self._mine(1, h, h).astype(BF)
        self.r1 = self.net.go(self.near.at[0, self.hi], self.nb.at[0, self.hi], self.pos.right)

    def left(self):
        h = self.rows // 2
        self.c[3].wait_recv()
        self.near[1, self.lo] = self._mine(3, 0, h).astype(BF)
        self.l0 = self.net.go(self.near.at[1, self.lo], self.nb.at[1, self.lo], self.pos.left)

    def last(self):
        net, pos, h = self.net, self.pos, self.rows // 2
        self.f0.wait_recv()
        self.near[0, self.lo] = (self._mine(1, 0, h) + self.opp[0].astype(F32)).astype(BF)
        self.r0 = net.go(self.near.at[0, self.lo], self.nb.at[0, self.lo], pos.right)
        self.f1.wait_recv()
        self.near[1, self.hi] = (self._mine(3, h, h) + self.opp[1].astype(F32)).astype(BF)
        self.l1 = net.go(self.near.at[1, self.hi], self.nb.at[1, self.hi], pos.left)

    def arrive(self):
        for copy in (self.r1, self.l0, self.r0, self.l1, self.c[0]):
            copy.wait_recv()

    def total(self, first):
        rows = pl.ds(first, 16)
        out = self._mine(0, first, 16)
        return out + self.nb[0, rows].astype(F32) + self.nb[1, rows].astype(F32)

    def finish(self):
        for copy in (self.f0, self.f1, self.r0, self.r1, self.l0, self.l1):
            copy.wait_send()
        for copy in self.c.values():
            copy.wait_send()


SCATTER_SEMS = 10


def scatter_scratch(rows=128):
    return [
        pltpu.VMEM((4, rows, D), BF),
        pltpu.VMEM((2, rows // 2, D), BF),
        pltpu.VMEM((2, rows, D), BF),
        pltpu.VMEM((rows, D), BF),
        pltpu.VMEM((2, rows, D), BF),
    ]


def reduce(halves, pos, fill):
    one, two = halves

    def give(dy):
        if fill is not None:
            fill(pos.ys(dy))
        one.give(dy)
        two.give(dy)

    give(2)
    give(1)
    one.far()
    give(3)
    one.right()
    one.left()
    give(0)
    two.far()
    one.last()
    two.right()
    two.left()
    two.last()


class Cross:
    def __init__(self, net, pos, src, own, ra, rb):
        self.net, self.pos, self.src, self.own, self.ra, self.rb = net, pos, src, own, ra, rb

    def start(self):
        net, pos = self.net, self.pos
        dst = self.own.at[:, pos.y, pos.core]
        self.one = []
        for peer in pos.tpeers():
            self.one.append(net.go(self.src.at[peer["y"] * 2 + peer["core"]], dst, peer))
        self.mine = net.local(self.src.at[pos.t], dst)

    def step(self):
        net, pos = self.net, self.pos
        self.mine.wait()
        for copy in self.one:
            copy.wait_recv()
        part_a, part_b = self.own.at[:, pl.ds(0, 2)], self.own.at[:, pl.ds(2, 2)]
        to_a, to_b = self.ra.at[:, pos.x], self.rb.at[:, pos.zlo, :, pos.zhi]
        self.two = []
        for xp, zp in zip(pos.xpeers(), pos.zpeers()):
            self.two.append(net.go(part_a, to_a, xp))
            self.two.append(net.go(part_b, to_b, zp))
        self.keep = [net.local(part_a, to_a), net.local(part_b, to_b)]

    def finish(self):
        for copy in self.one:
            copy.wait_send()
        for copy in self.two + self.keep:
            copy.wait()


class Spread:
    def __init__(self, net, pos, ra, rb, items):
        self.net, self.pos, self.ra, self.rb, self.items = net, pos, ra, rb, items
        self.up_z, self.down_z = pos.zpeers()[0], pos.zpeers()[2]
        self.up_x, self.down_x = pos.xpeers()[0], pos.xpeers()[2]

    def start(self):
        net, pos = self.net, self.pos
        low, high = pl.ds(0, 2), pl.ds(2, 2)
        self.one, self.two, self.keep = [], [], []
        for i, out in self.items:
            a = [out.at[h, pos.zlo, low, pos.zhi] for h in (low, high)]
            b = [out.at[pos.x, h, high, :] for h in (0, 1)]
            if i is not None:
                a = [(self.ra.at[i, h], dst) for h, dst in zip((low, high), a)]
                b = [(self.rb.at[i, h], dst) for h, dst in zip((0, 1), b)]
                self.keep += [net.local(*c) for c in a + b]
            else:
                a, b = [(c, c) for c in a], [(c, c) for c in b]
            up_z, down_z, up_x, down_x = self.up_z, self.down_z, self.up_x, self.down_x
            self.one.append(
                [net.go(*a[0], up_z), net.go(*a[1], down_z), net.go(*b[0], up_x), net.go(*b[1], down_x)]
                + [net.go(*a[1], up_z), net.go(*a[0], down_z), net.go(*b[1], up_x), net.go(*b[0], down_x)]
            )

    def step(self):
        net = self.net
        low, high = pl.ds(0, 2), pl.ds(2, 2)
        up_z, down_z, up_x, down_x = self.up_z, self.down_z, self.up_x, self.down_x
        for (_, out), one in zip(self.items, self.one):
            parts = (
                (out.at[low, down_z["zlo"], low, down_z["zhi"]], up_z),
                (out.at[high, up_z["zlo"], low, up_z["zhi"]], down_z),
                (out.at[down_x["x"], 0, high, :], up_x),
                (out.at[up_x["x"], 1, high, :], down_x),
            )
            for copy, (part, peer) in zip(one, parts):
                copy.wait_recv()
                self.two.append(net.go(part, part, peer))

    def arrive(self):
        for one in self.one:
            for copy in one[4:]:
                copy.wait_recv()
        for copy in self.two:
            copy.wait_recv()
        for copy in self.keep:
            copy.wait()

    def finish(self):
        for one in self.one:
            for copy in one:
                copy.wait_send()
        for copy in self.two:
            copy.wait_send()


class OutRows:
    def __init__(self, net, pos, src, out):
        self.net, self.pos, self.src, self.out = net, pos, src, out
        self.at = net.block(7)
        self.loc = net.m
        net.m += 1
        self.half = lax.div(pos.x, 2)
        self.mine = out.at[lax.rem(pos.x, 2)]
        self.pair = self.mine.at[pos.zlo, pos.zhi]

    def _sib(self):
        return self.net.make(self.src, self.pair.at[self.pos.core], self.pos.sib, self.at)

    def _own(self):
        return pltpu.make_async_copy(
            self.src, self.pair.at[self.pos.core], self.net.loc.at[self.loc]
        )

    def _z(self):
        return [
            self.net.make(self.pair, self.pair, p, self.at + 1 + i)
            for i, p in enumerate(self.pos.zpeers())
        ]

    def _x(self):
        return [
            self.net.make(self.mine, self.mine, p, self.at + 4 + i)
            for i, p in enumerate(self.pos.xpeers())
        ]

    def start(self):
        @pl.when(self.half == self.pos.core)
        def _():
            self._own().start()

        @pl.when(self.half != self.pos.core)
        def _():
            self._sib().start()

    def step(self):
        @pl.when(self.half == self.pos.core)
        def _():
            self._own().wait()
            self._sib().wait_recv()
            for copy in self._z():
                copy.start()

    def last(self):
        @pl.when(self.half == self.pos.core)
        def _():
            for copy in self._z():
                copy.wait_recv()
            for copy in self._x():
                copy.start()

    def finish(self):
        @pl.when(self.half == self.pos.core)
        def _():
            for copy in self._z() + self._x():
                copy.wait_send()

        @pl.when(self.half != self.pos.core)
        def _():
            self._sib().wait_send()

        for i, copy in enumerate(self._x()):
            back = lax.rem(self.pos.x + 3 - i, 4)

            @pl.when(lax.div(back, 2) == self.pos.core)
            def _(copy=copy):
                copy.wait_recv()


def first_kernel(
    n_ref, wq_ref, qkv_ref, nf_ref, wqf_ref, send, recv, local
):
    pos, net = Place(), Net(send, recv, local)
    tpeers, xpeers, zpeers = pos.tpeers(), pos.xpeers(), pos.zpeers()
    greet(tpeers + xpeers + zpeers)
    x, y, zlo, zhi, core = pos.x, pos.y, pos.zlo, pos.zhi, pos.core

    small = []
    for peer in tpeers:
        t = peer["y"] * 2 + peer["core"]
        small.append(net.go(wq_ref.at[t], wqf_ref.at[x, zlo, y, zhi, core], peer))
    mine = net.local(wq_ref.at[pos.t], wqf_ref.at[x, zlo, y, zhi, core])
    gather = Gather(net, pos, n_ref, nf_ref)
    gather.start()

    mine.wait()
    for copy in small:
        copy.wait_recv()
    one = []
    for peer in xpeers:
        part = wqf_ref.at[x, zlo, pl.ds(0, 2), zhi]
        one.append(net.go(part, part, peer))
    for peer in zpeers:
        part = wqf_ref.at[x, zlo, pl.ds(2, 2), zhi]
        one.append(net.go(part, part, peer))
    for copy in one:
        copy.wait_recv()
    spread = Spread(net, pos, None, None, [(None, wqf_ref)])
    spread.start()
    gather.step()
    spread.step()
    gather.last()
    spread.arrive()
    gather.have(0, 1, 2, 3, 4)

    @pl.loop(0, 4)
    def _(i):
        w = wqf_ref[...].reshape(D, QKV)
        a = nf_ref[pl.ds(i * 2, 2)].reshape(256, D)
        qkv_ref[pl.ds(pl.multiple_of(i * 256, 256), 256)] = dot_nn(a, w).astype(BF)

    for copy in small + one:
        copy.wait_send()
    gather.finish()
    spread.finish()


def run_first(normed, wq_blocks):
    return pl.pallas_call(
        first_kernel,
        out_shape=(
            shaped(1024, QKV),
            shaped(8, 128, D),
            shaped(4, 2, 4, 2, 2, 16, QKV),
        ),
        in_specs=[VM, VM],
        out_specs=(VM, VM, VM),
        scratch_shapes=sems(7 + 6 + 8 + 4 + GATHER_SEMS, 2),
        compiler_params=pltpu.CompilerParams(
            collective_id=0, has_side_effects=True, vmem_limit_bytes=VLIMIT
        ),
        name="first",
    )(normed, wq_blocks)


def dot_nt(a, b):
    return lax.dot_general(a, b, (((1,), (1,)), ((), ())), preferred_element_type=F32)


def dot_tn(a, b):
    return lax.dot_general(a, b, (((0,), (0,)), ((), ())), preferred_element_type=F32)


def dot_nn(a, b):
    return lax.dot_general(a, b, (((1,), (0,)), ((), ())), preferred_element_type=F32)


def first_half_mask(shape):
    return (lax.broadcasted_iota(jnp.int32, shape, 1) & 63) < 32


def turn(u, cos, sin):
    rot = jnp.where(first_half_mask(u.shape), -pltpu.roll(u, 96, 1), pltpu.roll(u, 32, 1))
    return u * cos + rot * sin


def turn_back(u, cos, sin):
    v = u * sin
    rot = jnp.where(first_half_mask(u.shape), pltpu.roll(v, 96, 1), -pltpu.roll(v, 32, 1))
    return u * cos + rot


def lane_first(shape):
    return lax.broadcasted_iota(jnp.int32, shape, 1) < 64


def causal(zhi):
    key = lax.broadcasted_iota(jnp.int32, (512, 512), 0)
    query = (lax.broadcasted_iota(jnp.int32, (512, 512), 1) & 255) + zhi * 256
    return key <= query


def attend_kernel(
    qkv_ref, cos_ref, sin_ref, wout_ref, wr_ref, cot_ref,
    o_ref, lse_ref, q_ref, kv_ref, ra_ref, rb_ref, wo_ref, cotf_ref,
    k_ref, v_ref, own_ref, send, recv, local,
):
    pos, net = Place(), Net(send, recv, local)
    zhi = pos.zhi
    greet(pos.tpeers() + pos.xpeers() + pos.zpeers())
    gather = Gather(net, pos, cot_ref, cotf_ref)
    cross = Cross(net, pos, wr_ref, own_ref, ra_ref, rb_ref)
    cross.start()
    rows = OutRows(net, pos, wout_ref, wo_ref)
    rows.start()

    swap = net.block(4)
    for j in range(4):
        r = pl.ds(j * 256, 256)
        cos, sin = cos_ref[r], sin_ref[r]
        for c in range(2):
            kv = qkv_ref[r, 256 + c * 128 : 384 + c * 128].astype(F32)
            mixed = jnp.where(lane_first(kv.shape), turn(kv, cos, sin), kv)
            kv_ref[j, zhi, :, c * 128 : (c + 1) * 128] = mixed.astype(BF)
        net.go(kv_ref.at[j, zhi], kv_ref.at[j, zhi], pos.zpart, swap + j)
    rows.step()
    gather.start()
    for j in range(4):
        r = pl.ds(j * 256, 256)
        cos, sin = cos_ref[r], sin_ref[r]
        for c in range(2):
            q = turn(qkv_ref[r, c * 128 : (c + 1) * 128].astype(F32), cos, sin)
            q = q.astype(BF) * jnp.asarray(HEAD**-0.5, BF)
            q_ref[j, c, 0:256] = q[:, 0:64]
            q_ref[j, c, 256:512] = q[:, 64:128]

    def update(c, key_at, query, state, mask):
        top, norm, acc = state
        s = dot_nt(k_ref[c, key_at], query)
        if mask is not None:
            s = jnp.where(mask, s, mask_fill)
        new = jnp.maximum(top, jnp.max(s, axis=0, keepdims=True))
        p = jnp.exp(s - new)
        keep = jnp.exp(top - new)
        norm = norm * keep + jnp.sum(p, axis=0, keepdims=True)
        acc = acc * keep + dot_tn(v_ref[c, key_at], p.astype(BF))
        return new, norm, acc

    def block(qb, _):
        part = kv_ref.at[qb, zhi]
        net.make(part, part, pos.zpart, swap + qb).wait_recv()
        kv = kv_ref[qb].reshape(512, 256)
        for c in range(2):
            k_ref[c, qb] = kv[:, c * 128 : c * 128 + 64]
            v_ref[c, qb] = kv[:, c * 128 + 64 : c * 128 + 128]
        mask = causal(zhi)
        state = []
        for c in range(2):
            zero = (
                jnp.full((1, 512), mask_fill, F32),
                jnp.zeros((1, 512), F32),
                jnp.zeros((64, 512), F32),
            )
            state.append(update(c, qb, q_ref[qb, c], zero, mask))

        def more(j, held):
            return tuple(update(c, j, q_ref[qb, c], held[c], None) for c in range(2))

        state = lax.fori_loop(0, qb, more, tuple(state))
        for c in range(2):
            top, norm, acc = state[c]
            lse_ref[qb, c] = top + jnp.log(norm)
            out = (acc / norm).T
            pair = jnp.concatenate([out[0:256], out[256:512]], axis=1)
            o_ref[qb, :, c * 128 : (c + 1) * 128] = pair.astype(BF)
        return 0

    cross.step()
    block(0, 0)
    rows.last()
    block(1, 0)
    gather.step()
    block(2, 0)
    gather.last()
    block(3, 0)
    gather.have(0, 1, 2, 3, 4)
    gather.finish()
    cross.finish()
    rows.finish()
    for j in range(4):
        part = kv_ref.at[j, zhi]
        net.make(part, part, pos.zpart, swap + j).wait_send()


def run_attend(qkv, cos, sin, wout, wr_blocks, cot):
    return pl.pallas_call(
        attend_kernel,
        out_shape=(
            shaped(4, 256, 256),
            shaped(4, 2, 1, 512, dtype=F32),
            shaped(4, 2, 512, 64),
            shaped(4, 2, 256, 256),
            shaped(3, 4, 2, 2, 16, SEG),
            shaped(3, 2, 2, 2, 2, 16, SEG),
            shaped(2, 2, 2, 2, 16, D),
            shaped(8, 128, D),
        ),
        in_specs=[VM] * 6,
        out_specs=(VM, VM, VM, VM, ANY, ANY, ANY, ANY),
        scratch_shapes=[
            pltpu.VMEM((2, 4, 512, 64), BF),
            pltpu.VMEM((2, 4, 512, 64), BF),
            pltpu.VMEM((3, 4, 2, 16, SEG), BF),
        ]
        + sems(4 + 13 + 7 + GATHER_SEMS, 5),
        compiler_params=pltpu.CompilerParams(
            collective_id=1, has_side_effects=True, vmem_limit_bytes=VLIMIT
        ),
        name="attend",
    )(qkv, cos, sin, wout, wr_blocks, cot)


class Fold:
    def __init__(self, net, pos, src, scratch, sums, scratch_two):
        self.net, self.pos, self.src = net, pos, src
        self.ring = scratch
        self.sa, self.sb = sums
        if scratch_two is not None:
            self.ta, self.tb = scratch_two
        low, high = pl.ds(0, 2), pl.ds(2, 2)
        zp, xp = pos.zpeers(), pos.xpeers()
        if src is not None:
            self.axes = (
                ([src.at[:, p["zlo"], low, p["zhi"]] for p in zp], (low, high), zp),
                ([src.at[p["x"], :, high, :] for p in xp], (pl.ds(0, 1), pl.ds(1, 1)), xp),
            )

    def start(self):
        net, pos = self.net, self.pos
        self.one, self.two = [], []
        for (blocks, (lo, hi), peers), (opp, _, nb) in zip(self.axes, self.ring):
            up, far, down = blocks
            self.one.append(
                [
                    net.go(far.at[lo], opp.at[0], peers[0]),
                    net.go(far.at[hi], opp.at[1], peers[2]),
                    net.go(up.at[hi], nb.at[0, hi], peers[0]),
                    net.go(down.at[lo], nb.at[1, lo], peers[2]),
                ]
            )
        low, high = pl.ds(0, 2), pl.ds(2, 2)
        self.keep = [
            net.local(self.src.at[:, pos.zlo, low, pos.zhi], self.sa),
            net.local(self.src.at[pos.x, :, high, :], self.sb),
        ]

    def step(self):
        net = self.net
        for n, ((blocks, (lo, hi), peers), (opp, stage, nb), one) in enumerate(
            zip(self.axes, self.ring, self.one)
        ):
            up, _, down = blocks
            count = 2 - n

            for k, (block, cut, peer) in enumerate(((up, lo, peers[0]), (down, hi, peers[2]))):
                one[k].wait_recv()
                mine = block.at[cut]
                for i in range(count):
                    for j in range(2):
                        both = mine[i, j].astype(F32) + opp[k, i, j].astype(F32)
                        stage[k, i, j] = both.astype(BF)
                self.two.append(net.go(stage.at[k], nb.at[k, cut], peer))

    def add(self):
        for copy in self.keep:
            copy.wait()
        for one in self.one:
            for copy in one[2:]:
                copy.wait_recv()
        for copy in self.two:
            copy.wait_recv()
        (_, _, na), (_, _, nb) = self.ring

        @pl.loop(0, 4)
        def _(i):
            for j in range(2):
                here = self.sa[i, j].astype(F32) + na[0, i, j].astype(F32)
                self.sa[i, j] = (here + na[1, i, j].astype(F32)).astype(BF)
            lo, hi = lax.div(i, 2), lax.rem(i, 2)
            for j in range(2):
                here = self.sb[lo, j, hi].astype(F32) + nb[0, lo, j, hi].astype(F32)
                self.sb[lo, j, hi] = (here + nb[1, lo, j, hi].astype(F32)).astype(BF)

        for one in self.one:
            for copy in one:
                copy.wait_send()
        for copy in self.two:
            copy.wait_send()

    def second(self):
        net, pos = self.net, self.pos
        self.three = []
        for i, (za, xb) in enumerate(zip(pos.zpeers(), pos.xpeers())):
            self.three.append(net.go(self.sa.at[xb["x"]], self.ta.at[i], xb))
            self.three.append(net.go(self.sb.at[za["zlo"], :, za["zhi"]], self.tb.at[i], za))

    def finish(self, out):
        pos = self.pos
        for copy in self.three:
            copy.wait_recv()
        for j in range(2):
            here = self.sa[pos.x, j].astype(F32)
            for k in range(3):
                here += self.ta[k, j].astype(F32)
            out[j] = here.astype(BF)
            here = self.sb[pos.zlo, j, pos.zhi].astype(F32)
            for k in range(3):
                here += self.tb[k, j].astype(F32)
            out[2 + j] = here.astype(BF)
        for copy in self.three:
            copy.wait_send()


FOLD_ONE, FOLD_TWO = 12, 6


def fold_one(cols):
    return [
        pltpu.VMEM((2, 2, 2, 2, 16, cols), BF),
        pltpu.VMEM((2, 2, 2, 2, 16, cols), BF),
        pltpu.VMEM((2, 4, 2, 2, 16, cols), BF),
        pltpu.VMEM((2, 1, 2, 2, 2, 16, cols), BF),
        pltpu.VMEM((2, 1, 2, 2, 2, 16, cols), BF),
        pltpu.VMEM((2, 2, 2, 2, 2, 16, cols), BF),
    ]


def fold_sums(cols):
    return [pltpu.VMEM((4, 2, 2, 16, cols), BF), pltpu.VMEM((2, 2, 2, 2, 16, cols), BF)]


def fold_two(cols):
    return [pltpu.VMEM((3, 2, 2, 16, cols), BF), pltpu.VMEM((3, 2, 2, 16, cols), BF)]


def by_axis(refs):
    return tuple(refs[0:3]), tuple(refs[3:6])


def norm_back(t, r, back):
    inv = lax.rsqrt(jnp.mean(r * r, axis=-1, keepdims=True) + norm_eps)
    normed = r * inv
    return back + inv * (t - normed * jnp.mean(t * normed, axis=-1, keepdims=True))


def each16(first, count, body):
    @pl.loop(0, count // 16)
    def _(i):
        body(pl.multiple_of(first + i * 16, 16), pl.multiple_of(i * 16, 16))


def ffn_kernel(
    o_ref, wo_ref, tok_ref, cot_ref, ra_ref, rb_ref, cot_in,
    resid_ref, dmid_ref, full_ref, sda_ref, sdb_ref, sga_ref, sgb_ref, down_out, gu_out,
    wg_ref, wu_ref, wd_ref, n_ref, cotf_ref, dg_ref, du_ref, hid_ref, part_ref, blk,
    gd_ref, gg_ref, gu_ref, *rest,
):
    scr, folds, rest = (rest[:5], rest[5:10]), rest[10:22], rest[22:]
    pos, net = Place(), Net(*rest)
    bring = net.local(cot_in, cotf_ref)
    greet([pos.sib, pos.right, pos.left] + pos.xpeers() + pos.zpeers())
    spread = Spread(net, pos, ra_ref, rb_ref, [(0, wg_ref), (1, wu_ref), (2, wd_ref)])
    spread.start()

    def halves():
        return [Scatter(net, pos, part_ref, scr[h], h * 64, 64) for h in range(2)]

    def project(y):
        @pl.loop(0, 4)
        def _(i):
            cols = pl.ds(pl.multiple_of(i * 512, 512), 512)
            part_ref[y, :, cols] = dot_nn(o_ref[y], wo_ref[:, cols]).astype(BF)

    first = halves()
    reduce(first, pos, project)
    gather = [Gather(net, pos, blk, n_ref, h * 64, 64) for h in range(2)]
    for h, sc in enumerate(first):
        sc.arrive()

        def norm(row, at, sc=sc):
            rows = pl.ds(row, 16)
            r = sc.total(at) + tok_ref[rows].astype(F32)
            resid_ref[rows] = r
            inv = lax.rsqrt(jnp.mean(r * r, axis=-1, keepdims=True) + norm_eps)
            blk[rows] = (r * inv).astype(BF)

        each16(h * 64, 64, norm)
        gather[h].start()


    def whole(ref):
        return ref[...].reshape(D, SEG)

    def feed(dy):
        y = pos.ys(dy)
        rows = pl.ds(pl.multiple_of(y * 256, 256), 256)
        n = n_ref[pl.ds(y * 2, 2)].reshape(256, D)
        cot = cotf_ref[pl.ds(y * 2, 2)].reshape(256, D)
        gate, up = dot_nn(n, whole(wg_ref)), dot_nn(n, whole(wu_ref))
        d_hidden = dot_nn(cot, whole(wd_ref))
        sig = jax.nn.sigmoid(gate)
        silu = gate * sig
        hid_ref[rows] = (silu * up).astype(BF)
        dg_ref[rows] = (d_hidden * up * sig * (1.0 + gate * (1.0 - sig))).astype(BF)
        du_ref[rows] = (d_hidden * silu).astype(BF)

    spread.step()
    gather[0].step()
    bring.wait()
    spread.arrive()
    for g in gather:
        g.have(0)
    feed(0)
    gather[1].step()
    for g in gather:
        g.have(2)
    feed(1)
    for g in gather:
        g.last()
    for g in gather:
        g.have(1)
    feed(3)
    for sc in first:
        sc.finish()
    for g in gather:
        g.have(3, 4)
    feed(2)
    for g in gather:
        g.finish()

    def regress(y):
        rows = pl.ds(pl.multiple_of(y * 256, 256), 256)

        @pl.loop(0, 4)
        def _(i):
            wrows = pl.ds(i, 1)
            w_g, w_u = (w[wrows].reshape(512, SEG) for w in (wg_ref, wu_ref))
            both = dot_nt(dg_ref[rows], w_g) + dot_nt(du_ref[rows], w_u)
            part_ref[y, :, pl.ds(pl.multiple_of(i * 512, 512), 512)] = both.astype(BF)

    def grad(left, right, out, first, last):
        @pl.loop(first, last)
        def _(i):
            cols = pl.ds(pl.multiple_of(i * 256, 256), 256)
            g = dot_tn(left[:, :, cols].reshape(1024, 256), right[...]).astype(BF)
            out[lax.div(i, 2), lax.rem(i, 2)] = g.reshape(4, 2, 2, 16, SEG)

    second = halves()
    one, two = second
    fold = Fold(net, pos, gd_ref, by_axis(folds[:6]), (sda_ref, sdb_ref), None)
    fold_g = Fold(net, pos, gg_ref, by_axis(folds[6:]), (sga_ref, sgb_ref), None)

    def give(dy):
        regress(pos.ys(dy))
        one.give(dy)
        two.give(dy)

    give(2)
    give(1)
    one.far()
    give(3)
    one.right()
    one.left()
    give(0)
    two.far()
    one.last()
    two.right()
    two.left()
    grad(cotf_ref, hid_ref, gd_ref, 0, 4)
    two.last()
    gather = [Gather(net, pos, blk, full_ref, h * 64, 64) for h in range(2)]

    def norm_half(h):
        sc = second[h]
        sc.arrive()

        def norm(row, at):
            rows = pl.ds(row, 16)
            dmid = norm_back(sc.total(at), resid_ref[rows], cot_ref[rows].astype(F32))
            dmid_ref[rows] = dmid
            blk[rows] = dmid.astype(BF)

        each16(h * 64, 64, norm)
        gather[h].start()

    norm_half(0)
    grad(cotf_ref, hid_ref, gd_ref, 4, 8)
    fold.start()
    norm_half(1)
    grad(n_ref, dg_ref, gg_ref, 0, 4)
    gather[0].step()
    grad(n_ref, dg_ref, gg_ref, 4, 8)
    fold_g.start()
    gather[1].step()
    grad(n_ref, du_ref, gu_ref, 0, 4)
    fold.step()
    gather[0].last()
    grad(n_ref, du_ref, gu_ref, 4, 8)
    keep = [net.local(gu_ref, gu_out)]
    gather[1].last()
    fold_g.step()
    for sc in second:
        sc.finish()

    @pl.loop(0, 4)
    def _(y):
        rows = pl.ds(pl.multiple_of(y * 256, 256), 256)

        @pl.loop(0, 4)
        def _(i):
            w = wd_ref[pl.ds(i, 1)].reshape(512, SEG)
            cols = pl.ds(pl.multiple_of(i * 512, 512), 512)
            part_ref[y, :, cols] = dot_nt(hid_ref[rows], w).astype(BF)

    keep.append(net.local(part_ref, down_out))
    fold.add()
    fold_g.add()
    for g in gather:
        g.have(0, 1, 2, 3, 4)
        g.finish()
    spread.finish()
    for copy in keep:
        copy.wait()


def run_ffn(o, wo, tok, cot, ra, rb, cotf):
    full = shaped(4, 2, 4, 2, 2, 16, SEG)
    whole = pltpu.VMEM((4, 2, 4, 2, 2, 16, SEG), BF)
    sums = (shaped(4, 2, 2, 16, SEG), shaped(2, 2, 2, 2, 16, SEG))
    return pl.pallas_call(
        ffn_kernel,
        out_shape=(
            shaped(128, D, dtype=F32),
            shaped(128, D, dtype=F32),
            shaped(8, 128, D),
            *sums,
            *sums,
            shaped(4, 256, D),
            full,
        ),
        in_specs=[VM] * 4 + [ANY] * 3,
        out_specs=(VM, VM, ANY, VM, VM, VM, VM, ANY, ANY),
        scratch_shapes=[whole] * 3
        + [pltpu.VMEM((8, 128, D), BF)] * 2
        + [pltpu.VMEM((1024, SEG), BF)] * 3
        + [pltpu.VMEM((4, 256, D), BF), pltpu.VMEM((128, D), BF)]
        + [whole] * 3
        + scatter_scratch(64) * 2
        + fold_one(SEG) * 2
        + sems(4 * SCATTER_SEMS + 4 * GATHER_SEMS + 24 + 12 + 2 * FOLD_ONE, 24),
        compiler_params=pltpu.CompilerParams(
            collective_id=2, has_side_effects=True, vmem_limit_bytes=VLIMIT
        ),
        name="ffn",
    )(o, wo, tok, cot, ra, rb, cotf)


class OutFold:
    def __init__(self, net, pos, src, scratch):
        self.net, self.pos, self.src = net, pos, src
        self.lx, self.sx, self.lz, self.sz, self.ls = scratch
        self.at = net.block(9)
        self.keep = net.loc.at[net.m]
        net.m += 1
        self.mine = lax.div(pos.x, 2) == pos.core

    def _x(self, xh):
        pos, net = self.pos, self.net
        src = self.src.at[pl.ds(xh * 2, 2)]
        return pltpu.make_async_remote_copy(
            src, self.lx.at[pos.x], net.send.at[self.at + xh], net.recv.at[self.at + pos.x],
            device_id={"x": pos.core * 2 + xh}, device_id_type=MESH,
        )

    def _own(self):
        xh = lax.rem(self.pos.x, 2)
        return pltpu.make_async_copy(
            self.src.at[pl.ds(xh * 2, 2)], self.lx.at[self.pos.x], self.keep
        )

    def _from_x(self, x):
        net = self.net
        return pltpu.make_async_remote_copy(
            self.src.at[pl.ds(0, 2)], self.lx.at[x], net.send.at[self.at], net.recv.at[self.at + x],
            device_id=self.pos.xpeers()[0], device_id_type=MESH,
        )

    def _z(self):
        net = self.net
        out = []
        for i, p in enumerate(self.pos.zpeers()):
            src = self.sx.at[p["zlo"], p["zhi"]]
            out.append(net.make(src, self.lz.at[i], p, self.at + 4 + i))
        return out

    def _sib(self):
        return self.net.make(self.sz.at[1 - self.pos.core], self.ls, self.pos.sib, self.at + 7)

    def start(self):
        for xh in range(2):
            here = self.pos.core * 2 + xh == self.pos.x

            @pl.when(here)
            def _():
                self._own().start()

            @pl.when(jnp.logical_not(here))
            def _(xh=xh):
                self._x(xh).start()

    def step(self):
        @pl.when(self.mine)
        def _():
            self._own().wait()
            for x in range(4):

                @pl.when(self.pos.x != x)
                def _(x=x):
                    self._from_x(x).wait_recv()

            for i in range(2):
                for j in range(2):
                    for k in range(2):
                        here = self.lx[0, i, j, k].astype(F32)
                        for x in range(1, 4):
                            here += self.lx[x, i, j, k].astype(F32)
                        self.sx[i, j, k] = here.astype(BF)
            for copy in self._z():
                copy.start()

    def last(self):
        @pl.when(self.mine)
        def _():
            pos = self.pos
            for copy in self._z():
                copy.wait_recv()
            for k in range(2):
                here = self.sx[pos.zlo, pos.zhi, k].astype(F32)
                for i in range(3):
                    here += self.lz[i, k].astype(F32)
                self.sz[k] = here.astype(BF)
            self._sib().start()

    def finish(self, out):
        for xh in range(2):
            here = self.pos.core * 2 + xh == self.pos.x

            @pl.when(jnp.logical_not(here))
            def _(xh=xh):
                self._x(xh).wait_send()

        @pl.when(self.mine)
        def _():
            for copy in self._z():
                copy.wait_send()
            self._sib().wait_send()
            out[...] = self.sz[self.pos.core].astype(F32)

        @pl.when(jnp.logical_not(self.mine))
        def _():
            self._sib().wait_recv()
            out[...] = self.ls[...].astype(F32)


def out_scratch():
    return [
        pltpu.VMEM((4, 2, 2, 2, 16, D), BF),
        pltpu.VMEM((2, 2, 2, 16, D), BF),
        pltpu.VMEM((3, 2, 16, D), BF),
        pltpu.VMEM((2, 16, D), BF),
        pltpu.VMEM((16, D), BF),
    ]


def attend_back_kernel(
    q_ref, kv_ref, lse_ref, o_ref, wo_ref, cos_ref, sin_ref, resid_ref, dat_in, part_in, gu_in,
    dqkv_ref, block_ref, sua_ref, sub_ref, fo_ref,
    dat_ref, part_ref, gu_ref, go_ref,
    k_ref, v_ref, do2_ref, delta_ref, dq_ref, dk_ref, dv_ref, send_ref, got_ref, mine_ref,
    *rest,
):
    pos = Place()
    folds, rest = rest[:6], rest[6:]
    land, rest = rest[:5], rest[5:]
    scr, rest = (rest[:5], rest[5:10]), rest[10:]
    net = Net(*rest)
    zhi = pos.zhi
    bring = [net.local(dat_in.at[pl.ds(j * 2, 2)], dat_ref.at[pl.ds(j * 2, 2)]) for j in range(4)]
    bring_part, bring_gu = net.local(part_in, part_ref), net.local(gu_in, gu_ref)
    greet([pos.sib, pos.right, pos.left] + pos.xpeers() + pos.zpeers())
    one, two = halves = [Scatter(net, pos, part_ref, scr[h], h * 64, 64) for h in range(2)]
    fold = Fold(net, pos, gu_ref, by_axis(folds), (sua_ref, sub_ref), None)
    rows = OutFold(net, pos, go_ref, land)

    for j in range(4):
        kv = kv_ref[j].reshape(512, 256)
        bring[j].wait()
        d_o = dot_nt(dat_ref[pl.ds(j * 2, 2)].reshape(256, D), wo_ref[...]).astype(BF)
        for c in range(2):
            k_ref[c, j] = kv[:, c * 128 : c * 128 + 64]
            v_ref[c, j] = kv[:, c * 128 + 64 : c * 128 + 128]
            cols = slice(c * 128, (c + 1) * 128)
            do = d_o[:, cols]
            do2_ref[j, c, 0:256] = do[:, 0:64]
            do2_ref[j, c, 256:512] = do[:, 64:128]
            both = (do.astype(F32) * o_ref[j, :, cols].astype(F32)).T
            delta_ref[j, c] = jnp.concatenate(
                [
                    jnp.sum(both[0:64], axis=0, keepdims=True),
                    jnp.sum(both[64:128], axis=0, keepdims=True),
                ],
                axis=1,
            )
    bring_gu.wait()
    fold.start()
    bring_part.wait()
    for dy in (2, 1, 3, 0):
        one.give(dy)
        two.give(dy)

    @pl.loop(0, 4)
    def _(i):
        cols = pl.ds(pl.multiple_of(i * 512, 512), 512)
        left = o_ref[...].reshape(1024, 256)
        g = dot_tn(left, dat_ref[:, :, cols].reshape(1024, 512)).astype(BF)
        go_ref[:, :, :, :, cols] = g.reshape(4, 2, 2, 16, 512)

    rows.start()
    one.far()
    one.right()
    one.left()
    two.far()
    dq_ref[...] = jnp.zeros_like(dq_ref)

    swap = net.block(4)

    def pair(c, j, qb, mask):
        k, v, q, do = k_ref[c, j], v_ref[c, j], q_ref[qb, c], do2_ref[qb, c]
        p = jnp.exp(dot_nt(k, q) - lse_ref[qb, c])
        if mask is not None:
            p = jnp.where(mask, p, 0.0)
        ds = (p * (dot_nt(v, do) - delta_ref[qb, c])).astype(BF)
        dv = dot_nn(p.astype(BF), do)
        dk = dot_nn(ds, q)
        dq_ref[qb, c] += dot_tn(k, ds)
        return dk, dv

    def column(j):
        mask = causal(zhi)
        for c in range(2):
            dk, dv = pair(c, j, j, mask)
            dk_ref[c] = dk
            dv_ref[c] = dv

        def more(qb, _):
            for c in range(2):
                dk, dv = pair(c, j, qb, None)
                dk_ref[c] += dk
                dv_ref[c] += dv
            return 0

        lax.fori_loop(j + 1, 4, more, 0)
        both = jnp.concatenate([dk_ref[0], dv_ref[0], dk_ref[1], dv_ref[1]], axis=1)
        both = both.reshape(2, 256, 256)

        @pl.when(zhi == 0)
        def _():
            mine_ref[j] = both[0]
            send_ref[j] = both[1].astype(BF)

        @pl.when(zhi == 1)
        def _():
            mine_ref[j] = both[1]
            send_ref[j] = both[0].astype(BF)

        net.go(send_ref.at[j], got_ref.at[j], pos.zpart, swap + j)

    column(0)
    one.last()
    two.right()
    two.left()
    column(1)
    two.last()
    rows.step()
    fold.step()
    column(2)
    rows.last()
    column(3)

    for h, sc in enumerate(halves):
        sc.arrive()

        def block(row, at, sc=sc):
            r = pl.ds(row, 16)
            block_ref[r] = (sc.total(at) + resid_ref[r]).astype(BF)

        each16(h * 64, 64, block)

    for j in range(4):
        r = pl.ds(j * 256, 256)
        cos, sin = cos_ref[r], sin_ref[r]
        for c in range(2):
            dq = dq_ref[j, c].T * HEAD**-0.5
            dq = jnp.concatenate([dq[0:256], dq[256:512]], axis=1)
            dqkv_ref[r, c * 128 : (c + 1) * 128] = turn_back(dq, cos, sin).astype(BF)
    for j in range(4):
        r = pl.ds(j * 256, 256)
        cos, sin = cos_ref[r], sin_ref[r]
        net.make(send_ref.at[j], got_ref.at[j], pos.zpart, swap + j).wait()
        for c in range(2):
            cols = slice(c * 128, (c + 1) * 128)
            dkv = mine_ref[j, :, cols] + got_ref[j, :, cols].astype(F32)
            dkv = jnp.where(lane_first(dkv.shape), turn_back(dkv, cos, sin), dkv)
            dqkv_ref[r, 256 + c * 128 : 384 + c * 128] = dkv.astype(BF)

    fold.add()
    rows.finish(fo_ref)
    for sc in halves:
        sc.finish()


def run_attend_back(q, kv, lse, o, wo, cos, sin, resid, d_attn, part, gu):
    sums = (shaped(4, 2, 2, 16, SEG), shaped(2, 2, 2, 2, 16, SEG))
    return pl.pallas_call(
        attend_back_kernel,
        out_shape=(
            shaped(1024, QKV),
            shaped(128, D),
            *sums,
            shaped(16, D, dtype=F32),
        ),
        in_specs=[VM] * 8 + [ANY] * 3,
        out_specs=(VM,) * 5,
        scratch_shapes=[
            pltpu.VMEM((8, 128, D), BF),
            pltpu.VMEM((4, 256, D), BF),
            pltpu.VMEM((4, 2, 4, 2, 2, 16, SEG), BF),
            pltpu.VMEM((4, 2, 2, 16, D), BF),
            pltpu.VMEM((2, 4, 512, 64), BF),
            pltpu.VMEM((2, 4, 512, 64), BF),
            pltpu.VMEM((4, 2, 512, 64), BF),
            pltpu.VMEM((4, 2, 1, 512), F32),
            pltpu.VMEM((4, 2, 64, 512), F32),
            pltpu.VMEM((2, 512, 64), F32),
            pltpu.VMEM((2, 512, 64), F32),
            pltpu.VMEM((4, 256, 256), BF),
            pltpu.VMEM((4, 256, 256), BF),
            pltpu.VMEM((4, 256, 256), F32),
        ]
        + fold_one(SEG)
        + out_scratch()
        + scatter_scratch(64) * 2
        + sems(4 + FOLD_ONE + 9 + 2 * SCATTER_SEMS, 9),
        compiler_params=pltpu.CompilerParams(
            collective_id=4, has_side_effects=True, vmem_limit_bytes=VLIMIT
        ),
        name="attend_back",
    )(q, kv, lse, o, wo, cos, sin, resid, d_attn, part, gu)


def last_kernel(
    dqkv_ref, wq_ref, tok_ref, dmid_ref, n_in, sga_in, sgb_in, sua_in, sub_in, sda_in, sdb_in,
    dtok_ref, outq_ref, outr_ref,
    part_ref, gq_ref, sumq_ref, sumr_ref, n_ref, *rest,
):
    pos = Place()
    sums, rest = rest[:6], rest[6:]
    fold_s, rest = rest[:16], rest[16:]
    scr, rest = (rest[:5], rest[5:10]), rest[10:]
    net = Net(*rest)
    tpeers = pos.tpeers()
    bring = net.local(n_in, n_ref)
    held = (sga_in, sgb_in, sua_in, sub_in, sda_in, sdb_in)
    greet(tpeers + pos.xpeers() + pos.zpeers())
    fd = Fold(net, pos, gq_ref, by_axis(fold_s[:6]), fold_s[6:8], fold_s[8:10])
    others = [
        Fold(net, pos, None, None, held[2 * i : 2 * i + 2], fold_s[10 + 2 * i : 12 + 2 * i])
        for i in range(3)
    ]
    for f in others:
        f.second()
    get = [net.local(a, b) for a, b in zip(held, sums)]
    halves = [Scatter(net, pos, part_ref, scr[h], h * 64, 64) for h in range(2)]
    one, two = halves

    def give(dy):
        y = pos.ys(dy)
        rows = pl.ds(pl.multiple_of(y * 256, 256), 256)

        @pl.loop(0, 4)
        def _(i):
            cols = pl.ds(pl.multiple_of(i * 512, 512), 512)
            part_ref[y, :, cols] = dot_nt(dqkv_ref[rows], wq_ref[cols]).astype(BF)

        one.give(dy)
        two.give(dy)

    give(2)
    give(1)
    one.far()
    bring.wait()

    @pl.loop(0, 8)
    def _(i):
        cols = pl.ds(pl.multiple_of(i * 256, 256), 256)
        g = dot_tn(n_ref[:, cols], dqkv_ref[...]).astype(BF)
        gq_ref[lax.div(i, 2), lax.rem(i, 2)] = g.reshape(4, 2, 2, 16, QKV)

    fd.start()
    give(3)
    one.right()
    one.left()
    give(0)
    two.far()
    one.last()
    two.right()
    two.left()
    fd.step()
    two.last()
    for copy in get:
        copy.wait()
    for i, f in enumerate(others):
        f.sa, f.sb = sums[2 * i : 2 * i + 2]
        f.finish(sumr_ref.at[i])
    ship = []
    for peer in tpeers:
        ship.append(net.go(sumr_ref.at[:, peer["y"], peer["core"]], outr_ref.at[pos.t], peer))
    keep = [net.local(sumr_ref.at[:, pos.y, pos.core], outr_ref.at[pos.t])]
    fd.add()
    fd.second()

    def half(h):
        sc = halves[h]
        sc.arrive()

        def token(row, at):
            rows = pl.ds(row, 16)
            r = tok_ref[rows].astype(F32)
            dtok_ref[rows] = norm_back(sc.total(at), r, dmid_ref[rows]).astype(BF)

        each16(h * 64, 64, token)

    half(0)
    fd.finish(sumq_ref)
    for peer in tpeers:
        ship.append(net.go(sumq_ref.at[peer["y"], peer["core"]], outq_ref.at[pos.t], peer))
    keep.append(net.local(sumq_ref.at[pos.y, pos.core], outq_ref.at[pos.t]))
    half(1)
    for copy in ship + keep:
        copy.wait()
    for sc in halves:
        sc.finish()


def run_last(dqkv, wq, n, tok, dmid, sums):
    return pl.pallas_call(
        last_kernel,
        out_shape=(shaped(128, D), shaped(8, 16, QKV), shaped(8, 3, 16, SEG)),
        in_specs=[VM] * 4 + [ANY] * 7,
        out_specs=(VM, ANY, ANY),
        scratch_shapes=[
            pltpu.VMEM((4, 256, D), BF),
            pltpu.VMEM((4, 2, 4, 2, 2, 16, QKV), BF),
            pltpu.VMEM((4, 2, 16, QKV), BF),
            pltpu.VMEM((3, 4, 2, 16, SEG), BF),
            pltpu.VMEM((1024, D), BF),
        ]
        + fold_sums(SEG) * 3
        + fold_one(QKV)
        + fold_sums(QKV)
        + fold_two(QKV)
        + fold_two(SEG) * 3
        + scatter_scratch(64) * 2
        + sems(FOLD_ONE + 4 * FOLD_TWO + 2 * SCATTER_SEMS + 14, 11),
        compiler_params=pltpu.CompilerParams(
            collective_id=5, has_side_effects=True, vmem_limit_bytes=VLIMIT
        ),
        name="last",
    )(dqkv, wq, tok, dmid, n, *sums)


def rope_tables():
    half = HEAD // 2
    freq = np.exp(np.arange(half, dtype=np.float32) * np.float32(-2.0 * math.log(rope_base) / HEAD))
    spots = np.arange(2048, dtype=np.float32).reshape(4, 2, 256).transpose(1, 0, 2).reshape(2, 1024)
    angles = (spots[:, :, None] * freq.astype(np.float32)).astype(np.float32)
    angles = np.concatenate([angles] * 4, axis=2)
    return np.cos(angles).astype(np.float32), np.sin(angles).astype(np.float32)


def adam(weight, gradient, first_moment, second, step_rate, decay_weight):
    first_new = beta_one * first_moment + (1.0 - beta_one) * gradient
    second_new = beta_two * second + (1.0 - beta_two) * gradient * gradient
    first_hat = first_new / (1.0 - beta_one**STEP)
    second_hat = second_new / (1.0 - beta_two**STEP)
    weight_new = weight - step_rate * (
        first_hat / (jnp.sqrt(second_hat) + adam_eps) + decay_weight * weight
    )
    return (first_new, second_new, weight_new)


def local(
    tokens, cotangent, w_qkv, w_out, w_gate_up, w_down_t, gains,
    first_qkv, second_qkv, first_out, second_out, first_gate_up, second_gate_up,
    first_down, second_down, first_gains, second_gains,
):
    tok, cot = tokens[0], cotangent[0]
    inputs = tok.astype(F32)
    inv = lax.rsqrt(jnp.mean(inputs * inputs, axis=-1, keepdims=True) + norm_eps)
    normed = (inputs * inv).astype(BF)

    gain = gains.astype(BF).astype(F32)
    low_qkv = w_qkv.astype(BF).astype(F32)
    low_gu = w_gate_up.astype(BF).astype(F32)
    qkv_g = (low_qkv * gain[:, 0:1]).astype(BF)
    gu_g = (low_gu * gain[:, 1:2]).astype(BF)
    q_cut = qkv_g[:, :D].reshape(16, 2, 4, 4, HEAD).transpose(3, 1, 0, 2, 4).reshape(4, 2, 16, 256)
    kv_cut = jnp.concatenate(
        [qkv_g[:, D : D + 256].reshape(16, 2, 2, HEAD), qkv_g[:, D + 256 :].reshape(16, 2, 2, HEAD)],
        axis=3,
    )
    kv_cut = kv_cut.transpose(1, 0, 2, 3).reshape(1, 2, 16, 256)
    wq_blocks = jnp.concatenate(
        [q_cut, jnp.broadcast_to(kv_cut, (4, 2, 16, 256))], axis=3
    ).reshape(8, 16, QKV)

    def cut(rows):
        return rows.reshape(16, 8, SEG).transpose(1, 0, 2)

    wr_blocks = jnp.stack(
        [cut(gu_g[:, :FF]), cut(gu_g[:, FF:]), cut(w_down_t.astype(BF))], axis=1
    )

    zhi = lax.axis_index("zhi")
    cos_all, sin_all = rope_tables()
    cos = lax.dynamic_index_in_dim(jnp.asarray(cos_all), zhi, 0, keepdims=False)
    sin = lax.dynamic_index_in_dim(jnp.asarray(sin_all), zhi, 0, keepdims=False)

    qkv, n_in, wq = run_first(normed, wq_blocks)
    n_in, wq = n_in.reshape(1024, D), wq.reshape(D, QKV)
    o, lse, q, kv, ra, rb, wo, cotf = run_attend(
        qkv, cos, sin, w_out.astype(BF), wr_blocks, cot
    )
    wo = wo.reshape(256, D)
    resid, d_mid, d_attn, sda, sdb, sga, sgb, part_b, gu = run_ffn(
        o, wo, tok, cot, ra, rb, cotf
    )
    dqkv, block_out, sua, sub, grad_out = run_attend_back(
        q, kv, lse, o, wo, cos, sin, resid, d_attn, part_b, gu
    )
    d_tokens, sum_q, sum_r = run_last(
        dqkv, wq, n_in, tok, d_mid, (sga, sgb, sua, sub, sda, sdb)
    )

    sum_q = sum_q.reshape(4, 2, 16, QKV).astype(F32)
    grad_q = sum_q[..., :256].reshape(4, 2, 16, 4, HEAD).transpose(2, 1, 3, 0, 4).reshape(16, D)
    grad_kv = jnp.sum(sum_q[..., 256:], axis=0).reshape(2, 16, 2, 2, HEAD)
    grad_kv = grad_kv.transpose(1, 3, 0, 2, 4).reshape(16, 512)
    raw_qkv = jnp.concatenate([grad_q, grad_kv], axis=1)
    sum_r = sum_r.astype(F32)
    raw_gu = sum_r[:, 0:2].transpose(2, 1, 0, 3).reshape(16, 2 * FF)
    grad_down = sum_r[:, 2].transpose(1, 0, 2).reshape(16, FF)
    grad_qkv = raw_qkv * gain[:, 0:1]
    grad_gu = raw_gu * gain[:, 1:2]
    grad_gains = jnp.stack(
        [jnp.sum(low_qkv * raw_qkv, axis=1), jnp.sum(low_gu * raw_gu, axis=1)], axis=1
    )

    first_q, second_q, weight_q = adam(w_qkv, grad_qkv, first_qkv, second_qkv, rate_matrix, decay_rate)
    first_o, second_o, weight_o = adam(w_out, grad_out, first_out, second_out, rate_matrix, decay_rate)
    first_g, second_g, weight_g = adam(
        w_gate_up, grad_gu, first_gate_up, second_gate_up, rate_matrix, decay_rate
    )
    first_d, second_d, weight_d = adam(
        w_down_t, grad_down, first_down, second_down, rate_matrix, decay_rate
    )
    first_n, second_n, weight_n = adam(gains, grad_gains, first_gains, second_gains, rate_gain, 0.0)
    return (
        block_out[None], d_tokens[None],
        first_q, second_q, weight_q, first_o, second_o, weight_o,
        first_g, second_g, weight_g, first_d, second_d, weight_d,
        first_n, second_n, weight_n,
    )


def solution(mesh):
    fine = Mesh(mesh.devices.reshape(4, 2, 4, 2, 2), ("x", "zlo", "y", "zhi", "core"))
    dp, seq = ("x", "zlo"), ("y", "zhi", "core")
    act, row = P(dp, seq, None), P(dp + seq, None)
    return jax.shard_map(
        local,
        mesh=fine,
        in_specs=(act, act) + (row,) * 15,
        out_specs=(act, act) + (row,) * 15,
        check_vma=False,
    )
```

```python
import functools
import math

import jax
import jax.numpy as jnp
import numpy as np
from jax import lax
from jax.experimental import pallas as pl
from jax.experimental.pallas import tpu as pltpu
from jax.sharding import Mesh
from jax.sharding import PartitionSpec as P

D = 2048
HEAD = 64
FF = 5632
STEP = 10
SEG = FF // 8
QKV = 512

norm_eps = 1e-05
rope_base = 10000.0
mask_fill = -1e30
beta_one = 0.9
beta_two = 0.95
adam_eps = 1e-08
decay_rate = 0.1
rate_matrix = 0.08
rate_gain = 0.8

BF = jnp.bfloat16
F32 = jnp.float32
MESH = pl.DeviceIdType.MESH
ANY = pl.BlockSpec(memory_space=pl.ANY)
VM = pl.BlockSpec(memory_space=pltpu.VMEM)
VLIMIT = 60 * 2**20


def shaped(*shape, dtype=BF):
    return jax.ShapeDtypeStruct(shape, dtype)


class Place:
    def __init__(self):
        self.x, self.zlo, self.y = (lax.axis_index(a) for a in ("x", "zlo", "y"))
        self.zhi, self.core = lax.axis_index("zhi"), lax.axis_index("core")
        self.z = self.zhi * 2 + self.zlo
        self.t = self.y * 2 + self.core
        self.sib = {"core": 1 - self.core}
        self.right = {"y": lax.rem(self.y + 1, 4)}
        self.left = {"y": lax.rem(self.y + 3, 4)}
        self.zpart = {"zhi": 1 - self.zhi}

    def xs(self, step):
        return lax.rem(self.x + step, 4)

    def ys(self, step):
        return lax.rem(self.y + step, 4)

    def zs(self, step):
        z = lax.rem(self.z + step, 4)
        return lax.div(z, 2), lax.rem(z, 2)

    def xpeers(self):
        return [{"x": self.xs(i)} for i in (1, 2, 3)]

    def zpeers(self):
        out = []
        for i in (1, 2, 3):
            zhi, zlo = self.zs(i)
            out.append({"zhi": zhi, "zlo": zlo})
        return out

    def tpeers(self):
        return [
            {"y": self.ys(dy), "core": lax.rem(self.core + dc, 2)}
            for dy in range(4)
            for dc in range(2)
            if (dy, dc) != (0, 0)
        ]


def greet(peers):
    barrier = pltpu.get_barrier_semaphore()
    for peer in peers:
        pl.semaphore_signal(barrier, inc=1, device_id=peer, device_id_type=MESH)
    pl.semaphore_wait(barrier, len(peers))


class Net:
    def __init__(self, send, recv, local):
        self.send, self.recv, self.loc = send, recv, local
        self.n = 0
        self.m = 0

    def block(self, count):
        first = self.n
        self.n += count
        return first

    def make(self, src, dst, peer, at=None):
        if at is None:
            at = self.block(1)
        return pltpu.make_async_remote_copy(
            src, dst, self.send.at[at], self.recv.at[at], device_id=peer, device_id_type=MESH
        )

    def go(self, src, dst, peer, at=None):
        copy = self.make(src, dst, peer, at)
        copy.start()
        return copy

    def local(self, src, dst):
        copy = pltpu.make_async_copy(src, dst, self.loc.at[self.m])
        self.m += 1
        copy.start()
        return copy


def sems(remote, local):
    return [
        pltpu.SemaphoreType.DMA((remote,)),
        pltpu.SemaphoreType.DMA((remote,)),
        pltpu.SemaphoreType.DMA((max(local, 1),)),
    ]


def norm_back(t, r, back):
    inv = lax.rsqrt(jnp.mean(r * r, axis=-1, keepdims=True) + norm_eps)
    normed = r * inv
    return back + inv * (t - normed * jnp.mean(t * normed, axis=-1, keepdims=True))


def each16(first, count, body):
    @pl.loop(0, count // 16)
    def _(i):
        body(pl.multiple_of(first + i * 16, 16), pl.multiple_of(i * 16, 16))


class Gather:
    def __init__(self, net, pos, src, out, base=0, rows=128):
        self.net, self.pos, self.src, self.out = net, pos, src, out
        self.all = pl.ds(base, rows)
        self.lo, self.hi = pl.ds(base, rows // 2), pl.ds(base + rows // 2, rows // 2)

    def start(self):
        net, pos, src, lo, hi = self.net, self.pos, self.src, self.lo, self.hi
        mine = self.out.at[pos.t]
        self.r = [net.go(src.at[lo], mine.at[lo], pos.right)]
        self.l = [net.go(src.at[hi], mine.at[hi], pos.left)]
        self.r.append(net.go(src.at[hi], mine.at[hi], pos.right))
        self.l.append(net.go(src.at[lo], mine.at[lo], pos.left))
        self.s = [net.go(src.at[self.all], mine.at[self.all], pos.sib)]
        self.own = net.local(src.at[self.all], mine.at[self.all])

    def step(self):
        net, pos, out, lo, hi = self.net, self.pos, self.out, self.lo, self.hi
        from_left = out.at[pos.ys(3) * 2 + pos.core]
        from_right = out.at[pos.ys(1) * 2 + pos.core]
        self.r[0].wait_recv()
        self.r2 = net.go(from_left.at[lo], from_left.at[lo], pos.right)
        self.l[0].wait_recv()
        self.l2 = net.go(from_right.at[hi], from_right.at[hi], pos.left)
        self.r[1].wait_recv()
        self.s.append(net.go(from_left.at[self.all], from_left.at[self.all], pos.sib))
        self.l[1].wait_recv()
        self.s.append(net.go(from_right.at[self.all], from_right.at[self.all], pos.sib))

    def last(self):
        net, pos, lo, hi = self.net, self.pos, self.lo, self.hi
        far = self.out.at[pos.ys(2) * 2 + pos.core]
        self.r2.wait_recv()
        self.s.append(net.go(far.at[lo], far.at[lo], pos.sib))
        self.l2.wait_recv()
        self.s.append(net.go(far.at[hi], far.at[hi], pos.sib))

    def have(self, *which):
        for i in which:
            self.s[i].wait_recv()
        if 0 in which:
            self.own.wait()

    def finish(self):
        for copy in self.r + self.l + [self.r2, self.l2] + self.s:
            copy.wait_send()


GATHER_SEMS = 11


class Scatter:
    def __init__(self, net, pos, part, scratch, base=0, rows=128):
        self.net, self.pos, self.part, self.base, self.rows = net, pos, part, base, rows
        self.lo, self.hi = pl.ds(0, rows // 2), pl.ds(rows // 2, rows // 2)
        self.sib, self.opp, self.nb, self.far_ref, self.near = scratch
        self.c = {}

    def give(self, dy):
        pos = self.pos
        rows = pl.ds(pl.multiple_of((1 - pos.core) * 128 + self.base, 16), self.rows)
        self.c[dy] = self.net.go(self.part.at[pos.ys(dy), rows], self.sib.at[dy], pos.sib)

    def _mine(self, dy, first, count):
        pos = self.pos
        rows = pl.ds(pl.multiple_of(pos.core * 128 + self.base + first, 16), count)
        return self.part[pos.ys(dy), rows].astype(F32) + self.sib[dy, pl.ds(first, count)].astype(F32)

    def far(self):
        net, pos, h = self.net, self.pos, self.rows // 2
        self.c[2].wait_recv()
        self.far_ref[self.lo] = self._mine(2, 0, h).astype(BF)
        self.f0 = net.go(self.far_ref.at[self.lo], self.opp.at[0], pos.right)
        self.far_ref[self.hi] = self._mine(2, h, h).astype(BF)
        self.f1 = net.go(self.far_ref.at[self.hi], self.opp.at[1], pos.left)

    def right(self):
        h = self.rows // 2
        self.c[1].wait_recv()
        self.near[0, self.hi] = self._mine(1, h, h).astype(BF)
        self.r1 = self.net.go(self.near.at[0, self.hi], self.nb.at[0, self.hi], self.pos.right)

    def left(self):
        h = self.rows // 2
        self.c[3].wait_recv()
        self.near[1, self.lo] = self._mine(3, 0, h).astype(BF)
        self.l0 = self.net.go(self.near.at[1, self.lo], self.nb.at[1, self.lo], self.pos.left)

    def last(self):
        net, pos, h = self.net, self.pos, self.rows // 2
        self.f0.wait_recv()
        self.near[0, self.lo] = (self._mine(1, 0, h) + self.opp[0].astype(F32)).astype(BF)
        self.r0 = net.go(self.near.at[0, self.lo], self.nb.at[0, self.lo], pos.right)
        self.f1.wait_recv()
        self.near[1, self.hi] = (self._mine(3, h, h) + self.opp[1].astype(F32)).astype(BF)
        self.l1 = net.go(self.near.at[1, self.hi], self.nb.at[1, self.hi], pos.left)

    def arrive(self):
        for copy in (self.r1, self.l0, self.r0, self.l1, self.c[0]):
            copy.wait_recv()

    def total(self, first):
        rows = pl.ds(first, 16)
        out = self._mine(0, first, 16)
        return out + self.nb[0, rows].astype(F32) + self.nb[1, rows].astype(F32)

    def finish(self):
        for copy in (self.f0, self.f1, self.r0, self.r1, self.l0, self.l1):
            copy.wait_send()
        for copy in self.c.values():
            copy.wait_send()


SCATTER_SEMS = 10


def scatter_scratch(rows=128):
    return [
        pltpu.VMEM((4, rows, D), BF),
        pltpu.VMEM((2, rows // 2, D), BF),
        pltpu.VMEM((2, rows, D), BF),
        pltpu.VMEM((rows, D), BF),
        pltpu.VMEM((2, rows, D), BF),
    ]


def reduce(halves, pos, fill):
    one, two = halves

    def give(dy):
        if fill is not None:
            fill(pos.ys(dy))
        one.give(dy)
        two.give(dy)

    give(2)
    give(1)
    one.far()
    give(3)
    one.right()
    one.left()
    give(0)
    two.far()
    one.last()
    two.right()
    two.left()
    two.last()


class Cross:
    def __init__(self, net, pos, src, own, ra, rb):
        self.net, self.pos, self.src, self.own, self.ra, self.rb = net, pos, src, own, ra, rb

    def start(self):
        net, pos = self.net, self.pos
        dst = self.own.at[:, pos.y, pos.core]
        self.one = []
        for peer in pos.tpeers():
            self.one.append(net.go(self.src.at[peer["y"] * 2 + peer["core"]], dst, peer))
        self.mine = net.local(self.src.at[pos.t], dst)

    def step(self):
        net, pos = self.net, self.pos
        self.mine.wait()
        for copy in self.one:
            copy.wait_recv()
        part_a, part_b = self.own.at[:, pl.ds(0, 2)], self.own.at[:, pl.ds(2, 2)]
        to_a, to_b = self.ra.at[:, pos.x], self.rb.at[:, pos.zlo, :, pos.zhi]
        self.two = []
        for xp, zp in zip(pos.xpeers(), pos.zpeers()):
            self.two.append(net.go(part_a, to_a, xp))
            self.two.append(net.go(part_b, to_b, zp))
        self.keep = [net.local(part_a, to_a), net.local(part_b, to_b)]

    def finish(self):
        for copy in self.one:
            copy.wait_send()
        for copy in self.two + self.keep:
            copy.wait()


class Spread:
    def __init__(self, net, pos, ra, rb, items):
        self.net, self.pos, self.ra, self.rb, self.items = net, pos, ra, rb, items
        self.up_z, self.down_z = pos.zpeers()[0], pos.zpeers()[2]
        self.up_x, self.down_x = pos.xpeers()[0], pos.xpeers()[2]

    def start(self):
        net, pos = self.net, self.pos
        low, high = pl.ds(0, 2), pl.ds(2, 2)
        self.one, self.two, self.keep = [], [], []
        for i, out in self.items:
            a = [out.at[h, pos.zlo, low, pos.zhi] for h in (low, high)]
            b = [out.at[pos.x, h, high, :] for h in (0, 1)]
            if i is not None:
                a = [(self.ra.at[i, h], dst) for h, dst in zip((low, high), a)]
                b = [(self.rb.at[i, h], dst) for h, dst in zip((0, 1), b)]
                self.keep += [net.local(*c) for c in a + b]
            else:
                a, b = [(c, c) for c in a], [(c, c) for c in b]
            up_z, down_z, up_x, down_x = self.up_z, self.down_z, self.up_x, self.down_x
            self.one.append(
                [net.go(*a[0], up_z), net.go(*a[1], down_z), net.go(*b[0], up_x), net.go(*b[1], down_x)]
                + [net.go(*a[1], up_z), net.go(*a[0], down_z), net.go(*b[1], up_x), net.go(*b[0], down_x)]
            )

    def step(self):
        net = self.net
        low, high = pl.ds(0, 2), pl.ds(2, 2)
        up_z, down_z, up_x, down_x = self.up_z, self.down_z, self.up_x, self.down_x
        for (_, out), one in zip(self.items, self.one):
            parts = (
                (out.at[low, down_z["zlo"], low, down_z["zhi"]], up_z),
                (out.at[high, up_z["zlo"], low, up_z["zhi"]], down_z),
                (out.at[down_x["x"], 0, high, :], up_x),
                (out.at[up_x["x"], 1, high, :], down_x),
            )
            for copy, (part, peer) in zip(one, parts):
                copy.wait_recv()
                self.two.append(net.go(part, part, peer))

    def arrive(self):
        for one in self.one:
            for copy in one[4:]:
                copy.wait_recv()
        for copy in self.two:
            copy.wait_recv()
        for copy in self.keep:
            copy.wait()

    def finish(self):
        for one in self.one:
            for copy in one:
                copy.wait_send()
        for copy in self.two:
            copy.wait_send()


class OutRows:
    def __init__(self, net, pos, src, out):
        self.net, self.pos, self.src, self.out = net, pos, src, out
        self.at = net.block(7)
        self.loc = net.m
        net.m += 1
        self.half = lax.div(pos.x, 2)
        self.mine = out.at[lax.rem(pos.x, 2)]
        self.pair = self.mine.at[pos.zlo, pos.zhi]

    def _sib(self):
        return self.net.make(self.src, self.pair.at[self.pos.core], self.pos.sib, self.at)

    def _own(self):
        return pltpu.make_async_copy(
            self.src, self.pair.at[self.pos.core], self.net.loc.at[self.loc]
        )

    def _z(self):
        return [
            self.net.make(self.pair, self.pair, p, self.at + 1 + i)
            for i, p in enumerate(self.pos.zpeers())
        ]

    def _x(self):
        return [
            self.net.make(self.mine, self.mine, p, self.at + 4 + i)
            for i, p in enumerate(self.pos.xpeers())
        ]

    def start(self):
        @pl.when(self.half == self.pos.core)
        def _():
            self._own().start()

        @pl.when(self.half != self.pos.core)
        def _():
            self._sib().start()

    def step(self):
        @pl.when(self.half == self.pos.core)
        def _():
            self._own().wait()
            self._sib().wait_recv()
            for copy in self._z():
                copy.start()

    def last(self):
        @pl.when(self.half == self.pos.core)
        def _():
            for copy in self._z():
                copy.wait_recv()
            for copy in self._x():
                copy.start()

    def finish(self):
        @pl.when(self.half == self.pos.core)
        def _():
            for copy in self._z() + self._x():
                copy.wait_send()

        @pl.when(self.half != self.pos.core)
        def _():
            self._sib().wait_send()

        for i, copy in enumerate(self._x()):
            back = lax.rem(self.pos.x + 3 - i, 4)

            @pl.when(lax.div(back, 2) == self.pos.core)
            def _(copy=copy):
                copy.wait_recv()


def first_kernel(
    tok_ref, wqkv_ref, wgu_ref, wdn_ref, wout_ref, gains_ref,
    qkv_ref, nf_ref, wqf_ref, wr_ref, wol_ref, wq_ref, n_ref, send, recv, local,
):
    pos, net = Place(), Net(send, recv, local)
    tpeers, xpeers, zpeers = pos.tpeers(), pos.xpeers(), pos.zpeers()
    greet(tpeers + xpeers + zpeers)
    x, y, zlo, zhi, core = pos.x, pos.y, pos.zlo, pos.zhi, pos.core

    gain = gains_ref[...].astype(BF).astype(F32)
    w = (wqkv_ref[...].astype(BF).astype(F32) * gain[:, 0:1]).astype(BF)
    for yy in range(4):
        for cc in range(2):
            heads = [(cc * 4 + d) * 4 + yy for d in range(4)]
            for c in range(2):
                heads += [32 + cc * 2 + c, 36 + cc * 2 + c]
            cut = [w[:, h * HEAD : (h + 1) * HEAD] for h in heads]
            wq_ref[yy * 2 + cc] = jnp.concatenate(cut, axis=1)

    small = []
    for peer in tpeers:
        t = peer["y"] * 2 + peer["core"]
        small.append(net.go(wq_ref.at[t], wqf_ref.at[x, zlo, y, zhi, core], peer))
    mine = net.local(wq_ref.at[pos.t], wqf_ref.at[x, zlo, y, zhi, core])

    def norm(row, at):
        rows = pl.ds(row, 16)
        r = tok_ref[rows].astype(F32)
        inv = lax.rsqrt(jnp.mean(r * r, axis=-1, keepdims=True) + norm_eps)
        n_ref[rows] = (r * inv).astype(BF)

    each16(0, 128, norm)
    gather = Gather(net, pos, n_ref, nf_ref)
    gather.start()

    mine.wait()
    for copy in small:
        copy.wait_recv()
    one = []
    for peer in xpeers:
        part = wqf_ref.at[x, zlo, pl.ds(0, 2), zhi]
        one.append(net.go(part, part, peer))
    for peer in zpeers:
        part = wqf_ref.at[x, zlo, pl.ds(2, 2), zhi]
        one.append(net.go(part, part, peer))
    for copy in one:
        copy.wait_recv()
    spread = Spread(net, pos, None, None, [(None, wqf_ref)])
    spread.start()

    wol_ref[...] = wout_ref[...].astype(BF)
    for t in range(8):
        for i, (src, first) in enumerate(((wgu_ref, 0), (wgu_ref, FF), (wdn_ref, 0))):
            part = src[:, first + t * SEG : first + (t + 1) * SEG].astype(BF)
            if i < 2:
                part = (part.astype(F32) * gain[:, 1:2]).astype(BF)
            wr_ref[t, i] = part
    gather.step()
    spread.step()
    gather.last()
    spread.arrive()
    gather.have(0, 1, 2, 3, 4)

    @pl.loop(0, 4)
    def _(i):
        w = wqf_ref[...].reshape(D, QKV)
        a = nf_ref[pl.ds(i * 2, 2)].reshape(256, D)
        qkv_ref[pl.ds(pl.multiple_of(i * 256, 256), 256)] = dot_nn(a, w).astype(BF)

    for copy in small + one:
        copy.wait_send()
    gather.finish()
    spread.finish()


def run_first(tok, wqkv, wgu, wdn, wout, gains):
    return pl.pallas_call(
        first_kernel,
        out_shape=(
            shaped(1024, QKV),
            shaped(8, 128, D),
            shaped(4, 2, 4, 2, 2, 16, QKV),
            shaped(8, 3, 16, SEG),
            shaped(16, D),
        ),
        in_specs=[VM] * 6,
        out_specs=(VM,) * 5,
        scratch_shapes=[pltpu.VMEM((8, 16, QKV), BF), pltpu.VMEM((128, D), BF)]
        + sems(7 + 6 + 8 + 4 + GATHER_SEMS, 2),
        compiler_params=pltpu.CompilerParams(
            collective_id=0, has_side_effects=True, vmem_limit_bytes=VLIMIT
        ),
        name="first",
    )(tok, wqkv, wgu, wdn, wout, gains)


def dot_nt(a, b):
    return lax.dot_general(a, b, (((1,), (1,)), ((), ())), preferred_element_type=F32)


def dot_tn(a, b):
    return lax.dot_general(a, b, (((0,), (0,)), ((), ())), preferred_element_type=F32)


def dot_nn(a, b):
    return lax.dot_general(a, b, (((1,), (0,)), ((), ())), preferred_element_type=F32)


def first_half_mask(shape):
    return (lax.broadcasted_iota(jnp.int32, shape, 1) & 63) < 32


def turn(u, cos, sin):
    rot = jnp.where(first_half_mask(u.shape), -pltpu.roll(u, 96, 1), pltpu.roll(u, 32, 1))
    return u * cos + rot * sin


def turn_back(u, cos, sin):
    v = u * sin
    rot = jnp.where(first_half_mask(u.shape), pltpu.roll(v, 96, 1), -pltpu.roll(v, 32, 1))
    return u * cos + rot


def lane_first(shape):
    return lax.broadcasted_iota(jnp.int32, shape, 1) < 64


def causal(zhi):
    key = lax.broadcasted_iota(jnp.int32, (512, 512), 0)
    query = (lax.broadcasted_iota(jnp.int32, (512, 512), 1) & 255) + zhi * 256
    return key <= query


def attend_kernel(
    qkv_ref, wout_ref, wr_ref, cot_ref, cos_in, sin_in,
    o_ref, lse_ref, q_ref, kv_ref, ra_ref, rb_ref, wo_ref, cotf_ref,
    k_ref, v_ref, own_ref, cos_ref, sin_ref, send, recv, local,
):
    pos, net = Place(), Net(send, recv, local)
    zhi = pos.zhi
    tables = [net.local(cos_in.at[zhi], cos_ref), net.local(sin_in.at[zhi], sin_ref)]
    greet(pos.tpeers() + pos.xpeers() + pos.zpeers())
    gather = Gather(net, pos, cot_ref, cotf_ref)
    cross = Cross(net, pos, wr_ref, own_ref, ra_ref, rb_ref)
    cross.start()
    rows = OutRows(net, pos, wout_ref, wo_ref)
    rows.start()

    for copy in tables:
        copy.wait()
    swap = net.block(4)
    for j in range(4):
        r = pl.ds(j * 256, 256)
        cos, sin = cos_ref[r], sin_ref[r]
        for c in range(2):
            kv = qkv_ref[r, 256 + c * 128 : 384 + c * 128].astype(F32)
            mixed = jnp.where(lane_first(kv.shape), turn(kv, cos, sin), kv)
            kv_ref[j, zhi, :, c * 128 : (c + 1) * 128] = mixed.astype(BF)
        if j == 0:
            rows.step()
        net.go(kv_ref.at[j, zhi], kv_ref.at[j, zhi], pos.zpart, swap + j)
    gather.start()
    for j in range(4):
        r = pl.ds(j * 256, 256)
        cos, sin = cos_ref[r], sin_ref[r]
        for c in range(2):
            q = turn(qkv_ref[r, c * 128 : (c + 1) * 128].astype(F32), cos, sin)
            q = q.astype(BF) * jnp.asarray(HEAD**-0.5, BF)
            q_ref[j, c, 0:256] = q[:, 0:64]
            q_ref[j, c, 256:512] = q[:, 64:128]
        if j == 1:
            rows.last()

    def update(c, key_at, query, state, mask):
        top, norm, acc = state
        s = dot_nt(k_ref[c, key_at], query)
        if mask is not None:
            s = jnp.where(mask, s, mask_fill)
        new = jnp.maximum(top, jnp.max(s, axis=0, keepdims=True))
        p = jnp.exp(s - new)
        keep = jnp.exp(top - new)
        norm = norm * keep + jnp.sum(p, axis=0, keepdims=True)
        acc = acc * keep + dot_tn(v_ref[c, key_at], p.astype(BF))
        return new, norm, acc

    def block(qb, _):
        part = kv_ref.at[qb, zhi]
        net.make(part, part, pos.zpart, swap + qb).wait_recv()
        kv = kv_ref[qb].reshape(512, 256)
        for c in range(2):
            k_ref[c, qb] = kv[:, c * 128 : c * 128 + 64]
            v_ref[c, qb] = kv[:, c * 128 + 64 : c * 128 + 128]
        mask = causal(zhi)
        state = []
        for c in range(2):
            zero = (
                jnp.full((1, 512), mask_fill, F32),
                jnp.zeros((1, 512), F32),
                jnp.zeros((64, 512), F32),
            )
            state.append(update(c, qb, q_ref[qb, c], zero, mask))

        def more(j, held):
            return tuple(update(c, j, q_ref[qb, c], held[c], None) for c in range(2))

        state = lax.fori_loop(0, qb, more, tuple(state))
        for c in range(2):
            top, norm, acc = state[c]
            lse_ref[qb, c] = top + jnp.log(norm)
            out = (acc / norm).T
            pair = jnp.concatenate([out[0:256], out[256:512]], axis=1)
            o_ref[qb, :, c * 128 : (c + 1) * 128] = pair.astype(BF)
        return 0

    cross.step()
    block(0, 0)
    block(1, 0)
    gather.step()
    block(2, 0)
    gather.last()
    block(3, 0)
    gather.have(0, 1, 2, 3, 4)
    gather.finish()
    cross.finish()
    rows.finish()
    for j in range(4):
        part = kv_ref.at[j, zhi]
        net.make(part, part, pos.zpart, swap + j).wait_send()


def run_attend(qkv, wout, wr_blocks, cot, cos, sin):
    return pl.pallas_call(
        attend_kernel,
        out_shape=(
            shaped(4, 256, 256),
            shaped(4, 2, 1, 512, dtype=F32),
            shaped(4, 2, 512, 64),
            shaped(4, 2, 256, 256),
            shaped(3, 4, 2, 2, 16, SEG),
            shaped(3, 2, 2, 2, 2, 16, SEG),
            shaped(2, 2, 2, 2, 16, D),
            shaped(8, 128, D),
        ),
        in_specs=[VM] * 4 + [ANY] * 2,
        out_specs=(VM, VM, VM, VM, ANY, ANY, ANY, ANY),
        scratch_shapes=[
            pltpu.VMEM((2, 4, 512, 64), BF),
            pltpu.VMEM((2, 4, 512, 64), BF),
            pltpu.VMEM((3, 4, 2, 16, SEG), BF),
            pltpu.VMEM((1024, 128), F32),
            pltpu.VMEM((1024, 128), F32),
        ]
        + sems(4 + 13 + 7 + GATHER_SEMS, 7),
        compiler_params=pltpu.CompilerParams(
            collective_id=1, has_side_effects=True, vmem_limit_bytes=VLIMIT
        ),
        name="attend",
    )(qkv, wout, wr_blocks, cot, cos, sin)


class Fold:
    def __init__(self, net, pos, src, scratch, sums, scratch_two):
        self.net, self.pos, self.src = net, pos, src
        self.ring = scratch
        self.sa, self.sb = sums
        if scratch_two is not None:
            self.ta, self.tb = scratch_two
        low, high = pl.ds(0, 2), pl.ds(2, 2)
        zp, xp = pos.zpeers(), pos.xpeers()
        if src is not None:
            self.axes = (
                ([src.at[:, p["zlo"], low, p["zhi"]] for p in zp], (low, high), zp),
                ([src.at[p["x"], :, high, :] for p in xp], (pl.ds(0, 1), pl.ds(1, 1)), xp),
            )

    def start(self):
        net, pos = self.net, self.pos
        self.one, self.two = [], []
        for (blocks, (lo, hi), peers), (opp, _, nb) in zip(self.axes, self.ring):
            up, far, down = blocks
            self.one.append(
                [
                    net.go(far.at[lo], opp.at[0], peers[0]),
                    net.go(far.at[hi], opp.at[1], peers[2]),
                    net.go(up.at[hi], nb.at[0, hi], peers[0]),
                    net.go(down.at[lo], nb.at[1, lo], peers[2]),
                ]
            )
        low, high = pl.ds(0, 2), pl.ds(2, 2)
        self.keep = [
            net.local(self.src.at[:, pos.zlo, low, pos.zhi], self.sa),
            net.local(self.src.at[pos.x, :, high, :], self.sb),
        ]

    def step(self):
        net = self.net
        for n, ((blocks, (lo, hi), peers), (opp, stage, nb), one) in enumerate(
            zip(self.axes, self.ring, self.one)
        ):
            up, _, down = blocks
            count = 2 - n

            for k, (block, cut, peer) in enumerate(((up, lo, peers[0]), (down, hi, peers[2]))):
                one[k].wait_recv()
                mine = block.at[cut]
                for i in range(count):
                    for j in range(2):
                        both = mine[i, j].astype(F32) + opp[k, i, j].astype(F32)
                        stage[k, i, j] = both.astype(BF)
                self.two.append(net.go(stage.at[k], nb.at[k, cut], peer))

    def add(self):
        for copy in self.keep:
            copy.wait()
        for one in self.one:
            for copy in one[2:]:
                copy.wait_recv()
        for copy in self.two:
            copy.wait_recv()
        (_, _, na), (_, _, nb) = self.ring

        @pl.loop(0, 4)
        def _(i):
            for j in range(2):
                here = self.sa[i, j].astype(F32) + na[0, i, j].astype(F32)
                self.sa[i, j] = (here + na[1, i, j].astype(F32)).astype(BF)
            lo, hi = lax.div(i, 2), lax.rem(i, 2)
            for j in range(2):
                here = self.sb[lo, j, hi].astype(F32) + nb[0, lo, j, hi].astype(F32)
                self.sb[lo, j, hi] = (here + nb[1, lo, j, hi].astype(F32)).astype(BF)

        for one in self.one:
            for copy in one:
                copy.wait_send()
        for copy in self.two:
            copy.wait_send()

    def second(self):
        net, pos = self.net, self.pos
        self.three = []
        for i, (za, xb) in enumerate(zip(pos.zpeers(), pos.xpeers())):
            self.three.append(net.go(self.sa.at[xb["x"]], self.ta.at[i], xb))
            self.three.append(net.go(self.sb.at[za["zlo"], :, za["zhi"]], self.tb.at[i], za))

    def finish(self, out, own=None):
        pos = self.pos
        if own is None:
            own = (self.sa.at[pos.x], self.sb.at[pos.zlo, :, pos.zhi])
        for copy in self.three:
            copy.wait_recv()
        for j in range(2):
            here = own[0][j].astype(F32)
            for k in range(3):
                here += self.ta[k, j].astype(F32)
            out[j] = here.astype(BF)
            here = own[1][j].astype(F32)
            for k in range(3):
                here += self.tb[k, j].astype(F32)
            out[2 + j] = here.astype(BF)
        for copy in self.three:
            copy.wait_send()


FOLD_ONE, FOLD_TWO = 12, 6


def fold_one(cols):
    return [
        pltpu.VMEM((2, 2, 2, 2, 16, cols), BF),
        pltpu.VMEM((2, 2, 2, 2, 16, cols), BF),
        pltpu.VMEM((2, 4, 2, 2, 16, cols), BF),
        pltpu.VMEM((2, 1, 2, 2, 2, 16, cols), BF),
        pltpu.VMEM((2, 1, 2, 2, 2, 16, cols), BF),
        pltpu.VMEM((2, 2, 2, 2, 2, 16, cols), BF),
    ]


def fold_sums(cols):
    return [pltpu.VMEM((4, 2, 2, 16, cols), BF), pltpu.VMEM((2, 2, 2, 2, 16, cols), BF)]


def fold_two(cols):
    return [pltpu.VMEM((3, 2, 2, 16, cols), BF), pltpu.VMEM((3, 2, 2, 16, cols), BF)]


def by_axis(refs):
    return tuple(refs[0:3]), tuple(refs[3:6])


def ffn_kernel(
    o_ref, wo_ref, tok_ref, cot_ref, ra_ref, rb_ref, cot_in,
    resid_ref, dmid_ref, full_ref, sumd_ref, sga_ref, sgb_ref, down_out, gu_out,
    wg_ref, wu_ref, wd_ref, n_ref, cotf_ref, dg_ref, du_ref, hid_ref, part_ref, blk,
    gd_ref, gg_ref, gu_ref, *rest,
):
    scr, folds, rest = (rest[:5], rest[5:10]), rest[10:26], rest[26:]
    pos, net = Place(), Net(*rest)
    bring = net.local(cot_in, cotf_ref)
    greet([pos.sib, pos.right, pos.left] + pos.xpeers() + pos.zpeers())
    sp_d, sp_g, sp_u = (
        Spread(net, pos, ra_ref, rb_ref, [item]) for item in ((2, wd_ref), (0, wg_ref), (1, wu_ref))
    )
    for sp in (sp_d, sp_g, sp_u):
        sp.start()

    def halves():
        return [Scatter(net, pos, part_ref, scr[h], h * 64, 64) for h in range(2)]

    def project(y):
        @pl.loop(0, 4)
        def _(i):
            cols = pl.ds(pl.multiple_of(i * 512, 512), 512)
            part_ref[y, :, cols] = dot_nn(o_ref[y], wo_ref[:, cols]).astype(BF)

    first = halves()
    reduce(first, pos, project)
    gather = [Gather(net, pos, blk, n_ref, h * 64, 64) for h in range(2)]
    for h, sc in enumerate(first):
        sc.arrive()

        def norm(row, at, sc=sc):
            rows = pl.ds(row, 16)
            r = sc.total(at) + tok_ref[rows].astype(F32)
            resid_ref[rows] = r
            inv = lax.rsqrt(jnp.mean(r * r, axis=-1, keepdims=True) + norm_eps)
            blk[rows] = (r * inv).astype(BF)

        each16(h * 64, 64, norm)
        gather[h].start()

    def whole(ref):
        return ref[...].reshape(D, SEG)

    def spans(y):
        return pl.ds(pl.multiple_of(y * 256, 256), 256)

    def feed(dy):
        y = pos.ys(dy)
        rows = spans(y)
        n = n_ref[pl.ds(y * 2, 2)].reshape(256, D)
        gate, up = dot_nn(n, whole(wg_ref)), dot_nn(n, whole(wu_ref))
        d_hidden = dot_nn(cotf_ref[pl.ds(y * 2, 2)].reshape(256, D), whole(wd_ref))
        sig = jax.nn.sigmoid(gate)
        silu = gate * sig
        hid_ref[rows] = (silu * up).astype(BF)
        dg_ref[rows] = (d_hidden * up * sig * (1.0 + gate * (1.0 - sig))).astype(BF)
        du_ref[rows] = (d_hidden * silu).astype(BF)

    sp_d.step()
    sp_g.step()
    sp_u.step()
    gather[0].step()
    gather[1].step()

    for sc in first:
        sc.finish()
    gather[0].last()
    gather[1].last()
    for g in gather:
        g.have(0, 1, 2, 3, 4)
        g.finish()
    bring.wait()
    for sp in (sp_d, sp_g, sp_u):
        sp.arrive()

    def regress(y):
        rows = pl.ds(pl.multiple_of(y * 256, 256), 256)

        @pl.loop(0, 4)
        def _(i):
            wrows = pl.ds(i, 1)
            w_g, w_u = (w[wrows].reshape(512, SEG) for w in (wg_ref, wu_ref))
            both = dot_nt(dg_ref[rows], w_g) + dot_nt(du_ref[rows], w_u)
            part_ref[y, :, pl.ds(pl.multiple_of(i * 512, 512), 512)] = both.astype(BF)

    def grad(left, right, out, first, last, base=0):
        @pl.loop(first, last)
        def _(i):
            cols = pl.ds(pl.multiple_of(i * 256, 256), 256)
            g = dot_tn(left[:, :, cols].reshape(1024, 256), right[...]).astype(BF)
            out[lax.div(i, 2) - base, lax.rem(i, 2)] = g.reshape(4, 2, 2, 16, SEG)

    second = halves()
    one, two = second
    fold = Fold(net, pos, gd_ref, by_axis(folds[:6]), folds[6:8], folds[8:10])
    fold_g = Fold(net, pos, gg_ref, by_axis(folds[10:]), (sga_ref, sgb_ref), None)

    def give(dy):
        feed(dy)
        regress(pos.ys(dy))
        one.give(dy)
        two.give(dy)

    give(2)
    one.far()
    two.far()
    give(1)
    one.right()
    two.right()
    give(3)
    one.left()
    two.left()
    one.last()
    give(0)
    two.last()
    grad(cotf_ref, hid_ref, gd_ref, 0, 4)
    gather = [Gather(net, pos, blk, full_ref, h * 64, 64) for h in range(2)]

    def norm_half(h):
        sc = second[h]
        sc.arrive()

        def norm(row, at):
            rows = pl.ds(row, 16)
            dmid = norm_back(sc.total(at), resid_ref[rows], cot_ref[rows].astype(F32))
            dmid_ref[rows] = dmid
            blk[rows] = dmid.astype(BF)

        each16(h * 64, 64, norm)
        gather[h].start()

    norm_half(0)
    grad(cotf_ref, hid_ref, gd_ref, 4, 8)
    fold.start()
    norm_half(1)
    grad(n_ref, dg_ref, gg_ref, 0, 4)
    gather[0].step()
    grad(n_ref, dg_ref, gg_ref, 4, 8)
    fold_g.start()
    gather[1].step()
    grad(n_ref, du_ref, gu_ref, 0, 4)
    half_u = net.local(gu_ref, gu_out.at[pl.ds(0, 2)])
    fold.step()
    gather[0].last()
    half_u.wait()
    grad(n_ref, du_ref, gu_ref, 4, 8, 2)
    keep = [net.local(gu_ref, gu_out.at[pl.ds(2, 2)])]
    gather[1].last()
    fold_g.step()
    for sc in second:
        sc.finish()

    def down(first, last):
        @pl.loop(first, last)
        def _(y):
            rows = pl.ds(pl.multiple_of(y * 256, 256), 256)

            @pl.loop(0, 4)
            def _(i):
                w = wd_ref[pl.ds(i, 1)].reshape(512, SEG)
                cols = pl.ds(pl.multiple_of(i * 512, 512), 512)
                part_ref[y, :, cols] = dot_nt(hid_ref[rows], w).astype(BF)

    down(0, 2)
    fold.add()
    fold.second()
    down(2, 4)
    keep.append(net.local(part_ref, down_out))
    fold_g.add()
    fold.finish(sumd_ref)
    for g in gather:
        g.have(0, 1, 2, 3, 4)
        g.finish()
    for sp in (sp_d, sp_g, sp_u):
        sp.finish()
    for copy in keep:
        copy.wait()


def run_ffn(o, wo, tok, cot, ra, rb, cotf):
    full = shaped(4, 2, 4, 2, 2, 16, SEG)
    whole = pltpu.VMEM((4, 2, 4, 2, 2, 16, SEG), BF)
    sums = (shaped(4, 2, 2, 16, SEG), shaped(2, 2, 2, 2, 16, SEG))
    return pl.pallas_call(
        ffn_kernel,
        out_shape=(
            shaped(128, D, dtype=F32),
            shaped(128, D, dtype=F32),
            shaped(8, 128, D),
            shaped(4, 2, 16, SEG),
            *sums,
            shaped(4, 256, D),
            full,
        ),
        in_specs=[VM] * 4 + [ANY] * 3,
        out_specs=(VM, VM, ANY, VM, VM, VM, ANY, ANY),
        scratch_shapes=[whole] * 3
        + [pltpu.VMEM((8, 128, D), BF)] * 2
        + [pltpu.VMEM((1024, SEG), BF)] * 3
        + [pltpu.VMEM((4, 256, D), BF), pltpu.VMEM((128, D), BF)]
        + [whole] * 2
        + [pltpu.VMEM((2, 2, 4, 2, 2, 16, SEG), BF)]
        + scatter_scratch(64) * 2
        + (fold_one(SEG) + fold_sums(SEG) + fold_two(SEG))
        + fold_one(SEG)
        + sems(4 * SCATTER_SEMS + 4 * GATHER_SEMS + 24 + 12 + 2 * FOLD_ONE + FOLD_TWO, 24),
        compiler_params=pltpu.CompilerParams(
            collective_id=2, has_side_effects=True, vmem_limit_bytes=VLIMIT
        ),
        name="ffn",
    )(o, wo, tok, cot, ra, rb, cotf)


class OutFold:
    def __init__(self, net, pos, src, scratch):
        self.net, self.pos, self.src = net, pos, src
        self.lx, self.sx, self.lz, self.sz, self.ls = scratch
        self.at = net.block(9)
        self.keep = net.loc.at[net.m]
        net.m += 1
        self.mine = lax.div(pos.x, 2) == pos.core

    def _x(self, xh):
        pos, net = self.pos, self.net
        src = self.src.at[pl.ds(xh * 2, 2)]
        return pltpu.make_async_remote_copy(
            src, self.lx.at[pos.x], net.send.at[self.at + xh], net.recv.at[self.at + pos.x],
            device_id={"x": pos.core * 2 + xh}, device_id_type=MESH,
        )

    def _own(self):
        xh = lax.rem(self.pos.x, 2)
        return pltpu.make_async_copy(
            self.src.at[pl.ds(xh * 2, 2)], self.lx.at[self.pos.x], self.keep
        )

    def _from_x(self, x):
        net = self.net
        return pltpu.make_async_remote_copy(
            self.src.at[pl.ds(0, 2)], self.lx.at[x], net.send.at[self.at], net.recv.at[self.at + x],
            device_id=self.pos.xpeers()[0], device_id_type=MESH,
        )

    def _z(self):
        net = self.net
        out = []
        for i, p in enumerate(self.pos.zpeers()):
            src = self.sx.at[p["zlo"], p["zhi"]]
            out.append(net.make(src, self.lz.at[i], p, self.at + 4 + i))
        return out

    def _sib(self):
        return self.net.make(self.sz.at[1 - self.pos.core], self.ls, self.pos.sib, self.at + 7)

    def start(self):
        for xh in range(2):
            here = self.pos.core * 2 + xh == self.pos.x

            @pl.when(here)
            def _():
                self._own().start()

            @pl.when(jnp.logical_not(here))
            def _(xh=xh):
                self._x(xh).start()

    def step(self):
        @pl.when(self.mine)
        def _():
            self._own().wait()
            for x in range(4):

                @pl.when(self.pos.x != x)
                def _(x=x):
                    self._from_x(x).wait_recv()

            for i in range(2):
                for j in range(2):
                    for k in range(2):
                        here = self.lx[0, i, j, k].astype(F32)
                        for x in range(1, 4):
                            here += self.lx[x, i, j, k].astype(F32)
                        self.sx[i, j, k] = here.astype(BF)
            for copy in self._z():
                copy.start()

    def last(self):
        @pl.when(self.mine)
        def _():
            pos = self.pos
            for copy in self._z():
                copy.wait_recv()
            for k in range(2):
                here = self.sx[pos.zlo, pos.zhi, k].astype(F32)
                for i in range(3):
                    here += self.lz[i, k].astype(F32)
                self.sz[k] = here.astype(BF)
            self._sib().start()

    def finish(self, out):
        for xh in range(2):
            here = self.pos.core * 2 + xh == self.pos.x

            @pl.when(jnp.logical_not(here))
            def _(xh=xh):
                self._x(xh).wait_send()

        @pl.when(self.mine)
        def _():
            for copy in self._z():
                copy.wait_send()
            self._sib().wait_send()
            out[...] = self.sz[self.pos.core].astype(F32)

        @pl.when(jnp.logical_not(self.mine))
        def _():
            self._sib().wait_recv()
            out[...] = self.ls[...].astype(F32)


def out_scratch():
    return [
        pltpu.VMEM((4, 2, 2, 2, 16, D), BF),
        pltpu.VMEM((2, 2, 2, 16, D), BF),
        pltpu.VMEM((3, 2, 16, D), BF),
        pltpu.VMEM((2, 16, D), BF),
        pltpu.VMEM((16, D), BF),
    ]


def tail_kernel(
    q_ref, kv_ref, lse_ref, o_ref, wo_ref, resid_ref, tok_ref, dmid_ref, wq_ref,
    cos_in, sin_in, dat_in, part_in, gu_in, n_in, sumd_in, sga_in, sgb_in,
    block_ref, dtok_ref, fo_ref, outq_ref, outr_ref,
    dqkv_ref, dat_ref, part_ref, gu_ref, go_ref, gq_ref, sumq_ref, sumr_ref, cos_ref, sin_ref,
    k_ref, v_ref, do2_ref, delta_ref, dq_ref, dk_ref, dv_ref, send_ref, got_ref, mine_ref,
    *rest,
):
    pos = Place()
    rest = list(rest)

    def take(count):
        out = rest[:count]
        del rest[:count]
        return out

    one_u, sums_u, two_u = take(6), take(2), take(2)
    one_q, sums_q, two_q = take(6), take(2), take(2)
    own_g, two_g = take(2), take(2)
    land, scr_a, scr_b = take(5), [take(5), take(5)], [take(5), take(5)]
    net = Net(*rest)
    zhi = pos.zhi
    bring = [net.local(dat_in.at[pl.ds(j * 2, 2)], dat_ref.at[pl.ds(j * 2, 2)]) for j in range(4)]
    bring_part, bring_gu = net.local(part_in, part_ref), net.local(gu_in, gu_ref)
    get = [net.local(cos_in.at[zhi], cos_ref), net.local(sin_in.at[zhi], sin_ref)]
    get.append(net.local(sga_in.at[pos.x], own_g[0]))
    get.append(net.local(sgb_in.at[pos.zlo, :, pos.zhi], own_g[1]))
    tpeers = pos.tpeers()
    greet(tpeers + pos.xpeers() + pos.zpeers())
    one, two = halves = [Scatter(net, pos, part_ref, scr_a[h], h * 64, 64) for h in range(2)]
    fold = Fold(net, pos, gu_ref, by_axis(one_u), sums_u, two_u)
    fold_q = Fold(net, pos, gq_ref, by_axis(one_q), sums_q, two_q)
    fold_g = Fold(net, pos, None, None, (sga_in, sgb_in), two_g)
    rows = OutFold(net, pos, go_ref, land)
    fold_g.second()
    ship, keep = [], []

    def send_off(i, src):
        for peer in tpeers:
            ship.append(net.go(src.at[peer["y"], peer["core"]], outr_ref.at[pos.t, i], peer))
        keep.append(net.local(src.at[pos.y, pos.core], outr_ref.at[pos.t, i]))

    send_off(2, sumd_in)

    for j in range(4):
        kv = kv_ref[j].reshape(512, 256)
        bring[j].wait()
        d_o = dot_nt(dat_ref[pl.ds(j * 2, 2)].reshape(256, D), wo_ref[...]).astype(BF)
        for c in range(2):
            k_ref[c, j] = kv[:, c * 128 : c * 128 + 64]
            v_ref[c, j] = kv[:, c * 128 + 64 : c * 128 + 128]
            cols = slice(c * 128, (c + 1) * 128)
            do = d_o[:, cols]
            do2_ref[j, c, 0:256] = do[:, 0:64]
            do2_ref[j, c, 256:512] = do[:, 64:128]
            both = (do.astype(F32) * o_ref[j, :, cols].astype(F32)).T
            delta_ref[j, c] = jnp.concatenate(
                [
                    jnp.sum(both[0:64], axis=0, keepdims=True),
                    jnp.sum(both[64:128], axis=0, keepdims=True),
                ],
                axis=1,
            )
    bring_gu.wait()
    fold.start()
    bring_part.wait()
    for dy in (2, 1, 3, 0):
        one.give(dy)
        two.give(dy)

    @pl.loop(0, 4)
    def _(i):
        cols = pl.ds(pl.multiple_of(i * 512, 512), 512)
        left = o_ref[...].reshape(1024, 256)
        g = dot_tn(left, dat_ref[:, :, cols].reshape(1024, 512)).astype(BF)
        go_ref[:, :, :, :, cols] = g.reshape(4, 2, 2, 16, 512)

    bring_n = net.local(n_in, dat_ref)
    rows.start()
    one.far()
    one.right()
    one.left()
    two.far()
    dq_ref[...] = jnp.zeros_like(dq_ref)

    swap = net.block(4)

    def pair(c, j, qb, mask):
        k, v, q, do = k_ref[c, j], v_ref[c, j], q_ref[qb, c], do2_ref[qb, c]
        p = jnp.exp(dot_nt(k, q) - lse_ref[qb, c])
        if mask is not None:
            p = jnp.where(mask, p, 0.0)
        ds = (p * (dot_nt(v, do) - delta_ref[qb, c])).astype(BF)
        dv = dot_nn(p.astype(BF), do)
        dk = dot_nn(ds, q)
        dq_ref[qb, c] += dot_tn(k, ds)
        return dk, dv

    def column(j):
        mask = causal(zhi)
        for c in range(2):
            dk, dv = pair(c, j, j, mask)
            dk_ref[c] = dk
            dv_ref[c] = dv

        def more(qb, _):
            for c in range(2):
                dk, dv = pair(c, j, qb, None)
                dk_ref[c] += dk
                dv_ref[c] += dv
            return 0

        lax.fori_loop(j + 1, 4, more, 0)
        both = jnp.concatenate([dk_ref[0], dv_ref[0], dk_ref[1], dv_ref[1]], axis=1)
        both = both.reshape(2, 256, 256)

        @pl.when(zhi == 0)
        def _():
            mine_ref[j] = both[0]
            send_ref[j] = both[1].astype(BF)

        @pl.when(zhi == 1)
        def _():
            mine_ref[j] = both[1]
            send_ref[j] = both[0].astype(BF)

        net.go(send_ref.at[j], got_ref.at[j], pos.zpart, swap + j)

    def queries(j):
        r = pl.ds(j * 256, 256)
        cos, sin = cos_ref[r], sin_ref[r]
        for c in range(2):
            dq = dq_ref[j, c].T * HEAD**-0.5
            dq = jnp.concatenate([dq[0:256], dq[256:512]], axis=1)
            dqkv_ref[r, c * 128 : (c + 1) * 128] = turn_back(dq, cos, sin).astype(BF)

    def keys(j):
        r = pl.ds(j * 256, 256)
        cos, sin = cos_ref[r], sin_ref[r]
        net.make(send_ref.at[j], got_ref.at[j], pos.zpart, swap + j).wait()
        for c in range(2):
            cols = slice(c * 128, (c + 1) * 128)
            dkv = mine_ref[j, :, cols] + got_ref[j, :, cols].astype(F32)
            dkv = jnp.where(lane_first(dkv.shape), turn_back(dkv, cos, sin), dkv)
            dqkv_ref[r, 256 + c * 128 : 384 + c * 128] = dkv.astype(BF)

    column(0)
    one.last()
    two.right()
    two.left()
    for copy in get:
        copy.wait()
    queries(0)
    column(1)
    two.last()
    rows.step()
    fold.step()
    queries(1)
    keys(0)
    column(2)
    rows.last()
    queries(2)
    keys(1)
    fold_g.finish(sumr_ref.at[0], own_g)
    send_off(0, sumr_ref.at[0])
    fold.add()
    fold.second()
    column(3)
    queries(3)
    for h, sc in enumerate(halves):
        sc.arrive()

        def block(row, at, sc=sc):
            r = pl.ds(row, 16)
            block_ref[r] = (sc.total(at) + resid_ref[r]).astype(BF)

        each16(h * 64, 64, block)

    for sc in halves:
        sc.finish()
    bring_n.wait()

    def grad(at, count):
        @pl.loop(0, 8)
        def _(i):
            cols = pl.ds(pl.multiple_of(i * 256, 256), 256)
            left = dat_ref[:, :, cols].reshape(1024, 256)
            g = dot_tn(left, dqkv_ref[:, at : at + count]).astype(BF)
            out = gq_ref.at[lax.div(i, 2), lax.rem(i, 2)]
            out[:, :, :, :, at : at + count] = g.reshape(4, 2, 2, 16, count)

    grad(0, 256)
    keys(2)
    keys(3)
    grad(256, 256)
    fold_q.start()
    one, two = halves = [Scatter(net, pos, part_ref, scr_b[h], h * 64, 64) for h in range(2)]

    def give(dy):
        y = pos.ys(dy)
        span = pl.ds(pl.multiple_of(y * 256, 256), 256)

        @pl.loop(0, 4)
        def _(i):
            cols = pl.ds(pl.multiple_of(i * 512, 512), 512)
            part_ref[y, :, cols] = dot_nt(dqkv_ref[span], wq_ref[cols]).astype(BF)

        one.give(dy)
        two.give(dy)

    give(2)
    give(1)
    one.far()
    give(3)
    one.right()
    one.left()
    give(0)
    two.far()
    fold.finish(sumr_ref.at[1])
    send_off(1, sumr_ref.at[1])
    one.last()
    two.right()
    two.left()
    fold_q.step()
    two.last()
    rows.finish(fo_ref)
    fold_q.add()
    fold_q.second()

    def half(h):
        sc = halves[h]
        sc.arrive()

        def token(row, at):
            span = pl.ds(row, 16)
            r = tok_ref[span].astype(F32)
            dtok_ref[span] = norm_back(sc.total(at), r, dmid_ref[span]).astype(BF)

        each16(h * 64, 64, token)

    half(0)
    fold_q.finish(sumq_ref)
    for peer in tpeers:
        ship.append(net.go(sumq_ref.at[peer["y"], peer["core"]], outq_ref.at[pos.t], peer))
    keep.append(net.local(sumq_ref.at[pos.y, pos.core], outq_ref.at[pos.t]))
    half(1)
    for copy in ship + keep:
        copy.wait()
    for sc in halves:
        sc.finish()


def run_tail(*args):
    sums = fold_sums(SEG)
    return pl.pallas_call(
        tail_kernel,
        out_shape=(
            shaped(128, D),
            shaped(128, D),
            shaped(16, D, dtype=F32),
            shaped(8, 16, QKV),
            shaped(8, 3, 16, SEG),
        ),
        in_specs=[VM] * 9 + [ANY] * 9,
        out_specs=(VM, VM, VM, ANY, ANY),
        scratch_shapes=[
            pltpu.VMEM((1024, QKV), BF),
            pltpu.VMEM((8, 128, D), BF),
            pltpu.VMEM((4, 256, D), BF),
            pltpu.VMEM((4, 2, 4, 2, 2, 16, SEG), BF),
            pltpu.VMEM((4, 2, 2, 16, D), BF),
            pltpu.VMEM((4, 2, 4, 2, 2, 16, QKV), BF),
            pltpu.VMEM((4, 2, 16, QKV), BF),
            pltpu.VMEM((2, 4, 2, 16, SEG), BF),
            pltpu.VMEM((1024, 128), F32),
            pltpu.VMEM((1024, 128), F32),
            pltpu.VMEM((2, 4, 512, 64), BF),
            pltpu.VMEM((2, 4, 512, 64), BF),
            pltpu.VMEM((4, 2, 512, 64), BF),
            pltpu.VMEM((4, 2, 1, 512), F32),
            pltpu.VMEM((4, 2, 64, 512), F32),
            pltpu.VMEM((2, 512, 64), F32),
            pltpu.VMEM((2, 512, 64), F32),
            pltpu.VMEM((4, 256, 256), BF),
            pltpu.VMEM((4, 256, 256), BF),
            pltpu.VMEM((4, 256, 256), F32),
        ]
        + (fold_one(SEG) + sums + fold_two(SEG))
        + (fold_one(QKV) + fold_sums(QKV) + fold_two(QKV))
        + ([pltpu.VMEM((2, 2, 16, SEG), BF)] * 2 + fold_two(SEG))
        + out_scratch()
        + scatter_scratch(64) * 4
        + sems(4 + 2 * FOLD_ONE + 3 * FOLD_TWO + 9 + 4 * SCATTER_SEMS + 28, 22),
        compiler_params=pltpu.CompilerParams(
            collective_id=4, has_side_effects=True, vmem_limit_bytes=VLIMIT
        ),
        name="tail",
    )(*args)


def rope_tables():
    half = HEAD // 2
    freq = np.exp(np.arange(half, dtype=np.float32) * np.float32(-2.0 * math.log(rope_base) / HEAD))
    spots = np.arange(2048, dtype=np.float32).reshape(4, 2, 256).transpose(1, 0, 2).reshape(2, 1024)
    angles = (spots[:, :, None] * freq.astype(np.float32)).astype(np.float32)
    angles = np.concatenate([angles] * 4, axis=2)
    return np.cos(angles).astype(np.float32), np.sin(angles).astype(np.float32)


def adam(weight, gradient, first_moment, second, step_rate, decay_weight):
    first_new = beta_one * first_moment + (1.0 - beta_one) * gradient
    second_new = beta_two * second + (1.0 - beta_two) * gradient * gradient
    first_hat = first_new / (1.0 - beta_one**STEP)
    second_hat = second_new / (1.0 - beta_two**STEP)
    weight_new = weight - step_rate * (
        first_hat / (jnp.sqrt(second_hat) + adam_eps) + decay_weight * weight
    )
    return (first_new, second_new, weight_new)


def local(
    tokens, cotangent, w_qkv, w_out, w_gate_up, w_down_t, gains,
    first_qkv, second_qkv, first_out, second_out, first_gate_up, second_gate_up,
    first_down, second_down, first_gains, second_gains,
):
    tok, cot = tokens[0], cotangent[0]
    gain = gains.astype(BF).astype(F32)
    low_qkv = w_qkv.astype(BF).astype(F32)
    low_gu = w_gate_up.astype(BF).astype(F32)
    cos, sin = (jnp.asarray(table) for table in rope_tables())
    qkv, n_in, wq, wr_blocks, wout = run_first(tok, w_qkv, w_gate_up, w_down_t, w_out, gains)
    wq = wq.reshape(D, QKV)
    o, lse, q, kv, ra, rb, wo, cotf = run_attend(
        qkv, wout, wr_blocks, cot, cos, sin
    )
    wo = wo.reshape(256, D)
    resid, d_mid, d_attn, sumd, sga, sgb, part_b, gu = run_ffn(
        o, wo, tok, cot, ra, rb, cotf
    )
    block_out, d_tokens, grad_out, sum_q, sum_r = run_tail(
        q, kv, lse, o, wo, resid, tok, d_mid, wq,
        cos, sin, d_attn, part_b, gu, n_in, sumd, sga, sgb,
    )

    sum_q = sum_q.reshape(4, 2, 16, QKV).astype(F32)
    grad_q = sum_q[..., :256].reshape(4, 2, 16, 4, HEAD).transpose(2, 1, 3, 0, 4).reshape(16, D)
    grad_kv = jnp.sum(sum_q[..., 256:], axis=0).reshape(2, 16, 2, 2, HEAD)
    grad_kv = grad_kv.transpose(1, 3, 0, 2, 4).reshape(16, 512)
    raw_qkv = jnp.concatenate([grad_q, grad_kv], axis=1)
    sum_r = sum_r.astype(F32)
    raw_gu = sum_r[:, 0:2].transpose(2, 1, 0, 3).reshape(16, 2 * FF)
    grad_down = sum_r[:, 2].transpose(1, 0, 2).reshape(16, FF)
    grad_qkv = raw_qkv * gain[:, 0:1]
    grad_gu = raw_gu * gain[:, 1:2]
    grad_gains = jnp.stack(
        [jnp.sum(low_qkv * raw_qkv, axis=1), jnp.sum(low_gu * raw_gu, axis=1)], axis=1
    )

    first_q, second_q, weight_q = adam(w_qkv, grad_qkv, first_qkv, second_qkv, rate_matrix, decay_rate)
    first_o, second_o, weight_o = adam(w_out, grad_out, first_out, second_out, rate_matrix, decay_rate)
    first_g, second_g, weight_g = adam(
        w_gate_up, grad_gu, first_gate_up, second_gate_up, rate_matrix, decay_rate
    )
    first_d, second_d, weight_d = adam(
        w_down_t, grad_down, first_down, second_down, rate_matrix, decay_rate
    )
    first_n, second_n, weight_n = adam(gains, grad_gains, first_gains, second_gains, rate_gain, 0.0)
    return (
        block_out[None], d_tokens[None],
        first_q, second_q, weight_q, first_o, second_o, weight_o,
        first_g, second_g, weight_g, first_d, second_d, weight_d,
        first_n, second_n, weight_n,
    )


def solution(mesh):
    fine = Mesh(mesh.devices.reshape(4, 2, 4, 2, 2), ("x", "zlo", "y", "zhi", "core"))
    dp, seq = ("x", "zlo"), ("y", "zhi", "core")
    act, row = P(dp, seq, None), P(dp + seq, None)
    return jax.shard_map(
        local,
        mesh=fine,
        in_specs=(act, act) + (row,) * 15,
        out_specs=(act, act) + (row,) * 15,
        check_vma=False,
    )
```

```python
import functools
import math

import jax
import jax.numpy as jnp
import numpy as np
from jax import lax
from jax.experimental import pallas as pl
from jax.experimental.pallas import tpu as pltpu
from jax.sharding import Mesh
from jax.sharding import PartitionSpec as P

D = 2048
HEAD = 64
FF = 5632
STEP = 10
SEG = FF // 8
QKV = 512

norm_eps = 1e-05
rope_base = 10000.0
mask_fill = -1e30
beta_one = 0.9
beta_two = 0.95
adam_eps = 1e-08
decay_rate = 0.1
rate_matrix = 0.08
rate_gain = 0.8

BF = jnp.bfloat16
F32 = jnp.float32
MESH = pl.DeviceIdType.MESH
ANY = pl.BlockSpec(memory_space=pl.ANY)
VM = pl.BlockSpec(memory_space=pltpu.VMEM)
VLIMIT = 60 * 2**20


def shaped(*shape, dtype=BF):
    return jax.ShapeDtypeStruct(shape, dtype)


class Place:
    def __init__(self):
        self.x, self.zlo, self.y = (lax.axis_index(a) for a in ("x", "zlo", "y"))
        self.zhi, self.core = lax.axis_index("zhi"), lax.axis_index("core")
        self.z = self.zhi * 2 + self.zlo
        self.t = self.y * 2 + self.core
        self.sib = {"core": 1 - self.core}
        self.right = {"y": lax.rem(self.y + 1, 4)}
        self.left = {"y": lax.rem(self.y + 3, 4)}
        self.zpart = {"zhi": 1 - self.zhi}

    def xs(self, step):
        return lax.rem(self.x + step, 4)

    def ys(self, step):
        return lax.rem(self.y + step, 4)

    def zs(self, step):
        z = lax.rem(self.z + step, 4)
        return lax.div(z, 2), lax.rem(z, 2)

    def xpeers(self):
        return [{"x": self.xs(i)} for i in (1, 2, 3)]

    def zpeers(self):
        out = []
        for i in (1, 2, 3):
            zhi, zlo = self.zs(i)
            out.append({"zhi": zhi, "zlo": zlo})
        return out

    def tpeers(self):
        return [
            {"y": self.ys(dy), "core": lax.rem(self.core + dc, 2)}
            for dy in range(4)
            for dc in range(2)
            if (dy, dc) != (0, 0)
        ]


def greet(peers):
    barrier = pltpu.get_barrier_semaphore()
    for peer in peers:
        pl.semaphore_signal(barrier, inc=1, device_id=peer, device_id_type=MESH)
    pl.semaphore_wait(barrier, len(peers))


class Net:
    def __init__(self, send, recv, local):
        self.send, self.recv, self.loc = send, recv, local
        self.n = 0
        self.m = 0

    def block(self, count):
        first = self.n
        self.n += count
        return first

    def make(self, src, dst, peer, at=None):
        if at is None:
            at = self.block(1)
        return pltpu.make_async_remote_copy(
            src, dst, self.send.at[at], self.recv.at[at], device_id=peer, device_id_type=MESH
        )

    def go(self, src, dst, peer, at=None):
        copy = self.make(src, dst, peer, at)
        copy.start()
        return copy

    def local(self, src, dst):
        copy = pltpu.make_async_copy(src, dst, self.loc.at[self.m])
        self.m += 1
        copy.start()
        return copy


def sems(remote, local):
    return [
        pltpu.SemaphoreType.DMA((remote,)),
        pltpu.SemaphoreType.DMA((remote,)),
        pltpu.SemaphoreType.DMA((max(local, 1),)),
    ]


def norm_back(t, r, back):
    inv = lax.rsqrt(jnp.mean(r * r, axis=-1, keepdims=True) + norm_eps)
    normed = r * inv
    return back + inv * (t - normed * jnp.mean(t * normed, axis=-1, keepdims=True))


def each16(first, count, body):
    @pl.loop(0, count // 16)
    def _(i):
        body(pl.multiple_of(first + i * 16, 16), pl.multiple_of(i * 16, 16))


class Gather:
    def __init__(self, net, pos, src, out, base=0, rows=128):
        self.net, self.pos, self.src, self.out = net, pos, src, out
        self.all = pl.ds(base, rows)
        self.lo, self.hi = pl.ds(base, rows // 2), pl.ds(base + rows // 2, rows // 2)

    def start(self):
        net, pos, src, lo, hi = self.net, self.pos, self.src, self.lo, self.hi
        mine = self.out.at[pos.t]
        self.r = [net.go(src.at[lo], mine.at[lo], pos.right)]
        self.l = [net.go(src.at[hi], mine.at[hi], pos.left)]
        self.r.append(net.go(src.at[hi], mine.at[hi], pos.right))
        self.l.append(net.go(src.at[lo], mine.at[lo], pos.left))
        self.s = [net.go(src.at[self.all], mine.at[self.all], pos.sib)]
        self.own = net.local(src.at[self.all], mine.at[self.all])

    def step(self):
        net, pos, out, lo, hi = self.net, self.pos, self.out, self.lo, self.hi
        from_left = out.at[pos.ys(3) * 2 + pos.core]
        from_right = out.at[pos.ys(1) * 2 + pos.core]
        self.r[0].wait_recv()
        self.r2 = net.go(from_left.at[lo], from_left.at[lo], pos.right)
        self.l[0].wait_recv()
        self.l2 = net.go(from_right.at[hi], from_right.at[hi], pos.left)
        self.r[1].wait_recv()
        self.s.append(net.go(from_left.at[self.all], from_left.at[self.all], pos.sib))
        self.l[1].wait_recv()
        self.s.append(net.go(from_right.at[self.all], from_right.at[self.all], pos.sib))

    def last(self):
        net, pos, lo, hi = self.net, self.pos, self.lo, self.hi
        far = self.out.at[pos.ys(2) * 2 + pos.core]
        self.r2.wait_recv()
        self.s.append(net.go(far.at[lo], far.at[lo], pos.sib))
        self.l2.wait_recv()
        self.s.append(net.go(far.at[hi], far.at[hi], pos.sib))

    def have(self, *which):
        for i in which:
            self.s[i].wait_recv()
        if 0 in which:
            self.own.wait()

    def finish(self):
        for copy in self.r + self.l + [self.r2, self.l2] + self.s:
            copy.wait_send()


GATHER_SEMS = 11


class Scatter:
    def __init__(self, net, pos, part, scratch, base=0, rows=128):
        self.net, self.pos, self.part, self.base, self.rows = net, pos, part, base, rows
        self.lo, self.hi = pl.ds(0, rows // 2), pl.ds(rows // 2, rows // 2)
        self.sib, self.opp, self.nb, self.far_ref, self.near = scratch
        self.c = {}

    def give(self, dy):
        pos = self.pos
        rows = pl.ds(pl.multiple_of((1 - pos.core) * 128 + self.base, 16), self.rows)
        self.c[dy] = self.net.go(self.part.at[pos.ys(dy), rows], self.sib.at[dy], pos.sib)

    def _mine(self, dy, first, count):
        pos = self.pos
        rows = pl.ds(pl.multiple_of(pos.core * 128 + self.base + first, 16), count)
        return self.part[pos.ys(dy), rows].astype(F32) + self.sib[dy, pl.ds(first, count)].astype(F32)

    def far(self):
        net, pos, h = self.net, self.pos, self.rows // 2
        self.c[2].wait_recv()
        self.far_ref[self.lo] = self._mine(2, 0, h).astype(BF)
        self.f0 = net.go(self.far_ref.at[self.lo], self.opp.at[0], pos.right)
        self.far_ref[self.hi] = self._mine(2, h, h).astype(BF)
        self.f1 = net.go(self.far_ref.at[self.hi], self.opp.at[1], pos.left)

    def right(self):
        h = self.rows // 2
        self.c[1].wait_recv()
        self.near[0, self.hi] = self._mine(1, h, h).astype(BF)
        self.r1 = self.net.go(self.near.at[0, self.hi], self.nb.at[0, self.hi], self.pos.right)

    def left(self):
        h = self.rows // 2
        self.c[3].wait_recv()
        self.near[1, self.lo] = self._mine(3, 0, h).astype(BF)
        self.l0 = self.net.go(self.near.at[1, self.lo], self.nb.at[1, self.lo], self.pos.left)

    def last(self):
        net, pos, h = self.net, self.pos, self.rows // 2
        self.f0.wait_recv()
        self.near[0, self.lo] = (self._mine(1, 0, h) + self.opp[0].astype(F32)).astype(BF)
        self.r0 = net.go(self.near.at[0, self.lo], self.nb.at[0, self.lo], pos.right)
        self.f1.wait_recv()
        self.near[1, self.hi] = (self._mine(3, h, h) + self.opp[1].astype(F32)).astype(BF)
        self.l1 = net.go(self.near.at[1, self.hi], self.nb.at[1, self.hi], pos.left)

    def arrive(self):
        for copy in (self.r1, self.l0, self.r0, self.l1, self.c[0]):
            copy.wait_recv()

    def total(self, first):
        rows = pl.ds(first, 16)
        out = self._mine(0, first, 16)
        return out + self.nb[0, rows].astype(F32) + self.nb[1, rows].astype(F32)

    def finish(self):
        for copy in (self.f0, self.f1, self.r0, self.r1, self.l0, self.l1):
            copy.wait_send()
        for copy in self.c.values():
            copy.wait_send()


SCATTER_SEMS = 10


def scatter_scratch(rows=128):
    return [
        pltpu.VMEM((4, rows, D), BF),
        pltpu.VMEM((2, rows // 2, D), BF),
        pltpu.VMEM((2, rows, D), BF),
        pltpu.VMEM((rows, D), BF),
        pltpu.VMEM((2, rows, D), BF),
    ]


def reduce(halves, pos, fill):
    one, two = halves

    def give(dy):
        if fill is not None:
            fill(pos.ys(dy))
        one.give(dy)
        two.give(dy)

    give(2)
    give(1)
    one.far()
    give(3)
    one.right()
    one.left()
    give(0)
    two.far()
    one.last()
    two.right()
    two.left()
    two.last()


class Cross:
    def __init__(self, net, pos, src, own, ra, rb):
        self.net, self.pos, self.src, self.own, self.ra, self.rb = net, pos, src, own, ra, rb

    def start(self):
        net, pos = self.net, self.pos
        dst = self.own.at[:, pos.y, pos.core]
        self.one = []
        for peer in pos.tpeers():
            self.one.append(net.go(self.src.at[peer["y"] * 2 + peer["core"]], dst, peer))
        self.mine = net.local(self.src.at[pos.t], dst)

    def step(self):
        net, pos = self.net, self.pos
        self.mine.wait()
        for copy in self.one:
            copy.wait_recv()
        part_a, part_b = self.own.at[:, pl.ds(0, 2)], self.own.at[:, pl.ds(2, 2)]
        to_a, to_b = self.ra.at[:, pos.x], self.rb.at[:, pos.zlo, :, pos.zhi]
        self.two = []
        for xp, zp in zip(pos.xpeers(), pos.zpeers()):
            self.two.append(net.go(part_a, to_a, xp))
            self.two.append(net.go(part_b, to_b, zp))
        self.keep = [net.local(part_a, to_a), net.local(part_b, to_b)]

    def finish(self):
        for copy in self.one:
            copy.wait_send()
        for copy in self.two + self.keep:
            copy.wait()


class Spread:
    def __init__(self, net, pos, ra, rb, items):
        self.net, self.pos, self.ra, self.rb, self.items = net, pos, ra, rb, items
        self.up_z, self.down_z = pos.zpeers()[0], pos.zpeers()[2]
        self.up_x, self.down_x = pos.xpeers()[0], pos.xpeers()[2]

    def start(self):
        net, pos = self.net, self.pos
        low, high = pl.ds(0, 2), pl.ds(2, 2)
        self.one, self.two, self.keep = [], [], []
        for i, out in self.items:
            a = [out.at[h, pos.zlo, low, pos.zhi] for h in (low, high)]
            b = [out.at[pos.x, h, high, :] for h in (0, 1)]
            if i is not None:
                a = [(self.ra.at[i, h], dst) for h, dst in zip((low, high), a)]
                b = [(self.rb.at[i, h], dst) for h, dst in zip((0, 1), b)]
                self.keep += [net.local(*c) for c in a + b]
            else:
                a, b = [(c, c) for c in a], [(c, c) for c in b]
            up_z, down_z, up_x, down_x = self.up_z, self.down_z, self.up_x, self.down_x
            self.one.append(
                [net.go(*a[0], up_z), net.go(*a[1], down_z), net.go(*b[0], up_x), net.go(*b[1], down_x)]
                + [net.go(*a[1], up_z), net.go(*a[0], down_z), net.go(*b[1], up_x), net.go(*b[0], down_x)]
            )

    def step(self):
        net = self.net
        low, high = pl.ds(0, 2), pl.ds(2, 2)
        up_z, down_z, up_x, down_x = self.up_z, self.down_z, self.up_x, self.down_x
        for (_, out), one in zip(self.items, self.one):
            parts = (
                (out.at[low, down_z["zlo"], low, down_z["zhi"]], up_z),
                (out.at[high, up_z["zlo"], low, up_z["zhi"]], down_z),
                (out.at[down_x["x"], 0, high, :], up_x),
                (out.at[up_x["x"], 1, high, :], down_x),
            )
            for copy, (part, peer) in zip(one, parts):
                copy.wait_recv()
                self.two.append(net.go(part, part, peer))

    def arrive(self):
        for one in self.one:
            for copy in one[4:]:
                copy.wait_recv()
        for copy in self.two:
            copy.wait_recv()
        for copy in self.keep:
            copy.wait()

    def finish(self):
        for one in self.one:
            for copy in one:
                copy.wait_send()
        for copy in self.two:
            copy.wait_send()


class OutRows:
    def __init__(self, net, pos, src, out):
        self.net, self.pos, self.src, self.out = net, pos, src, out
        self.at = net.block(7)
        self.loc = net.m
        net.m += 1
        self.half = lax.div(pos.x, 2)
        self.mine = out.at[lax.rem(pos.x, 2)]
        self.pair = self.mine.at[pos.zlo, pos.zhi]

    def _sib(self):
        return self.net.make(self.src, self.pair.at[self.pos.core], self.pos.sib, self.at)

    def _own(self):
        return pltpu.make_async_copy(
            self.src, self.pair.at[self.pos.core], self.net.loc.at[self.loc]
        )

    def _z(self):
        return [
            self.net.make(self.pair, self.pair, p, self.at + 1 + i)
            for i, p in enumerate(self.pos.zpeers())
        ]

    def _x(self):
        return [
            self.net.make(self.mine, self.mine, p, self.at + 4 + i)
            for i, p in enumerate(self.pos.xpeers())
        ]

    def start(self):
        @pl.when(self.half == self.pos.core)
        def _():
            self._own().start()

        @pl.when(self.half != self.pos.core)
        def _():
            self._sib().start()

    def step(self):
        @pl.when(self.half == self.pos.core)
        def _():
            self._own().wait()
            self._sib().wait_recv()
            for copy in self._z():
                copy.start()

    def last(self):
        @pl.when(self.half == self.pos.core)
        def _():
            for copy in self._z():
                copy.wait_recv()
            for copy in self._x():
                copy.start()

    def finish(self):
        @pl.when(self.half == self.pos.core)
        def _():
            for copy in self._z() + self._x():
                copy.wait_send()

        @pl.when(self.half != self.pos.core)
        def _():
            self._sib().wait_send()

        for i, copy in enumerate(self._x()):
            back = lax.rem(self.pos.x + 3 - i, 4)

            @pl.when(lax.div(back, 2) == self.pos.core)
            def _(copy=copy):
                copy.wait_recv()


def first_kernel(
    tok_ref, wqkv_ref, wgu_ref, wdn_ref, wout_ref, gains_ref,
    qkv_ref, nf_ref, wqf_ref, wr_ref, wol_ref, wq_ref, n_ref, send, recv, local,
):
    pos, net = Place(), Net(send, recv, local)
    tpeers, xpeers, zpeers = pos.tpeers(), pos.xpeers(), pos.zpeers()
    greet(tpeers + xpeers + zpeers)
    x, y, zlo, zhi, core = pos.x, pos.y, pos.zlo, pos.zhi, pos.core

    gain = gains_ref[...].astype(BF).astype(F32)
    w = (wqkv_ref[...].astype(BF).astype(F32) * gain[:, 0:1]).astype(BF)
    for yy in range(4):
        for cc in range(2):
            heads = [(cc * 4 + d) * 4 + yy for d in range(4)]
            for c in range(2):
                heads += [32 + cc * 2 + c, 36 + cc * 2 + c]
            cut = [w[:, h * HEAD : (h + 1) * HEAD] for h in heads]
            wq_ref[yy * 2 + cc] = jnp.concatenate(cut, axis=1)

    small = []
    for peer in tpeers:
        t = peer["y"] * 2 + peer["core"]
        small.append(net.go(wq_ref.at[t], wqf_ref.at[x, zlo, y, zhi, core], peer))
    mine = net.local(wq_ref.at[pos.t], wqf_ref.at[x, zlo, y, zhi, core])

    def norm(row, at):
        rows = pl.ds(row, 16)
        r = tok_ref[rows].astype(F32)
        inv = lax.rsqrt(jnp.mean(r * r, axis=-1, keepdims=True) + norm_eps)
        n_ref[rows] = (r * inv).astype(BF)

    each16(0, 128, norm)
    gather = Gather(net, pos, n_ref, nf_ref)
    gather.start()

    mine.wait()
    for copy in small:
        copy.wait_recv()
    one = []
    for peer in xpeers:
        part = wqf_ref.at[x, zlo, pl.ds(0, 2), zhi]
        one.append(net.go(part, part, peer))
    for peer in zpeers:
        part = wqf_ref.at[x, zlo, pl.ds(2, 2), zhi]
        one.append(net.go(part, part, peer))
    for copy in one:
        copy.wait_recv()
    spread = Spread(net, pos, None, None, [(None, wqf_ref)])
    spread.start()

    wol_ref[...] = wout_ref[...].astype(BF)
    for t in range(8):
        for i, (src, first) in enumerate(((wgu_ref, 0), (wgu_ref, FF), (wdn_ref, 0))):
            part = src[:, first + t * SEG : first + (t + 1) * SEG].astype(BF)
            if i < 2:
                part = (part.astype(F32) * gain[:, 1:2]).astype(BF)
            wr_ref[t, i] = part
    gather.step()
    spread.step()
    gather.last()
    spread.arrive()
    gather.have(0, 1, 2, 3, 4)

    @pl.loop(0, 4)
    def _(i):
        w = wqf_ref[...].reshape(D, QKV)
        a = nf_ref[pl.ds(i * 2, 2)].reshape(256, D)
        qkv_ref[pl.ds(pl.multiple_of(i * 256, 256), 256)] = dot_nn(a, w).astype(BF)

    for copy in small + one:
        copy.wait_send()
    gather.finish()
    spread.finish()


def run_first(tok, wqkv, wgu, wdn, wout, gains):
    return pl.pallas_call(
        first_kernel,
        out_shape=(
            shaped(1024, QKV),
            shaped(8, 128, D),
            shaped(4, 2, 4, 2, 2, 16, QKV),
            shaped(8, 3, 16, SEG),
            shaped(16, D),
        ),
        in_specs=[VM] * 6,
        out_specs=(VM,) * 5,
        scratch_shapes=[pltpu.VMEM((8, 16, QKV), BF), pltpu.VMEM((128, D), BF)]
        + sems(7 + 6 + 8 + 4 + GATHER_SEMS, 2),
        compiler_params=pltpu.CompilerParams(
            collective_id=0, has_side_effects=True, vmem_limit_bytes=VLIMIT
        ),
        name="first",
    )(tok, wqkv, wgu, wdn, wout, gains)


def dot_nt(a, b):
    return lax.dot_general(a, b, (((1,), (1,)), ((), ())), preferred_element_type=F32)


def dot_tn(a, b):
    return lax.dot_general(a, b, (((0,), (0,)), ((), ())), preferred_element_type=F32)


def dot_nn(a, b):
    return lax.dot_general(a, b, (((1,), (0,)), ((), ())), preferred_element_type=F32)


def first_half_mask(shape):
    return (lax.broadcasted_iota(jnp.int32, shape, 1) & 63) < 32


def turn(u, cos, sin):
    rot = jnp.where(first_half_mask(u.shape), -pltpu.roll(u, 96, 1), pltpu.roll(u, 32, 1))
    return u * cos + rot * sin


def turn_back(u, cos, sin):
    v = u * sin
    rot = jnp.where(first_half_mask(u.shape), pltpu.roll(v, 96, 1), -pltpu.roll(v, 32, 1))
    return u * cos + rot


def lane_first(shape):
    return lax.broadcasted_iota(jnp.int32, shape, 1) < 64


def causal(zhi):
    key = lax.broadcasted_iota(jnp.int32, (512, 512), 0)
    query = (lax.broadcasted_iota(jnp.int32, (512, 512), 1) & 255) + zhi * 256
    return key <= query


def attend_kernel(
    qkv_ref, wout_ref, wr_ref, cot_ref, cos_in, sin_in,
    o_ref, lse_ref, q_ref, kv_ref, ra_ref, rb_ref, wo_ref, cotf_ref,
    k_ref, v_ref, own_ref, cos_ref, sin_ref, send, recv, local,
):
    pos, net = Place(), Net(send, recv, local)
    zhi = pos.zhi
    tables = [net.local(cos_in.at[zhi], cos_ref), net.local(sin_in.at[zhi], sin_ref)]
    greet(pos.tpeers() + pos.xpeers() + pos.zpeers())
    gather = Gather(net, pos, cot_ref, cotf_ref)
    cross = Cross(net, pos, wr_ref, own_ref, ra_ref, rb_ref)
    cross.start()
    rows = OutRows(net, pos, wout_ref, wo_ref)
    rows.start()

    for copy in tables:
        copy.wait()
    swap = net.block(4)
    for j in range(4):
        r = pl.ds(j * 256, 256)
        cos, sin = cos_ref[r], sin_ref[r]
        for c in range(2):
            kv = qkv_ref[r, 256 + c * 128 : 384 + c * 128].astype(F32)
            mixed = jnp.where(lane_first(kv.shape), turn(kv, cos, sin), kv)
            kv_ref[j, zhi, :, c * 128 : (c + 1) * 128] = mixed.astype(BF)
        if j == 0:
            rows.step()
        net.go(kv_ref.at[j, zhi], kv_ref.at[j, zhi], pos.zpart, swap + j)
    gather.start()
    for j in range(4):
        r = pl.ds(j * 256, 256)
        cos, sin = cos_ref[r], sin_ref[r]
        for c in range(2):
            q = turn(qkv_ref[r, c * 128 : (c + 1) * 128].astype(F32), cos, sin)
            q = q.astype(BF) * jnp.asarray(HEAD**-0.5, BF)
            q_ref[j, c, 0:256] = q[:, 0:64]
            q_ref[j, c, 256:512] = q[:, 64:128]
        if j == 1:
            rows.last()

    def update(c, key_at, query, state, mask):
        top, norm, acc = state
        s = dot_nt(k_ref[c, key_at], query)
        if mask is not None:
            s = jnp.where(mask, s, mask_fill)
        new = jnp.maximum(top, jnp.max(s, axis=0, keepdims=True))
        p = jnp.exp(s - new)
        keep = jnp.exp(top - new)
        norm = norm * keep + jnp.sum(p, axis=0, keepdims=True)
        acc = acc * keep + dot_tn(v_ref[c, key_at], p.astype(BF))
        return new, norm, acc

    def block(qb, _):
        part = kv_ref.at[qb, zhi]
        net.make(part, part, pos.zpart, swap + qb).wait_recv()
        kv = kv_ref[qb].reshape(512, 256)
        for c in range(2):
            k_ref[c, qb] = kv[:, c * 128 : c * 128 + 64]
            v_ref[c, qb] = kv[:, c * 128 + 64 : c * 128 + 128]
        mask = causal(zhi)
        state = []
        for c in range(2):
            zero = (
                jnp.full((1, 512), mask_fill, F32),
                jnp.zeros((1, 512), F32),
                jnp.zeros((64, 512), F32),
            )
            state.append(update(c, qb, q_ref[qb, c], zero, mask))

        def more(j, held):
            return tuple(update(c, j, q_ref[qb, c], held[c], None) for c in range(2))

        state = lax.fori_loop(0, qb, more, tuple(state))
        for c in range(2):
            top, norm, acc = state[c]
            lse_ref[qb, c] = top + jnp.log(norm)
            out = (acc / norm).T
            pair = jnp.concatenate([out[0:256], out[256:512]], axis=1)
            o_ref[qb, :, c * 128 : (c + 1) * 128] = pair.astype(BF)
        return 0

    cross.step()
    block(0, 0)
    block(1, 0)
    gather.step()
    block(2, 0)
    gather.last()
    block(3, 0)
    gather.have(0, 1, 2, 3, 4)
    gather.finish()
    cross.finish()
    rows.finish()
    for j in range(4):
        part = kv_ref.at[j, zhi]
        net.make(part, part, pos.zpart, swap + j).wait_send()


def run_attend(qkv, wout, wr_blocks, cot, cos, sin):
    return pl.pallas_call(
        attend_kernel,
        out_shape=(
            shaped(4, 256, 256),
            shaped(4, 2, 1, 512, dtype=F32),
            shaped(4, 2, 512, 64),
            shaped(4, 2, 256, 256),
            shaped(3, 4, 2, 2, 16, SEG),
            shaped(3, 2, 2, 2, 2, 16, SEG),
            shaped(2, 2, 2, 2, 16, D),
            shaped(8, 128, D),
        ),
        in_specs=[VM] * 4 + [ANY] * 2,
        out_specs=(VM, VM, VM, VM, ANY, ANY, ANY, ANY),
        scratch_shapes=[
            pltpu.VMEM((2, 4, 512, 64), BF),
            pltpu.VMEM((2, 4, 512, 64), BF),
            pltpu.VMEM((3, 4, 2, 16, SEG), BF),
            pltpu.VMEM((1024, 128), F32),
            pltpu.VMEM((1024, 128), F32),
        ]
        + sems(4 + 13 + 7 + GATHER_SEMS, 7),
        compiler_params=pltpu.CompilerParams(
            collective_id=1, has_side_effects=True, vmem_limit_bytes=VLIMIT
        ),
        name="attend",
    )(qkv, wout, wr_blocks, cot, cos, sin)


class Fold:
    def __init__(self, net, pos, src, scratch, sums, scratch_two):
        self.net, self.pos, self.src = net, pos, src
        self.ring = scratch
        self.sa, self.sb = sums
        if scratch_two is not None:
            self.ta, self.tb = scratch_two
        low, high = pl.ds(0, 2), pl.ds(2, 2)
        zp, xp = pos.zpeers(), pos.xpeers()
        if src is not None:
            self.axes = (
                ([src.at[:, p["zlo"], low, p["zhi"]] for p in zp], (low, high), zp),
                ([src.at[p["x"], :, high, :] for p in xp], (pl.ds(0, 1), pl.ds(1, 1)), xp),
            )

    def start(self):
        net, pos = self.net, self.pos
        self.one, self.two = [], []
        for (blocks, (lo, hi), peers), (opp, _, nb) in zip(self.axes, self.ring):
            up, far, down = blocks
            self.one.append(
                [
                    net.go(far.at[lo], opp.at[0], peers[0]),
                    net.go(far.at[hi], opp.at[1], peers[2]),
                    net.go(up.at[hi], nb.at[0, hi], peers[0]),
                    net.go(down.at[lo], nb.at[1, lo], peers[2]),
                ]
            )
        low, high = pl.ds(0, 2), pl.ds(2, 2)
        self.keep = [
            net.local(self.src.at[:, pos.zlo, low, pos.zhi], self.sa),
            net.local(self.src.at[pos.x, :, high, :], self.sb),
        ]

    def step(self):
        net = self.net
        for n, ((blocks, (lo, hi), peers), (opp, stage, nb), one) in enumerate(
            zip(self.axes, self.ring, self.one)
        ):
            up, _, down = blocks
            count = 2 - n

            for k, (block, cut, peer) in enumerate(((up, lo, peers[0]), (down, hi, peers[2]))):
                one[k].wait_recv()
                mine = block.at[cut]
                for i in range(count):
                    for j in range(2):
                        both = mine[i, j].astype(F32) + opp[k, i, j].astype(F32)
                        stage[k, i, j] = both.astype(BF)
                self.two.append(net.go(stage.at[k], nb.at[k, cut], peer))

    def add(self):
        for copy in self.keep:
            copy.wait()
        for one in self.one:
            for copy in one[2:]:
                copy.wait_recv()
        for copy in self.two:
            copy.wait_recv()
        (_, _, na), (_, _, nb) = self.ring

        @pl.loop(0, 4)
        def _(i):
            for j in range(2):
                here = self.sa[i, j].astype(F32) + na[0, i, j].astype(F32)
                self.sa[i, j] = (here + na[1, i, j].astype(F32)).astype(BF)
            lo, hi = lax.div(i, 2), lax.rem(i, 2)
            for j in range(2):
                here = self.sb[lo, j, hi].astype(F32) + nb[0, lo, j, hi].astype(F32)
                self.sb[lo, j, hi] = (here + nb[1, lo, j, hi].astype(F32)).astype(BF)

        for one in self.one:
            for copy in one:
                copy.wait_send()
        for copy in self.two:
            copy.wait_send()

    def second(self):
        net, pos = self.net, self.pos
        self.three = []
        for i, (za, xb) in enumerate(zip(pos.zpeers(), pos.xpeers())):
            self.three.append(net.go(self.sa.at[xb["x"]], self.ta.at[i], xb))
            self.three.append(net.go(self.sb.at[za["zlo"], :, za["zhi"]], self.tb.at[i], za))

    def finish(self, out, own=None):
        pos = self.pos
        if own is None:
            own = (self.sa.at[pos.x], self.sb.at[pos.zlo, :, pos.zhi])
        for copy in self.three:
            copy.wait_recv()
        for j in range(2):
            here = own[0][j].astype(F32)
            for k in range(3):
                here += self.ta[k, j].astype(F32)
            out[j] = here.astype(BF)
            here = own[1][j].astype(F32)
            for k in range(3):
                here += self.tb[k, j].astype(F32)
            out[2 + j] = here.astype(BF)
        for copy in self.three:
            copy.wait_send()


FOLD_ONE, FOLD_TWO = 12, 6


def fold_one(cols):
    return [
        pltpu.VMEM((2, 2, 2, 2, 16, cols), BF),
        pltpu.VMEM((2, 2, 2, 2, 16, cols), BF),
        pltpu.VMEM((2, 4, 2, 2, 16, cols), BF),
        pltpu.VMEM((2, 1, 2, 2, 2, 16, cols), BF),
        pltpu.VMEM((2, 1, 2, 2, 2, 16, cols), BF),
        pltpu.VMEM((2, 2, 2, 2, 2, 16, cols), BF),
    ]


def fold_sums(cols):
    return [pltpu.VMEM((4, 2, 2, 16, cols), BF), pltpu.VMEM((2, 2, 2, 2, 16, cols), BF)]


def fold_two(cols):
    return [pltpu.VMEM((3, 2, 2, 16, cols), BF), pltpu.VMEM((3, 2, 2, 16, cols), BF)]


def by_axis(refs):
    return tuple(refs[0:3]), tuple(refs[3:6])


def ffn_kernel(
    o_ref, wo_ref, tok_ref, cot_ref, ra_ref, rb_ref, cot_in,
    resid_ref, dmid_ref, full_ref, sumd_ref, sga_ref, sgb_ref, down_out, gu_out,
    wg_ref, wu_ref, wd_ref, n_ref, cotf_ref, dg_ref, du_ref, hid_ref, part_ref, blk,
    gd_ref, gg_ref, gu_ref, *rest,
):
    scr, folds, rest = (rest[:5], rest[5:10]), rest[10:26], rest[26:]
    pos, net = Place(), Net(*rest)
    bring = net.local(cot_in, cotf_ref)
    greet([pos.sib, pos.right, pos.left] + pos.xpeers() + pos.zpeers())
    sp_d, sp_g, sp_u = (
        Spread(net, pos, ra_ref, rb_ref, [item]) for item in ((2, wd_ref), (0, wg_ref), (1, wu_ref))
    )
    for sp in (sp_d, sp_g, sp_u):
        sp.start()

    def halves():
        return [Scatter(net, pos, part_ref, scr[h], h * 64, 64) for h in range(2)]

    def project(y):
        @pl.loop(0, 4)
        def _(i):
            cols = pl.ds(pl.multiple_of(i * 512, 512), 512)
            part_ref[y, :, cols] = dot_nn(o_ref[y], wo_ref[:, cols]).astype(BF)

    first = halves()
    reduce(first, pos, project)
    gather = [Gather(net, pos, blk, n_ref, h * 64, 64) for h in range(2)]
    for h, sc in enumerate(first):
        sc.arrive()

        def norm(row, at, sc=sc):
            rows = pl.ds(row, 16)
            r = sc.total(at) + tok_ref[rows].astype(F32)
            resid_ref[rows] = r
            inv = lax.rsqrt(jnp.mean(r * r, axis=-1, keepdims=True) + norm_eps)
            blk[rows] = (r * inv).astype(BF)

        each16(h * 64, 64, norm)
        gather[h].start()

    def whole(ref):
        return ref[...].reshape(D, SEG)

    def spans(y):
        return pl.ds(pl.multiple_of(y * 256, 256), 256)

    def feed(dy):
        y = pos.ys(dy)
        rows = spans(y)
        n = n_ref[pl.ds(y * 2, 2)].reshape(256, D)
        gate, up = dot_nn(n, whole(wg_ref)), dot_nn(n, whole(wu_ref))
        d_hidden = dot_nn(cotf_ref[pl.ds(y * 2, 2)].reshape(256, D), whole(wd_ref))
        sig = jax.nn.sigmoid(gate)
        silu = gate * sig
        hid_ref[rows] = (silu * up).astype(BF)
        dg_ref[rows] = (d_hidden * up * sig * (1.0 + gate * (1.0 - sig))).astype(BF)
        du_ref[rows] = (d_hidden * silu).astype(BF)

    sp_d.step()
    sp_g.step()
    sp_u.step()
    gather[0].step()
    gather[1].step()

    for sc in first:
        sc.finish()
    gather[0].last()
    gather[1].last()
    for g in gather:
        g.have(0, 1, 2, 3, 4)
        g.finish()
    bring.wait()
    for sp in (sp_d, sp_g, sp_u):
        sp.arrive()

    def regress(y):
        rows = pl.ds(pl.multiple_of(y * 256, 256), 256)

        @pl.loop(0, 4)
        def _(i):
            wrows = pl.ds(i, 1)
            w_g, w_u = (w[wrows].reshape(512, SEG) for w in (wg_ref, wu_ref))
            both = dot_nt(dg_ref[rows], w_g) + dot_nt(du_ref[rows], w_u)
            part_ref[y, :, pl.ds(pl.multiple_of(i * 512, 512), 512)] = both.astype(BF)

    def grad(left, right, out, first, last, base=0):
        @pl.loop(first, last)
        def _(i):
            cols = pl.ds(pl.multiple_of(i * 256, 256), 256)
            g = dot_tn(left[:, :, cols].reshape(1024, 256), right[...]).astype(BF)
            out[lax.div(i, 2) - base, lax.rem(i, 2)] = g.reshape(4, 2, 2, 16, SEG)

    second = halves()
    one, two = second
    fold = Fold(net, pos, gd_ref, by_axis(folds[:6]), folds[6:8], folds[8:10])
    fold_g = Fold(net, pos, gg_ref, by_axis(folds[10:]), (sga_ref, sgb_ref), None)

    def give(dy):
        feed(dy)
        regress(pos.ys(dy))
        one.give(dy)
        two.give(dy)

    give(2)
    one.far()
    two.far()
    give(1)
    one.right()
    two.right()
    give(3)
    one.left()
    two.left()
    one.last()
    give(0)
    two.last()
    grad(cotf_ref, hid_ref, gd_ref, 0, 4)
    gather = [Gather(net, pos, blk, full_ref, h * 64, 64) for h in range(2)]

    def norm_half(h):
        sc = second[h]
        sc.arrive()

        def norm(row, at):
            rows = pl.ds(row, 16)
            dmid = norm_back(sc.total(at), resid_ref[rows], cot_ref[rows].astype(F32))
            dmid_ref[rows] = dmid
            blk[rows] = dmid.astype(BF)

        each16(h * 64, 64, norm)
        gather[h].start()

    norm_half(0)
    grad(cotf_ref, hid_ref, gd_ref, 4, 8)
    fold.start()
    norm_half(1)
    grad(n_ref, dg_ref, gg_ref, 0, 4)
    gather[0].step()
    grad(n_ref, dg_ref, gg_ref, 4, 8)
    fold_g.start()
    gather[1].step()
    grad(n_ref, du_ref, gu_ref, 0, 4)
    half_u = net.local(gu_ref, gu_out.at[pl.ds(0, 2)])
    fold.step()
    gather[0].last()
    half_u.wait()
    grad(n_ref, du_ref, gu_ref, 4, 8, 2)
    keep = [net.local(gu_ref, gu_out.at[pl.ds(2, 2)])]
    gather[1].last()
    fold_g.step()
    for sc in second:
        sc.finish()

    def down(first, last):
        @pl.loop(first, last)
        def _(y):
            rows = pl.ds(pl.multiple_of(y * 256, 256), 256)

            @pl.loop(0, 4)
            def _(i):
                w = wd_ref[pl.ds(i, 1)].reshape(512, SEG)
                cols = pl.ds(pl.multiple_of(i * 512, 512), 512)
                part_ref[y, :, cols] = dot_nt(hid_ref[rows], w).astype(BF)

    down(0, 2)
    fold.add()
    fold.second()
    down(2, 4)
    keep.append(net.local(part_ref, down_out))
    fold_g.add()
    fold.finish(sumd_ref)
    for g in gather:
        g.have(0, 1, 2, 3, 4)
        g.finish()
    for sp in (sp_d, sp_g, sp_u):
        sp.finish()
    for copy in keep:
        copy.wait()


def run_ffn(o, wo, tok, cot, ra, rb, cotf):
    full = shaped(4, 2, 4, 2, 2, 16, SEG)
    whole = pltpu.VMEM((4, 2, 4, 2, 2, 16, SEG), BF)
    sums = (shaped(4, 2, 2, 16, SEG), shaped(2, 2, 2, 2, 16, SEG))
    return pl.pallas_call(
        ffn_kernel,
        out_shape=(
            shaped(128, D, dtype=F32),
            shaped(128, D, dtype=F32),
            shaped(8, 128, D),
            shaped(4, 2, 16, SEG),
            *sums,
            shaped(4, 256, D),
            full,
        ),
        in_specs=[VM] * 4 + [ANY] * 3,
        out_specs=(VM, VM, ANY, VM, VM, VM, ANY, ANY),
        scratch_shapes=[whole] * 3
        + [pltpu.VMEM((8, 128, D), BF)] * 2
        + [pltpu.VMEM((1024, SEG), BF)] * 3
        + [pltpu.VMEM((4, 256, D), BF), pltpu.VMEM((128, D), BF)]
        + [whole] * 2
        + [pltpu.VMEM((2, 2, 4, 2, 2, 16, SEG), BF)]
        + scatter_scratch(64) * 2
        + (fold_one(SEG) + fold_sums(SEG) + fold_two(SEG))
        + fold_one(SEG)
        + sems(4 * SCATTER_SEMS + 4 * GATHER_SEMS + 24 + 12 + 2 * FOLD_ONE + FOLD_TWO, 24),
        compiler_params=pltpu.CompilerParams(
            collective_id=2, has_side_effects=True, vmem_limit_bytes=VLIMIT
        ),
        name="ffn",
    )(o, wo, tok, cot, ra, rb, cotf)


class OutFold:
    def __init__(self, net, pos, src, scratch):
        self.net, self.pos, self.src = net, pos, src
        self.lx, self.sx, self.lz, self.sz, self.ls = scratch
        self.at = net.block(9)
        self.keep = net.loc.at[net.m]
        net.m += 1
        self.mine = lax.div(pos.x, 2) == pos.core

    def _x(self, xh):
        pos, net = self.pos, self.net
        src = self.src.at[pl.ds(xh * 2, 2)]
        return pltpu.make_async_remote_copy(
            src, self.lx.at[pos.x], net.send.at[self.at + xh], net.recv.at[self.at + pos.x],
            device_id={"x": pos.core * 2 + xh}, device_id_type=MESH,
        )

    def _own(self):
        xh = lax.rem(self.pos.x, 2)
        return pltpu.make_async_copy(
            self.src.at[pl.ds(xh * 2, 2)], self.lx.at[self.pos.x], self.keep
        )

    def _from_x(self, x):
        net = self.net
        return pltpu.make_async_remote_copy(
            self.src.at[pl.ds(0, 2)], self.lx.at[x], net.send.at[self.at], net.recv.at[self.at + x],
            device_id=self.pos.xpeers()[0], device_id_type=MESH,
        )

    def _z(self):
        net = self.net
        out = []
        for i, p in enumerate(self.pos.zpeers()):
            src = self.sx.at[p["zlo"], p["zhi"]]
            out.append(net.make(src, self.lz.at[i], p, self.at + 4 + i))
        return out

    def _sib(self):
        return self.net.make(self.sz.at[1 - self.pos.core], self.ls, self.pos.sib, self.at + 7)

    def start(self):
        for xh in range(2):
            here = self.pos.core * 2 + xh == self.pos.x

            @pl.when(here)
            def _():
                self._own().start()

            @pl.when(jnp.logical_not(here))
            def _(xh=xh):
                self._x(xh).start()

    def step(self):
        @pl.when(self.mine)
        def _():
            self._own().wait()
            for x in range(4):

                @pl.when(self.pos.x != x)
                def _(x=x):
                    self._from_x(x).wait_recv()

            for i in range(2):
                for j in range(2):
                    for k in range(2):
                        here = self.lx[0, i, j, k].astype(F32)
                        for x in range(1, 4):
                            here += self.lx[x, i, j, k].astype(F32)
                        self.sx[i, j, k] = here.astype(BF)
            for copy in self._z():
                copy.start()

    def last(self):
        @pl.when(self.mine)
        def _():
            pos = self.pos
            for copy in self._z():
                copy.wait_recv()
            for k in range(2):
                here = self.sx[pos.zlo, pos.zhi, k].astype(F32)
                for i in range(3):
                    here += self.lz[i, k].astype(F32)
                self.sz[k] = here.astype(BF)
            self._sib().start()

    def finish(self, out):
        for xh in range(2):
            here = self.pos.core * 2 + xh == self.pos.x

            @pl.when(jnp.logical_not(here))
            def _(xh=xh):
                self._x(xh).wait_send()

        @pl.when(self.mine)
        def _():
            for copy in self._z():
                copy.wait_send()
            self._sib().wait_send()
            out[...] = self.sz[self.pos.core].astype(F32)

        @pl.when(jnp.logical_not(self.mine))
        def _():
            self._sib().wait_recv()
            out[...] = self.ls[...].astype(F32)


def out_scratch():
    return [
        pltpu.VMEM((4, 2, 2, 2, 16, D), BF),
        pltpu.VMEM((2, 2, 2, 16, D), BF),
        pltpu.VMEM((3, 2, 16, D), BF),
        pltpu.VMEM((2, 16, D), BF),
        pltpu.VMEM((16, D), BF),
    ]


def tail_kernel(
    q_ref, kv_ref, lse_ref, o_ref, wo_ref, resid_ref, tok_ref, dmid_ref, wq_ref,
    cos_in, sin_in, dat_in, part_in, gu_in, n_in, sumd_in, sga_in, sgb_in,
    block_ref, dtok_ref, fo_ref, outq_ref, outr_ref,
    dqkv_ref, dat_ref, part_ref, gu_ref, go_ref, gq_ref, sumq_ref, sumr_ref, cos_ref, sin_ref,
    k_ref, v_ref, do2_ref, delta_ref, dq_ref, dk_ref, dv_ref, send_ref, got_ref, mine_ref,
    *rest,
):
    pos = Place()
    rest = list(rest)

    def take(count):
        out = rest[:count]
        del rest[:count]
        return out

    one_u, sums_u, two_u = take(6), take(2), take(2)
    one_q, sums_q, two_q = take(6), take(2), take(2)
    own_g, two_g = take(2), take(2)
    land, scr_a, scr_b = take(5), [take(5), take(5)], [take(5), take(5)]
    net = Net(*rest)
    zhi = pos.zhi
    bring = [net.local(dat_in.at[pl.ds(j * 2, 2)], dat_ref.at[pl.ds(j * 2, 2)]) for j in range(4)]
    bring_part, bring_gu = net.local(part_in, part_ref), net.local(gu_in, gu_ref)
    get = [net.local(cos_in.at[zhi], cos_ref), net.local(sin_in.at[zhi], sin_ref)]
    get.append(net.local(sga_in.at[pos.x], own_g[0]))
    get.append(net.local(sgb_in.at[pos.zlo, :, pos.zhi], own_g[1]))
    tpeers = pos.tpeers()
    greet(tpeers + pos.xpeers() + pos.zpeers())
    one, two = halves = [Scatter(net, pos, part_ref, scr_a[h], h * 64, 64) for h in range(2)]
    fold = Fold(net, pos, gu_ref, by_axis(one_u), sums_u, two_u)
    fold_q = Fold(net, pos, gq_ref, by_axis(one_q), sums_q, two_q)
    fold_g = Fold(net, pos, None, None, (sga_in, sgb_in), two_g)
    rows = OutFold(net, pos, go_ref, land)
    fold_g.second()
    ship, keep = [], []

    def send_off(i, src):
        for peer in tpeers:
            ship.append(net.go(src.at[peer["y"], peer["core"]], outr_ref.at[pos.t, i], peer))
        keep.append(net.local(src.at[pos.y, pos.core], outr_ref.at[pos.t, i]))

    send_off(2, sumd_in)

    for j in range(4):
        kv = kv_ref[j].reshape(512, 256)
        bring[j].wait()
        d_o = dot_nt(dat_ref[pl.ds(j * 2, 2)].reshape(256, D), wo_ref[...]).astype(BF)
        for c in range(2):
            k_ref[c, j] = kv[:, c * 128 : c * 128 + 64]
            v_ref[c, j] = kv[:, c * 128 + 64 : c * 128 + 128]
            cols = slice(c * 128, (c + 1) * 128)
            do = d_o[:, cols]
            do2_ref[j, c, 0:256] = do[:, 0:64]
            do2_ref[j, c, 256:512] = do[:, 64:128]
            both = (do.astype(F32) * o_ref[j, :, cols].astype(F32)).T
            delta_ref[j, c] = jnp.concatenate(
                [
                    jnp.sum(both[0:64], axis=0, keepdims=True),
                    jnp.sum(both[64:128], axis=0, keepdims=True),
                ],
                axis=1,
            )
    bring_gu.wait()
    fold.start()
    bring_part.wait()
    for dy in (2, 1, 3, 0):
        one.give(dy)
        two.give(dy)

    @pl.loop(0, 4)
    def _(i):
        cols = pl.ds(pl.multiple_of(i * 512, 512), 512)
        left = o_ref[...].reshape(1024, 256)
        g = dot_tn(left, dat_ref[:, :, cols].reshape(1024, 512)).astype(BF)
        go_ref[:, :, :, :, cols] = g.reshape(4, 2, 2, 16, 512)

    bring_n = net.local(n_in, dat_ref)
    rows.start()
    one.far()
    one.right()
    one.left()
    two.far()
    dq_ref[...] = jnp.zeros_like(dq_ref)

    swap = net.block(4)

    def pair(c, j, qb, mask):
        k, v, q, do = k_ref[c, j], v_ref[c, j], q_ref[qb, c], do2_ref[qb, c]
        p = jnp.exp(dot_nt(k, q) - lse_ref[qb, c])
        if mask is not None:
            p = jnp.where(mask, p, 0.0)
        ds = (p * (dot_nt(v, do) - delta_ref[qb, c])).astype(BF)
        dv = dot_nn(p.astype(BF), do)
        dk = dot_nn(ds, q)
        dq_ref[qb, c] += dot_tn(k, ds)
        return dk, dv

    def column(j):
        mask = causal(zhi)
        for c in range(2):
            dk, dv = pair(c, j, j, mask)
            dk_ref[c] = dk
            dv_ref[c] = dv

        def more(qb, _):
            for c in range(2):
                dk, dv = pair(c, j, qb, None)
                dk_ref[c] += dk
                dv_ref[c] += dv
            return 0

        lax.fori_loop(j + 1, 4, more, 0)
        both = jnp.concatenate([dk_ref[0], dv_ref[0], dk_ref[1], dv_ref[1]], axis=1)
        both = both.reshape(2, 256, 256)

        @pl.when(zhi == 0)
        def _():
            mine_ref[j] = both[0]
            send_ref[j] = both[1].astype(BF)

        @pl.when(zhi == 1)
        def _():
            mine_ref[j] = both[1]
            send_ref[j] = both[0].astype(BF)

        net.go(send_ref.at[j], got_ref.at[j], pos.zpart, swap + j)

    def queries(j):
        r = pl.ds(j * 256, 256)
        cos, sin = cos_ref[r], sin_ref[r]
        for c in range(2):
            dq = dq_ref[j, c].T * HEAD**-0.5
            dq = jnp.concatenate([dq[0:256], dq[256:512]], axis=1)
            dqkv_ref[r, c * 128 : (c + 1) * 128] = turn_back(dq, cos, sin).astype(BF)

    def keys(j):
        r = pl.ds(j * 256, 256)
        cos, sin = cos_ref[r], sin_ref[r]
        net.make(send_ref.at[j], got_ref.at[j], pos.zpart, swap + j).wait()
        for c in range(2):
            cols = slice(c * 128, (c + 1) * 128)
            dkv = mine_ref[j, :, cols] + got_ref[j, :, cols].astype(F32)
            dkv = jnp.where(lane_first(dkv.shape), turn_back(dkv, cos, sin), dkv)
            dqkv_ref[r, 256 + c * 128 : 384 + c * 128] = dkv.astype(BF)

    column(0)
    one.last()
    two.right()
    two.left()
    for copy in get:
        copy.wait()
    queries(0)
    column(1)
    two.last()
    rows.step()
    queries(1)
    keys(0)
    fold.step()
    column(2)
    rows.last()
    queries(2)
    keys(1)
    fold_g.finish(sumr_ref.at[0], own_g)
    send_off(0, sumr_ref.at[0])
    column(3)
    queries(3)
    fold.add()
    fold.second()
    for h, sc in enumerate(halves):
        sc.arrive()

        def block(row, at, sc=sc):
            r = pl.ds(row, 16)
            block_ref[r] = (sc.total(at) + resid_ref[r]).astype(BF)

        each16(h * 64, 64, block)

    for sc in halves:
        sc.finish()
    bring_n.wait()

    def grad(at, count):
        @pl.loop(0, 8)
        def _(i):
            cols = pl.ds(pl.multiple_of(i * 256, 256), 256)
            left = dat_ref[:, :, cols].reshape(1024, 256)
            g = dot_tn(left, dqkv_ref[:, at : at + count]).astype(BF)
            out = gq_ref.at[lax.div(i, 2), lax.rem(i, 2)]
            out[:, :, :, :, at : at + count] = g.reshape(4, 2, 2, 16, count)

    keys(2)
    grad(0, 256)
    keys(3)
    one, two = halves = [Scatter(net, pos, part_ref, scr_b[h], h * 64, 64) for h in range(2)]

    def give(dy):
        y = pos.ys(dy)
        span = pl.ds(pl.multiple_of(y * 256, 256), 256)

        @pl.loop(0, 4)
        def _(i):
            cols = pl.ds(pl.multiple_of(i * 512, 512), 512)
            part_ref[y, :, cols] = dot_nt(dqkv_ref[span], wq_ref[cols]).astype(BF)

        one.give(dy)
        two.give(dy)

    give(2)
    give(1)
    one.far()
    grad(256, 256)
    fold_q.start()
    give(3)
    one.right()
    one.left()
    give(0)
    two.far()
    fold.finish(sumr_ref.at[1])
    send_off(1, sumr_ref.at[1])
    one.last()
    two.right()
    two.left()
    fold_q.step()
    two.last()
    rows.finish(fo_ref)
    fold_q.add()
    fold_q.second()

    def half(h):
        sc = halves[h]
        sc.arrive()

        def token(row, at):
            span = pl.ds(row, 16)
            r = tok_ref[span].astype(F32)
            dtok_ref[span] = norm_back(sc.total(at), r, dmid_ref[span]).astype(BF)

        each16(h * 64, 64, token)

    half(0)
    fold_q.finish(sumq_ref)
    for peer in tpeers:
        ship.append(net.go(sumq_ref.at[peer["y"], peer["core"]], outq_ref.at[pos.t], peer))
    keep.append(net.local(sumq_ref.at[pos.y, pos.core], outq_ref.at[pos.t]))
    half(1)
    for copy in ship + keep:
        copy.wait()
    for sc in halves:
        sc.finish()


def run_tail(*args):
    sums = fold_sums(SEG)
    return pl.pallas_call(
        tail_kernel,
        out_shape=(
            shaped(128, D),
            shaped(128, D),
            shaped(16, D, dtype=F32),
            shaped(8, 16, QKV),
            shaped(8, 3, 16, SEG),
        ),
        in_specs=[VM] * 9 + [ANY] * 9,
        out_specs=(VM, VM, VM, ANY, ANY),
        scratch_shapes=[
            pltpu.VMEM((1024, QKV), BF),
            pltpu.VMEM((8, 128, D), BF),
            pltpu.VMEM((4, 256, D), BF),
            pltpu.VMEM((4, 2, 4, 2, 2, 16, SEG), BF),
            pltpu.VMEM((4, 2, 2, 16, D), BF),
            pltpu.VMEM((4, 2, 4, 2, 2, 16, QKV), BF),
            pltpu.VMEM((4, 2, 16, QKV), BF),
            pltpu.VMEM((2, 4, 2, 16, SEG), BF),
            pltpu.VMEM((1024, 128), F32),
            pltpu.VMEM((1024, 128), F32),
            pltpu.VMEM((2, 4, 512, 64), BF),
            pltpu.VMEM((2, 4, 512, 64), BF),
            pltpu.VMEM((4, 2, 512, 64), BF),
            pltpu.VMEM((4, 2, 1, 512), F32),
            pltpu.VMEM((4, 2, 64, 512), F32),
            pltpu.VMEM((2, 512, 64), F32),
            pltpu.VMEM((2, 512, 64), F32),
            pltpu.VMEM((4, 256, 256), BF),
            pltpu.VMEM((4, 256, 256), BF),
            pltpu.VMEM((4, 256, 256), F32),
        ]
        + (fold_one(SEG) + sums + fold_two(SEG))
        + (fold_one(QKV) + fold_sums(QKV) + fold_two(QKV))
        + ([pltpu.VMEM((2, 2, 16, SEG), BF)] * 2 + fold_two(SEG))
        + out_scratch()
        + scatter_scratch(64) * 4
        + sems(4 + 2 * FOLD_ONE + 3 * FOLD_TWO + 9 + 4 * SCATTER_SEMS + 28, 22),
        compiler_params=pltpu.CompilerParams(
            collective_id=4, has_side_effects=True, vmem_limit_bytes=VLIMIT
        ),
        name="tail",
    )(*args)


def rope_tables():
    half = HEAD // 2
    freq = np.exp(np.arange(half, dtype=np.float32) * np.float32(-2.0 * math.log(rope_base) / HEAD))
    spots = np.arange(2048, dtype=np.float32).reshape(4, 2, 256).transpose(1, 0, 2).reshape(2, 1024)
    angles = (spots[:, :, None] * freq.astype(np.float32)).astype(np.float32)
    angles = np.concatenate([angles] * 4, axis=2)
    return np.cos(angles).astype(np.float32), np.sin(angles).astype(np.float32)


def adam(weight, gradient, first_moment, second, step_rate, decay_weight):
    first_new = beta_one * first_moment + (1.0 - beta_one) * gradient
    second_new = beta_two * second + (1.0 - beta_two) * gradient * gradient
    first_hat = first_new / (1.0 - beta_one**STEP)
    second_hat = second_new / (1.0 - beta_two**STEP)
    weight_new = weight - step_rate * (
        first_hat / (jnp.sqrt(second_hat) + adam_eps) + decay_weight * weight
    )
    return (first_new, second_new, weight_new)


def local(
    tokens, cotangent, w_qkv, w_out, w_gate_up, w_down_t, gains,
    first_qkv, second_qkv, first_out, second_out, first_gate_up, second_gate_up,
    first_down, second_down, first_gains, second_gains,
):
    tok, cot = tokens[0], cotangent[0]
    gain = gains.astype(BF).astype(F32)
    low_qkv = w_qkv.astype(BF).astype(F32)
    low_gu = w_gate_up.astype(BF).astype(F32)
    cos, sin = (jnp.asarray(table) for table in rope_tables())
    qkv, n_in, wq, wr_blocks, wout = run_first(tok, w_qkv, w_gate_up, w_down_t, w_out, gains)
    wq = wq.reshape(D, QKV)
    o, lse, q, kv, ra, rb, wo, cotf = run_attend(
        qkv, wout, wr_blocks, cot, cos, sin
    )
    wo = wo.reshape(256, D)
    resid, d_mid, d_attn, sumd, sga, sgb, part_b, gu = run_ffn(
        o, wo, tok, cot, ra, rb, cotf
    )
    block_out, d_tokens, grad_out, sum_q, sum_r = run_tail(
        q, kv, lse, o, wo, resid, tok, d_mid, wq,
        cos, sin, d_attn, part_b, gu, n_in, sumd, sga, sgb,
    )

    sum_q = sum_q.reshape(4, 2, 16, QKV).astype(F32)
    grad_q = sum_q[..., :256].reshape(4, 2, 16, 4, HEAD).transpose(2, 1, 3, 0, 4).reshape(16, D)
    grad_kv = jnp.sum(sum_q[..., 256:], axis=0).reshape(2, 16, 2, 2, HEAD)
    grad_kv = grad_kv.transpose(1, 3, 0, 2, 4).reshape(16, 512)
    raw_qkv = jnp.concatenate([grad_q, grad_kv], axis=1)
    sum_r = sum_r.astype(F32)
    raw_gu = sum_r[:, 0:2].transpose(2, 1, 0, 3).reshape(16, 2 * FF)
    grad_down = sum_r[:, 2].transpose(1, 0, 2).reshape(16, FF)
    grad_qkv = raw_qkv * gain[:, 0:1]
    grad_gu = raw_gu * gain[:, 1:2]
    grad_gains = jnp.stack(
        [jnp.sum(low_qkv * raw_qkv, axis=1), jnp.sum(low_gu * raw_gu, axis=1)], axis=1
    )

    first_q, second_q, weight_q = adam(w_qkv, grad_qkv, first_qkv, second_qkv, rate_matrix, decay_rate)
    first_o, second_o, weight_o = adam(w_out, grad_out, first_out, second_out, rate_matrix, decay_rate)
    first_g, second_g, weight_g = adam(
        w_gate_up, grad_gu, first_gate_up, second_gate_up, rate_matrix, decay_rate
    )
    first_d, second_d, weight_d = adam(
        w_down_t, grad_down, first_down, second_down, rate_matrix, decay_rate
    )
    first_n, second_n, weight_n = adam(gains, grad_gains, first_gains, second_gains, rate_gain, 0.0)
    return (
        block_out[None], d_tokens[None],
        first_q, second_q, weight_q, first_o, second_o, weight_o,
        first_g, second_g, weight_g, first_d, second_d, weight_d,
        first_n, second_n, weight_n,
    )


def solution(mesh):
    fine = Mesh(mesh.devices.reshape(4, 2, 4, 2, 2), ("x", "zlo", "y", "zhi", "core"))
    dp, seq = ("x", "zlo"), ("y", "zhi", "core")
    act, row = P(dp, seq, None), P(dp + seq, None)
    return jax.shard_map(
        local,
        mesh=fine,
        in_specs=(act, act) + (row,) * 15,
        out_specs=(act, act) + (row,) * 15,
        check_vma=False,
    )
```

```python
import functools
import math

import jax
import jax.numpy as jnp
import numpy as np
from jax import lax
from jax.experimental import pallas as pl
from jax.experimental.pallas import tpu as pltpu
from jax.sharding import Mesh
from jax.sharding import PartitionSpec as P

D = 2048
HEAD = 64
FF = 5632
STEP = 10
SEG = FF // 8
QKV = 512

norm_eps = 1e-05
rope_base = 10000.0
mask_fill = -1e30
beta_one = 0.9
beta_two = 0.95
adam_eps = 1e-08
decay_rate = 0.1
rate_matrix = 0.08
rate_gain = 0.8

BF = jnp.bfloat16
F32 = jnp.float32
MESH = pl.DeviceIdType.MESH
ANY = pl.BlockSpec(memory_space=pl.ANY)
VM = pl.BlockSpec(memory_space=pltpu.VMEM)
VLIMIT = 60 * 2**20


def shaped(*shape, dtype=BF):
    return jax.ShapeDtypeStruct(shape, dtype)


class Place:
    def __init__(self):
        self.x, self.zlo, self.y = (lax.axis_index(a) for a in ("x", "zlo", "y"))
        self.zhi, self.core = lax.axis_index("zhi"), lax.axis_index("core")
        self.z = self.zhi * 2 + self.zlo
        self.t = self.y * 2 + self.core
        self.sib = {"core": 1 - self.core}
        self.right = {"y": lax.rem(self.y + 1, 4)}
        self.left = {"y": lax.rem(self.y + 3, 4)}
        self.zpart = {"zhi": 1 - self.zhi}

    def xs(self, step):
        return lax.rem(self.x + step, 4)

    def ys(self, step):
        return lax.rem(self.y + step, 4)

    def zs(self, step):
        z = lax.rem(self.z + step, 4)
        return lax.div(z, 2), lax.rem(z, 2)

    def xpeers(self):
        return [{"x": self.xs(i)} for i in (1, 2, 3)]

    def zpeers(self):
        out = []
        for i in (1, 2, 3):
            zhi, zlo = self.zs(i)
            out.append({"zhi": zhi, "zlo": zlo})
        return out

    def tpeers(self):
        return [
            {"y": self.ys(dy), "core": lax.rem(self.core + dc, 2)}
            for dy in range(4)
            for dc in range(2)
            if (dy, dc) != (0, 0)
        ]


def greet(peers):
    barrier = pltpu.get_barrier_semaphore()
    for peer in peers:
        pl.semaphore_signal(barrier, inc=1, device_id=peer, device_id_type=MESH)
    pl.semaphore_wait(barrier, len(peers))


class Net:
    def __init__(self, send, recv, local):
        self.send, self.recv, self.loc = send, recv, local
        self.n = 0
        self.m = 0

    def block(self, count):
        first = self.n
        self.n += count
        return first

    def make(self, src, dst, peer, at=None):
        if at is None:
            at = self.block(1)
        return pltpu.make_async_remote_copy(
            src, dst, self.send.at[at], self.recv.at[at], device_id=peer, device_id_type=MESH
        )

    def go(self, src, dst, peer, at=None):
        copy = self.make(src, dst, peer, at)
        copy.start()
        return copy

    def local(self, src, dst):
        copy = pltpu.make_async_copy(src, dst, self.loc.at[self.m])
        self.m += 1
        copy.start()
        return copy


def sems(remote, local):
    return [
        pltpu.SemaphoreType.DMA((remote,)),
        pltpu.SemaphoreType.DMA((remote,)),
        pltpu.SemaphoreType.DMA((max(local, 1),)),
    ]


def norm_back(t, r, back):
    inv = lax.rsqrt(jnp.mean(r * r, axis=-1, keepdims=True) + norm_eps)
    normed = r * inv
    return back + inv * (t - normed * jnp.mean(t * normed, axis=-1, keepdims=True))


def each16(first, count, body):
    @pl.loop(0, count // 16)
    def _(i):
        body(pl.multiple_of(first + i * 16, 16), pl.multiple_of(i * 16, 16))


class Gather:
    def __init__(self, net, pos, src, out, base=0, rows=128):
        self.net, self.pos, self.src, self.out = net, pos, src, out
        self.all = pl.ds(base, rows)
        self.lo, self.hi = pl.ds(base, rows // 2), pl.ds(base + rows // 2, rows // 2)

    def start(self):
        net, pos, src, lo, hi = self.net, self.pos, self.src, self.lo, self.hi
        mine = self.out.at[pos.t]
        self.r = [net.go(src.at[lo], mine.at[lo], pos.right)]
        self.l = [net.go(src.at[hi], mine.at[hi], pos.left)]
        self.r.append(net.go(src.at[hi], mine.at[hi], pos.right))
        self.l.append(net.go(src.at[lo], mine.at[lo], pos.left))
        self.s = [net.go(src.at[self.all], mine.at[self.all], pos.sib)]
        self.own = net.local(src.at[self.all], mine.at[self.all])

    def step(self):
        net, pos, out, lo, hi = self.net, self.pos, self.out, self.lo, self.hi
        from_left = out.at[pos.ys(3) * 2 + pos.core]
        from_right = out.at[pos.ys(1) * 2 + pos.core]
        self.r[0].wait_recv()
        self.r2 = net.go(from_left.at[lo], from_left.at[lo], pos.right)
        self.l[0].wait_recv()
        self.l2 = net.go(from_right.at[hi], from_right.at[hi], pos.left)
        self.r[1].wait_recv()
        self.s.append(net.go(from_left.at[self.all], from_left.at[self.all], pos.sib))
        self.l[1].wait_recv()
        self.s.append(net.go(from_right.at[self.all], from_right.at[self.all], pos.sib))

    def last(self):
        net, pos, lo, hi = self.net, self.pos, self.lo, self.hi
        far = self.out.at[pos.ys(2) * 2 + pos.core]
        self.r2.wait_recv()
        self.s.append(net.go(far.at[lo], far.at[lo], pos.sib))
        self.l2.wait_recv()
        self.s.append(net.go(far.at[hi], far.at[hi], pos.sib))

    def have(self, *which):
        for i in which:
            self.s[i].wait_recv()
        if 0 in which:
            self.own.wait()

    def finish(self):
        for copy in self.r + self.l + [self.r2, self.l2] + self.s:
            copy.wait_send()


GATHER_SEMS = 11


class Scatter:
    def __init__(self, net, pos, part, scratch, base=0, rows=128):
        self.net, self.pos, self.part, self.base, self.rows = net, pos, part, base, rows
        self.lo, self.hi = pl.ds(0, rows // 2), pl.ds(rows // 2, rows // 2)
        self.sib, self.opp, self.nb, self.far_ref, self.near = scratch
        self.c = {}

    def give(self, dy):
        pos = self.pos
        rows = pl.ds(pl.multiple_of((1 - pos.core) * 128 + self.base, 16), self.rows)
        self.c[dy] = self.net.go(self.part.at[pos.ys(dy), rows], self.sib.at[dy], pos.sib)

    def _mine(self, dy, first, count):
        pos = self.pos
        rows = pl.ds(pl.multiple_of(pos.core * 128 + self.base + first, 16), count)
        return self.part[pos.ys(dy), rows].astype(F32) + self.sib[dy, pl.ds(first, count)].astype(F32)

    def far(self):
        net, pos, h = self.net, self.pos, self.rows // 2
        self.c[2].wait_recv()
        self.far_ref[self.lo] = self._mine(2, 0, h).astype(BF)
        self.f0 = net.go(self.far_ref.at[self.lo], self.opp.at[0], pos.right)
        self.far_ref[self.hi] = self._mine(2, h, h).astype(BF)
        self.f1 = net.go(self.far_ref.at[self.hi], self.opp.at[1], pos.left)

    def right(self):
        h = self.rows // 2
        self.c[1].wait_recv()
        self.near[0, self.hi] = self._mine(1, h, h).astype(BF)
        self.r1 = self.net.go(self.near.at[0, self.hi], self.nb.at[0, self.hi], self.pos.right)

    def left(self):
        h = self.rows // 2
        self.c[3].wait_recv()
        self.near[1, self.lo] = self._mine(3, 0, h).astype(BF)
        self.l0 = self.net.go(self.near.at[1, self.lo], self.nb.at[1, self.lo], self.pos.left)

    def last(self):
        net, pos, h = self.net, self.pos, self.rows // 2
        self.f0.wait_recv()
        self.near[0, self.lo] = (self._mine(1, 0, h) + self.opp[0].astype(F32)).astype(BF)
        self.r0 = net.go(self.near.at[0, self.lo], self.nb.at[0, self.lo], pos.right)
        self.f1.wait_recv()
        self.near[1, self.hi] = (self._mine(3, h, h) + self.opp[1].astype(F32)).astype(BF)
        self.l1 = net.go(self.near.at[1, self.hi], self.nb.at[1, self.hi], pos.left)

    def arrive(self):
        for copy in (self.r1, self.l0, self.r0, self.l1, self.c[0]):
            copy.wait_recv()

    def total(self, first):
        rows = pl.ds(first, 16)
        out = self._mine(0, first, 16)
        return out + self.nb[0, rows].astype(F32) + self.nb[1, rows].astype(F32)

    def finish(self):
        for copy in (self.f0, self.f1, self.r0, self.r1, self.l0, self.l1):
            copy.wait_send()
        for copy in self.c.values():
            copy.wait_send()


SCATTER_SEMS = 10


def scatter_scratch(rows=128):
    return [
        pltpu.VMEM((4, rows, D), BF),
        pltpu.VMEM((2, rows // 2, D), BF),
        pltpu.VMEM((2, rows, D), BF),
        pltpu.VMEM((rows, D), BF),
        pltpu.VMEM((2, rows, D), BF),
    ]


def reduce(halves, pos, fill):
    one, two = halves

    def give(dy):
        if fill is not None:
            fill(pos.ys(dy))
        one.give(dy)
        two.give(dy)

    give(2)
    give(1)
    one.far()
    give(3)
    one.right()
    one.left()
    give(0)
    two.far()
    one.last()
    two.right()
    two.left()
    two.last()


class Cross:
    def __init__(self, net, pos, src, own, ra, rb):
        self.net, self.pos, self.src, self.own, self.ra, self.rb = net, pos, src, own, ra, rb

    def start(self):
        net, pos = self.net, self.pos
        dst = self.own.at[:, pos.y, pos.core]
        self.one = []
        for peer in pos.tpeers():
            self.one.append(net.go(self.src.at[peer["y"] * 2 + peer["core"]], dst, peer))
        self.mine = net.local(self.src.at[pos.t], dst)

    def step(self):
        net, pos = self.net, self.pos
        self.mine.wait()
        for copy in self.one:
            copy.wait_recv()
        part_a, part_b = self.own.at[:, pl.ds(0, 2)], self.own.at[:, pl.ds(2, 2)]
        to_a, to_b = self.ra.at[:, pos.x], self.rb.at[:, pos.zlo, :, pos.zhi]
        self.two = []
        for xp, zp in zip(pos.xpeers(), pos.zpeers()):
            self.two.append(net.go(part_a, to_a, xp))
            self.two.append(net.go(part_b, to_b, zp))
        self.keep = [net.local(part_a, to_a), net.local(part_b, to_b)]

    def finish(self):
        for copy in self.one:
            copy.wait_send()
        for copy in self.two + self.keep:
            copy.wait()


class Spread:
    def __init__(self, net, pos, ra, rb, items):
        self.net, self.pos, self.ra, self.rb, self.items = net, pos, ra, rb, items
        self.up_z, self.down_z = pos.zpeers()[0], pos.zpeers()[2]
        self.up_x, self.down_x = pos.xpeers()[0], pos.xpeers()[2]

    def start(self):
        net, pos = self.net, self.pos
        low, high = pl.ds(0, 2), pl.ds(2, 2)
        self.one, self.two, self.keep = [], [], []
        for i, out in self.items:
            a = [out.at[h, pos.zlo, low, pos.zhi] for h in (low, high)]
            b = [out.at[pos.x, h, high, :] for h in (0, 1)]
            if i is not None:
                a = [(self.ra.at[i, h], dst) for h, dst in zip((low, high), a)]
                b = [(self.rb.at[i, h], dst) for h, dst in zip((0, 1), b)]
                self.keep += [net.local(*c) for c in a + b]
            else:
                a, b = [(c, c) for c in a], [(c, c) for c in b]
            up_z, down_z, up_x, down_x = self.up_z, self.down_z, self.up_x, self.down_x
            self.one.append(
                [net.go(*a[0], up_z), net.go(*a[1], down_z), net.go(*b[0], up_x), net.go(*b[1], down_x)]
                + [net.go(*a[1], up_z), net.go(*a[0], down_z), net.go(*b[1], up_x), net.go(*b[0], down_x)]
            )

    def step(self):
        net = self.net
        low, high = pl.ds(0, 2), pl.ds(2, 2)
        up_z, down_z, up_x, down_x = self.up_z, self.down_z, self.up_x, self.down_x
        for (_, out), one in zip(self.items, self.one):
            parts = (
                (out.at[low, down_z["zlo"], low, down_z["zhi"]], up_z),
                (out.at[high, up_z["zlo"], low, up_z["zhi"]], down_z),
                (out.at[down_x["x"], 0, high, :], up_x),
                (out.at[up_x["x"], 1, high, :], down_x),
            )
            for copy, (part, peer) in zip(one, parts):
                copy.wait_recv()
                self.two.append(net.go(part, part, peer))

    def arrive(self):
        for one in self.one:
            for copy in one[4:]:
                copy.wait_recv()
        for copy in self.two:
            copy.wait_recv()
        for copy in self.keep:
            copy.wait()

    def finish(self):
        for one in self.one:
            for copy in one:
                copy.wait_send()
        for copy in self.two:
            copy.wait_send()


class OutRows:
    def __init__(self, net, pos, src, out):
        self.net, self.pos, self.src, self.out = net, pos, src, out
        self.at = net.block(7)
        self.loc = net.m
        net.m += 1
        self.half = lax.div(pos.x, 2)
        self.mine = out.at[lax.rem(pos.x, 2)]
        self.pair = self.mine.at[pos.zlo, pos.zhi]

    def _sib(self):
        return self.net.make(self.src, self.pair.at[self.pos.core], self.pos.sib, self.at)

    def _own(self):
        return pltpu.make_async_copy(
            self.src, self.pair.at[self.pos.core], self.net.loc.at[self.loc]
        )

    def _z(self):
        return [
            self.net.make(self.pair, self.pair, p, self.at + 1 + i)
            for i, p in enumerate(self.pos.zpeers())
        ]

    def _x(self):
        return [
            self.net.make(self.mine, self.mine, p, self.at + 4 + i)
            for i, p in enumerate(self.pos.xpeers())
        ]

    def start(self):
        @pl.when(self.half == self.pos.core)
        def _():
            self._own().start()

        @pl.when(self.half != self.pos.core)
        def _():
            self._sib().start()

    def step(self):
        @pl.when(self.half == self.pos.core)
        def _():
            self._own().wait()
            self._sib().wait_recv()
            for copy in self._z():
                copy.start()

    def last(self):
        @pl.when(self.half == self.pos.core)
        def _():
            for copy in self._z():
                copy.wait_recv()
            for copy in self._x():
                copy.start()

    def finish(self):
        @pl.when(self.half == self.pos.core)
        def _():
            for copy in self._z() + self._x():
                copy.wait_send()

        @pl.when(self.half != self.pos.core)
        def _():
            self._sib().wait_send()

        for i, copy in enumerate(self._x()):
            back = lax.rem(self.pos.x + 3 - i, 4)

            @pl.when(lax.div(back, 2) == self.pos.core)
            def _(copy=copy):
                copy.wait_recv()


def first_kernel(
    tok_ref, wqkv_ref, wgu_ref, wdn_ref, wout_ref, gains_ref,
    qkv_ref, nf_ref, wqf_ref, wr_ref, wol_ref, wq_ref, n_ref, send, recv, local,
):
    pos, net = Place(), Net(send, recv, local)
    tpeers, xpeers, zpeers = pos.tpeers(), pos.xpeers(), pos.zpeers()
    greet(tpeers + xpeers + zpeers)
    x, y, zlo, zhi, core = pos.x, pos.y, pos.zlo, pos.zhi, pos.core

    gain = gains_ref[...].astype(BF).astype(F32)
    w = (wqkv_ref[...].astype(BF).astype(F32) * gain[:, 0:1]).astype(BF)
    for yy in range(4):
        for cc in range(2):
            heads = [(cc * 4 + d) * 4 + yy for d in range(4)]
            for c in range(2):
                heads += [32 + cc * 2 + c, 36 + cc * 2 + c]
            cut = [w[:, h * HEAD : (h + 1) * HEAD] for h in heads]
            wq_ref[yy * 2 + cc] = jnp.concatenate(cut, axis=1)

    small = []
    for peer in tpeers:
        t = peer["y"] * 2 + peer["core"]
        small.append(net.go(wq_ref.at[t], wqf_ref.at[x, zlo, y, zhi, core], peer))
    mine = net.local(wq_ref.at[pos.t], wqf_ref.at[x, zlo, y, zhi, core])

    def norm(row, at):
        rows = pl.ds(row, 16)
        r = tok_ref[rows].astype(F32)
        inv = lax.rsqrt(jnp.mean(r * r, axis=-1, keepdims=True) + norm_eps)
        n_ref[rows] = (r * inv).astype(BF)

    each16(0, 128, norm)
    gather = Gather(net, pos, n_ref, nf_ref)
    gather.start()

    mine.wait()
    for copy in small:
        copy.wait_recv()
    one = []
    for peer in xpeers:
        part = wqf_ref.at[x, zlo, pl.ds(0, 2), zhi]
        one.append(net.go(part, part, peer))
    for peer in zpeers:
        part = wqf_ref.at[x, zlo, pl.ds(2, 2), zhi]
        one.append(net.go(part, part, peer))
    for copy in one:
        copy.wait_recv()
    spread = Spread(net, pos, None, None, [(None, wqf_ref)])
    spread.start()

    wol_ref[...] = wout_ref[...].astype(BF)
    for t in range(8):
        for i, (src, first) in enumerate(((wgu_ref, 0), (wgu_ref, FF), (wdn_ref, 0))):
            part = src[:, first + t * SEG : first + (t + 1) * SEG].astype(BF)
            if i < 2:
                part = (part.astype(F32) * gain[:, 1:2]).astype(BF)
            wr_ref[t, i] = part
    gather.step()
    spread.step()
    gather.last()
    spread.arrive()
    gather.have(0, 1, 2, 3, 4)

    @pl.loop(0, 4)
    def _(i):
        w = wqf_ref[...].reshape(D, QKV)
        a = nf_ref[pl.ds(i * 2, 2)].reshape(256, D)
        qkv_ref[pl.ds(pl.multiple_of(i * 256, 256), 256)] = dot_nn(a, w).astype(BF)

    for copy in small + one:
        copy.wait_send()
    gather.finish()
    spread.finish()


def run_first(tok, wqkv, wgu, wdn, wout, gains):
    return pl.pallas_call(
        first_kernel,
        out_shape=(
            shaped(1024, QKV),
            shaped(8, 128, D),
            shaped(4, 2, 4, 2, 2, 16, QKV),
            shaped(8, 3, 16, SEG),
            shaped(16, D),
        ),
        in_specs=[VM] * 6,
        out_specs=(VM,) * 5,
        scratch_shapes=[pltpu.VMEM((8, 16, QKV), BF), pltpu.VMEM((128, D), BF)]
        + sems(7 + 6 + 8 + 4 + GATHER_SEMS, 2),
        compiler_params=pltpu.CompilerParams(
            collective_id=0, has_side_effects=True, vmem_limit_bytes=VLIMIT
        ),
        name="first",
    )(tok, wqkv, wgu, wdn, wout, gains)


def dot_nt(a, b):
    return lax.dot_general(a, b, (((1,), (1,)), ((), ())), preferred_element_type=F32)


def dot_tn(a, b):
    return lax.dot_general(a, b, (((0,), (0,)), ((), ())), preferred_element_type=F32)


def dot_nn(a, b):
    return lax.dot_general(a, b, (((1,), (0,)), ((), ())), preferred_element_type=F32)


def first_half_mask(shape):
    return (lax.broadcasted_iota(jnp.int32, shape, 1) & 63) < 32


def turn(u, cos, sin):
    rot = jnp.where(first_half_mask(u.shape), -pltpu.roll(u, 96, 1), pltpu.roll(u, 32, 1))
    return u * cos + rot * sin


def turn_back(u, cos, sin):
    v = u * sin
    rot = jnp.where(first_half_mask(u.shape), pltpu.roll(v, 96, 1), -pltpu.roll(v, 32, 1))
    return u * cos + rot


def lane_first(shape):
    return lax.broadcasted_iota(jnp.int32, shape, 1) < 64


def causal(zhi):
    key = lax.broadcasted_iota(jnp.int32, (512, 512), 0)
    query = (lax.broadcasted_iota(jnp.int32, (512, 512), 1) & 255) + zhi * 256
    return key <= query


def attend_kernel(
    qkv_ref, wout_ref, wr_ref, cot_ref, cos_in, sin_in,
    o_ref, lse_ref, q_ref, kv_ref, ra_ref, rb_ref, wo_ref, cotf_ref,
    k_ref, v_ref, own_ref, cos_ref, sin_ref, send, recv, local,
):
    pos, net = Place(), Net(send, recv, local)
    zhi = pos.zhi
    tables = [net.local(cos_in.at[zhi], cos_ref), net.local(sin_in.at[zhi], sin_ref)]
    greet(pos.tpeers() + pos.xpeers() + pos.zpeers())
    gather = Gather(net, pos, cot_ref, cotf_ref)
    cross = Cross(net, pos, wr_ref, own_ref, ra_ref, rb_ref)
    cross.start()
    rows = OutRows(net, pos, wout_ref, wo_ref)
    rows.start()

    for copy in tables:
        copy.wait()
    swap = net.block(4)
    for j in range(4):
        r = pl.ds(j * 256, 256)
        cos, sin = cos_ref[r], sin_ref[r]
        for c in range(2):
            kv = qkv_ref[r, 256 + c * 128 : 384 + c * 128].astype(F32)
            mixed = jnp.where(lane_first(kv.shape), turn(kv, cos, sin), kv)
            kv_ref[j, zhi, :, c * 128 : (c + 1) * 128] = mixed.astype(BF)
        if j == 0:
            rows.step()
        net.go(kv_ref.at[j, zhi], kv_ref.at[j, zhi], pos.zpart, swap + j)
    cross.step()
    gather.start()
    for j in range(4):
        r = pl.ds(j * 256, 256)
        cos, sin = cos_ref[r], sin_ref[r]
        for c in range(2):
            q = turn(qkv_ref[r, c * 128 : (c + 1) * 128].astype(F32), cos, sin)
            q = q.astype(BF) * jnp.asarray(HEAD**-0.5, BF)
            q_ref[j, c, 0:256] = q[:, 0:64]
            q_ref[j, c, 256:512] = q[:, 64:128]
        if j == 0:
            rows.last()

    def update(c, key_at, query, state, mask):
        top, norm, acc = state
        s = dot_nt(k_ref[c, key_at], query)
        if mask is not None:
            s = jnp.where(mask, s, mask_fill)
        new = jnp.maximum(top, jnp.max(s, axis=0, keepdims=True))
        p = jnp.exp(s - new)
        keep = jnp.exp(top - new)
        norm = norm * keep + jnp.sum(p, axis=0, keepdims=True)
        acc = acc * keep + dot_tn(v_ref[c, key_at], p.astype(BF))
        return new, norm, acc

    def block(qb, _):
        part = kv_ref.at[qb, zhi]
        net.make(part, part, pos.zpart, swap + qb).wait_recv()
        kv = kv_ref[qb].reshape(512, 256)
        for c in range(2):
            k_ref[c, qb] = kv[:, c * 128 : c * 128 + 64]
            v_ref[c, qb] = kv[:, c * 128 + 64 : c * 128 + 128]
        mask = causal(zhi)
        state = []
        for c in range(2):
            zero = (
                jnp.full((1, 512), mask_fill, F32),
                jnp.zeros((1, 512), F32),
                jnp.zeros((64, 512), F32),
            )
            state.append(update(c, qb, q_ref[qb, c], zero, mask))

        def more(j, held):
            return tuple(update(c, j, q_ref[qb, c], held[c], None) for c in range(2))

        state = lax.fori_loop(0, qb, more, tuple(state))
        for c in range(2):
            top, norm, acc = state[c]
            lse_ref[qb, c] = top + jnp.log(norm)
            out = (acc / norm).T
            pair = jnp.concatenate([out[0:256], out[256:512]], axis=1)
            o_ref[qb, :, c * 128 : (c + 1) * 128] = pair.astype(BF)
        return 0

    block(0, 0)
    block(1, 0)
    gather.step()
    block(2, 0)
    gather.last()
    block(3, 0)
    gather.have(0, 1, 2, 3, 4)
    gather.finish()
    cross.finish()
    rows.finish()
    for j in range(4):
        part = kv_ref.at[j, zhi]
        net.make(part, part, pos.zpart, swap + j).wait_send()


def run_attend(qkv, wout, wr_blocks, cot, cos, sin):
    return pl.pallas_call(
        attend_kernel,
        out_shape=(
            shaped(4, 256, 256),
            shaped(4, 2, 1, 512, dtype=F32),
            shaped(4, 2, 512, 64),
            shaped(4, 2, 256, 256),
            shaped(3, 4, 2, 2, 16, SEG),
            shaped(3, 2, 2, 2, 2, 16, SEG),
            shaped(2, 2, 2, 2, 16, D),
            shaped(8, 128, D),
        ),
        in_specs=[VM] * 4 + [ANY] * 2,
        out_specs=(VM, VM, VM, VM, ANY, ANY, ANY, ANY),
        scratch_shapes=[
            pltpu.VMEM((2, 4, 512, 64), BF),
            pltpu.VMEM((2, 4, 512, 64), BF),
            pltpu.VMEM((3, 4, 2, 16, SEG), BF),
            pltpu.VMEM((1024, 128), F32),
            pltpu.VMEM((1024, 128), F32),
        ]
        + sems(4 + 13 + 7 + GATHER_SEMS, 7),
        compiler_params=pltpu.CompilerParams(
            collective_id=1, has_side_effects=True, vmem_limit_bytes=VLIMIT
        ),
        name="attend",
    )(qkv, wout, wr_blocks, cot, cos, sin)


class Fold:
    def __init__(self, net, pos, src, scratch, sums, scratch_two):
        self.net, self.pos, self.src = net, pos, src
        self.ring = scratch
        self.sa, self.sb = sums
        if scratch_two is not None:
            self.ta, self.tb = scratch_two
        low, high = pl.ds(0, 2), pl.ds(2, 2)
        zp, xp = pos.zpeers(), pos.xpeers()
        if src is not None:
            self.axes = (
                ([src.at[:, p["zlo"], low, p["zhi"]] for p in zp], (low, high), zp),
                ([src.at[p["x"], :, high, :] for p in xp], (pl.ds(0, 1), pl.ds(1, 1)), xp),
            )

    def start(self):
        net, pos = self.net, self.pos
        self.one, self.two = [], []
        for (blocks, (lo, hi), peers), (opp, _, nb) in zip(self.axes, self.ring):
            up, far, down = blocks
            self.one.append(
                [
                    net.go(far.at[lo], opp.at[0], peers[0]),
                    net.go(far.at[hi], opp.at[1], peers[2]),
                    net.go(up.at[hi], nb.at[0, hi], peers[0]),
                    net.go(down.at[lo], nb.at[1, lo], peers[2]),
                ]
            )
        low, high = pl.ds(0, 2), pl.ds(2, 2)
        self.keep = [
            net.local(self.src.at[:, pos.zlo, low, pos.zhi], self.sa),
            net.local(self.src.at[pos.x, :, high, :], self.sb),
        ]

    def step(self):
        net = self.net
        for n, ((blocks, (lo, hi), peers), (opp, stage, nb), one) in enumerate(
            zip(self.axes, self.ring, self.one)
        ):
            up, _, down = blocks
            count = 2 - n

            for k, (block, cut, peer) in enumerate(((up, lo, peers[0]), (down, hi, peers[2]))):
                one[k].wait_recv()
                mine = block.at[cut]
                for i in range(count):
                    for j in range(2):
                        both = mine[i, j].astype(F32) + opp[k, i, j].astype(F32)
                        stage[k, i, j] = both.astype(BF)
                self.two.append(net.go(stage.at[k], nb.at[k, cut], peer))

    def add(self):
        for copy in self.keep:
            copy.wait()
        for one in self.one:
            for copy in one[2:]:
                copy.wait_recv()
        for copy in self.two:
            copy.wait_recv()
        (_, _, na), (_, _, nb) = self.ring

        @pl.loop(0, 4)
        def _(i):
            for j in range(2):
                here = self.sa[i, j].astype(F32) + na[0, i, j].astype(F32)
                self.sa[i, j] = (here + na[1, i, j].astype(F32)).astype(BF)
            lo, hi = lax.div(i, 2), lax.rem(i, 2)
            for j in range(2):
                here = self.sb[lo, j, hi].astype(F32) + nb[0, lo, j, hi].astype(F32)
                self.sb[lo, j, hi] = (here + nb[1, lo, j, hi].astype(F32)).astype(BF)

        for one in self.one:
            for copy in one:
                copy.wait_send()
        for copy in self.two:
            copy.wait_send()

    def second(self):
        net, pos = self.net, self.pos
        self.three = []
        for i, (za, xb) in enumerate(zip(pos.zpeers(), pos.xpeers())):
            self.three.append(net.go(self.sa.at[xb["x"]], self.ta.at[i], xb))
            self.three.append(net.go(self.sb.at[za["zlo"], :, za["zhi"]], self.tb.at[i], za))

    def finish(self, out, own=None):
        pos = self.pos
        if own is None:
            own = (self.sa.at[pos.x], self.sb.at[pos.zlo, :, pos.zhi])
        for copy in self.three:
            copy.wait_recv()
        for j in range(2):
            here = own[0][j].astype(F32)
            for k in range(3):
                here += self.ta[k, j].astype(F32)
            out[j] = here.astype(BF)
            here = own[1][j].astype(F32)
            for k in range(3):
                here += self.tb[k, j].astype(F32)
            out[2 + j] = here.astype(BF)
        for copy in self.three:
            copy.wait_send()


FOLD_ONE, FOLD_TWO = 12, 6


def fold_one(cols):
    return [
        pltpu.VMEM((2, 2, 2, 2, 16, cols), BF),
        pltpu.VMEM((2, 2, 2, 2, 16, cols), BF),
        pltpu.VMEM((2, 4, 2, 2, 16, cols), BF),
        pltpu.VMEM((2, 1, 2, 2, 2, 16, cols), BF),
        pltpu.VMEM((2, 1, 2, 2, 2, 16, cols), BF),
        pltpu.VMEM((2, 2, 2, 2, 2, 16, cols), BF),
    ]


def fold_sums(cols):
    return [pltpu.VMEM((4, 2, 2, 16, cols), BF), pltpu.VMEM((2, 2, 2, 2, 16, cols), BF)]


def fold_two(cols):
    return [pltpu.VMEM((3, 2, 2, 16, cols), BF), pltpu.VMEM((3, 2, 2, 16, cols), BF)]


def by_axis(refs):
    return tuple(refs[0:3]), tuple(refs[3:6])


def ffn_kernel(
    o_ref, wo_ref, tok_ref, cot_ref, ra_ref, rb_ref, cot_in,
    resid_ref, dmid_ref, full_ref, sumd_ref, sga_ref, sgb_ref, down_out, gu_out,
    wg_ref, wu_ref, wd_ref, n_ref, cotf_ref, dg_ref, du_ref, hid_ref, part_ref, blk,
    gd_ref, gg_ref, gu_ref, *rest,
):
    scr, folds, rest = (rest[:5], rest[5:10]), rest[10:26], rest[26:]
    pos, net = Place(), Net(*rest)
    bring = net.local(cot_in, cotf_ref)
    greet([pos.sib, pos.right, pos.left] + pos.xpeers() + pos.zpeers())
    sp_d, sp_g, sp_u = (
        Spread(net, pos, ra_ref, rb_ref, [item]) for item in ((2, wd_ref), (0, wg_ref), (1, wu_ref))
    )
    for sp in (sp_d, sp_g, sp_u):
        sp.start()

    def halves():
        return [Scatter(net, pos, part_ref, scr[h], h * 64, 64) for h in range(2)]

    def project(y):
        @pl.loop(0, 4)
        def _(i):
            cols = pl.ds(pl.multiple_of(i * 512, 512), 512)
            part_ref[y, :, cols] = dot_nn(o_ref[y], wo_ref[:, cols]).astype(BF)

    first = halves()
    reduce(first, pos, project)
    gather = [Gather(net, pos, blk, n_ref, h * 64, 64) for h in range(2)]
    for h, sc in enumerate(first):
        sc.arrive()

        def norm(row, at, sc=sc):
            rows = pl.ds(row, 16)
            r = sc.total(at) + tok_ref[rows].astype(F32)
            resid_ref[rows] = r
            inv = lax.rsqrt(jnp.mean(r * r, axis=-1, keepdims=True) + norm_eps)
            blk[rows] = (r * inv).astype(BF)

        each16(h * 64, 64, norm)
        gather[h].start()

    def whole(ref):
        return ref[...].reshape(D, SEG)

    def spans(y):
        return pl.ds(pl.multiple_of(y * 256, 256), 256)

    def feed(dy):
        y = pos.ys(dy)
        rows = spans(y)
        n = n_ref[pl.ds(y * 2, 2)].reshape(256, D)
        gate, up = dot_nn(n, whole(wg_ref)), dot_nn(n, whole(wu_ref))
        d_hidden = dot_nn(cotf_ref[pl.ds(y * 2, 2)].reshape(256, D), whole(wd_ref))
        sig = jax.nn.sigmoid(gate)
        silu = gate * sig
        hid_ref[rows] = (silu * up).astype(BF)
        dg_ref[rows] = (d_hidden * up * sig * (1.0 + gate * (1.0 - sig))).astype(BF)
        du_ref[rows] = (d_hidden * silu).astype(BF)

    sp_d.step()
    sp_g.step()
    sp_u.step()
    gather[0].step()
    gather[1].step()

    for sc in first:
        sc.finish()
    gather[0].last()
    gather[1].last()
    for g in gather:
        g.have(0, 1, 2, 3, 4)
        g.finish()
    bring.wait()
    for sp in (sp_d, sp_g, sp_u):
        sp.arrive()

    def regress(y):
        rows = pl.ds(pl.multiple_of(y * 256, 256), 256)

        @pl.loop(0, 4)
        def _(i):
            wrows = pl.ds(i, 1)
            w_g, w_u = (w[wrows].reshape(512, SEG) for w in (wg_ref, wu_ref))
            both = dot_nt(dg_ref[rows], w_g) + dot_nt(du_ref[rows], w_u)
            part_ref[y, :, pl.ds(pl.multiple_of(i * 512, 512), 512)] = both.astype(BF)

    def grad(left, right, out, first, last, base=0):
        @pl.loop(first, last)
        def _(i):
            cols = pl.ds(pl.multiple_of(i * 256, 256), 256)
            g = dot_tn(left[:, :, cols].reshape(1024, 256), right[...]).astype(BF)
            out[lax.div(i, 2) - base, lax.rem(i, 2)] = g.reshape(4, 2, 2, 16, SEG)

    second = halves()
    one, two = second
    fold = Fold(net, pos, gd_ref, by_axis(folds[:6]), folds[6:8], folds[8:10])
    fold_g = Fold(net, pos, gg_ref, by_axis(folds[10:]), (sga_ref, sgb_ref), None)

    def give(dy):
        feed(dy)
        regress(pos.ys(dy))
        one.give(dy)
        two.give(dy)

    give(2)
    one.far()
    two.far()
    give(1)
    one.right()
    two.right()
    give(3)
    one.left()
    two.left()
    one.last()
    give(0)
    two.last()
    grad(cotf_ref, hid_ref, gd_ref, 0, 4)
    gather = [Gather(net, pos, blk, full_ref, h * 64, 64) for h in range(2)]

    def norm_half(h):
        sc = second[h]
        sc.arrive()

        def norm(row, at):
            rows = pl.ds(row, 16)
            dmid = norm_back(sc.total(at), resid_ref[rows], cot_ref[rows].astype(F32))
            dmid_ref[rows] = dmid
            blk[rows] = dmid.astype(BF)

        each16(h * 64, 64, norm)
        gather[h].start()

    norm_half(0)
    grad(cotf_ref, hid_ref, gd_ref, 4, 8)
    fold.start()
    norm_half(1)
    grad(n_ref, dg_ref, gg_ref, 0, 4)
    gather[0].step()
    grad(n_ref, dg_ref, gg_ref, 4, 8)
    fold_g.start()
    gather[1].step()
    grad(n_ref, du_ref, gu_ref, 0, 4)
    half_u = net.local(gu_ref, gu_out.at[pl.ds(0, 2)])
    fold.step()
    gather[0].last()
    half_u.wait()
    grad(n_ref, du_ref, gu_ref, 4, 8, 2)
    keep = [net.local(gu_ref, gu_out.at[pl.ds(2, 2)])]
    gather[1].last()
    fold_g.step()
    for sc in second:
        sc.finish()

    def down(first, last):
        @pl.loop(first, last)
        def _(y):
            rows = pl.ds(pl.multiple_of(y * 256, 256), 256)

            @pl.loop(0, 4)
            def _(i):
                w = wd_ref[pl.ds(i, 1)].reshape(512, SEG)
                cols = pl.ds(pl.multiple_of(i * 512, 512), 512)
                part_ref[y, :, cols] = dot_nt(hid_ref[rows], w).astype(BF)

    down(0, 2)
    fold.add()
    fold.second()
    down(2, 4)
    keep.append(net.local(part_ref, down_out))
    fold_g.add()
    fold.finish(sumd_ref)
    for g in gather:
        g.have(0, 1, 2, 3, 4)
        g.finish()
    for sp in (sp_d, sp_g, sp_u):
        sp.finish()
    for copy in keep:
        copy.wait()


def run_ffn(o, wo, tok, cot, ra, rb, cotf):
    full = shaped(4, 2, 4, 2, 2, 16, SEG)
    whole = pltpu.VMEM((4, 2, 4, 2, 2, 16, SEG), BF)
    sums = (shaped(4, 2, 2, 16, SEG), shaped(2, 2, 2, 2, 16, SEG))
    return pl.pallas_call(
        ffn_kernel,
        out_shape=(
            shaped(128, D, dtype=F32),
            shaped(128, D, dtype=F32),
            shaped(8, 128, D),
            shaped(4, 2, 16, SEG),
            *sums,
            shaped(4, 256, D),
            full,
        ),
        in_specs=[VM] * 4 + [ANY] * 3,
        out_specs=(VM, VM, ANY, VM, VM, VM, ANY, ANY),
        scratch_shapes=[whole] * 3
        + [pltpu.VMEM((8, 128, D), BF)] * 2
        + [pltpu.VMEM((1024, SEG), BF)] * 3
        + [pltpu.VMEM((4, 256, D), BF), pltpu.VMEM((128, D), BF)]
        + [whole] * 2
        + [pltpu.VMEM((2, 2, 4, 2, 2, 16, SEG), BF)]
        + scatter_scratch(64) * 2
        + (fold_one(SEG) + fold_sums(SEG) + fold_two(SEG))
        + fold_one(SEG)
        + sems(4 * SCATTER_SEMS + 4 * GATHER_SEMS + 24 + 12 + 2 * FOLD_ONE + FOLD_TWO, 24),
        compiler_params=pltpu.CompilerParams(
            collective_id=2, has_side_effects=True, vmem_limit_bytes=VLIMIT
        ),
        name="ffn",
    )(o, wo, tok, cot, ra, rb, cotf)


class OutFold:
    def __init__(self, net, pos, src, scratch):
        self.net, self.pos, self.src = net, pos, src
        self.lx, self.sx, self.lz, self.sz, self.ls = scratch
        self.at = net.block(9)
        self.keep = net.loc.at[net.m]
        net.m += 1
        self.mine = lax.div(pos.x, 2) == pos.core

    def _x(self, xh):
        pos, net = self.pos, self.net
        src = self.src.at[pl.ds(xh * 2, 2)]
        return pltpu.make_async_remote_copy(
            src, self.lx.at[pos.x], net.send.at[self.at + xh], net.recv.at[self.at + pos.x],
            device_id={"x": pos.core * 2 + xh}, device_id_type=MESH,
        )

    def _own(self):
        xh = lax.rem(self.pos.x, 2)
        return pltpu.make_async_copy(
            self.src.at[pl.ds(xh * 2, 2)], self.lx.at[self.pos.x], self.keep
        )

    def _from_x(self, x):
        net = self.net
        return pltpu.make_async_remote_copy(
            self.src.at[pl.ds(0, 2)], self.lx.at[x], net.send.at[self.at], net.recv.at[self.at + x],
            device_id=self.pos.xpeers()[0], device_id_type=MESH,
        )

    def _z(self):
        net = self.net
        out = []
        for i, p in enumerate(self.pos.zpeers()):
            src = self.sx.at[p["zlo"], p["zhi"]]
            out.append(net.make(src, self.lz.at[i], p, self.at + 4 + i))
        return out

    def _sib(self):
        return self.net.make(self.sz.at[1 - self.pos.core], self.ls, self.pos.sib, self.at + 7)

    def start(self):
        for xh in range(2):
            here = self.pos.core * 2 + xh == self.pos.x

            @pl.when(here)
            def _():
                self._own().start()

            @pl.when(jnp.logical_not(here))
            def _(xh=xh):
                self._x(xh).start()

    def step(self):
        @pl.when(self.mine)
        def _():
            self._own().wait()
            for x in range(4):

                @pl.when(self.pos.x != x)
                def _(x=x):
                    self._from_x(x).wait_recv()

            for i in range(2):
                for j in range(2):
                    for k in range(2):
                        here = self.lx[0, i, j, k].astype(F32)
                        for x in range(1, 4):
                            here += self.lx[x, i, j, k].astype(F32)
                        self.sx[i, j, k] = here.astype(BF)
            for copy in self._z():
                copy.start()

    def last(self):
        @pl.when(self.mine)
        def _():
            pos = self.pos
            for copy in self._z():
                copy.wait_recv()
            for k in range(2):
                here = self.sx[pos.zlo, pos.zhi, k].astype(F32)
                for i in range(3):
                    here += self.lz[i, k].astype(F32)
                self.sz[k] = here.astype(BF)
            self._sib().start()

    def finish(self, out):
        for xh in range(2):
            here = self.pos.core * 2 + xh == self.pos.x

            @pl.when(jnp.logical_not(here))
            def _(xh=xh):
                self._x(xh).wait_send()

        @pl.when(self.mine)
        def _():
            for copy in self._z():
                copy.wait_send()
            self._sib().wait_send()
            out[...] = self.sz[self.pos.core].astype(F32)

        @pl.when(jnp.logical_not(self.mine))
        def _():
            self._sib().wait_recv()
            out[...] = self.ls[...].astype(F32)


def out_scratch():
    return [
        pltpu.VMEM((4, 2, 2, 2, 16, D), BF),
        pltpu.VMEM((2, 2, 2, 16, D), BF),
        pltpu.VMEM((3, 2, 16, D), BF),
        pltpu.VMEM((2, 16, D), BF),
        pltpu.VMEM((16, D), BF),
    ]


def tail_kernel(
    q_ref, kv_ref, lse_ref, o_ref, wo_ref, resid_ref, tok_ref, dmid_ref, wq_ref,
    cos_in, sin_in, dat_in, part_in, gu_in, n_in, sumd_in, sga_in, sgb_in,
    block_ref, dtok_ref, fo_ref, outq_ref, outr_ref,
    dqkv_ref, dat_ref, part_ref, gu_ref, go_ref, gq_ref, sumq_ref, sumr_ref, cos_ref, sin_ref,
    k_ref, v_ref, do2_ref, delta_ref, dq_ref, dk_ref, dv_ref, send_ref, got_ref, mine_ref,
    *rest,
):
    pos = Place()
    rest = list(rest)

    def take(count):
        out = rest[:count]
        del rest[:count]
        return out

    one_u, sums_u, two_u = take(6), take(2), take(2)
    one_q, sums_q, two_q = take(6), take(2), take(2)
    own_g, two_g = take(2), take(2)
    land, scr_a, scr_b = take(5), [take(5), take(5)], [take(5), take(5)]
    net = Net(*rest)
    zhi = pos.zhi
    bring = [net.local(dat_in.at[pl.ds(j * 2, 2)], dat_ref.at[pl.ds(j * 2, 2)]) for j in range(4)]
    bring_part, bring_gu = net.local(part_in, part_ref), net.local(gu_in, gu_ref)
    get = [net.local(cos_in.at[zhi], cos_ref), net.local(sin_in.at[zhi], sin_ref)]
    get.append(net.local(sga_in.at[pos.x], own_g[0]))
    get.append(net.local(sgb_in.at[pos.zlo, :, pos.zhi], own_g[1]))
    tpeers = pos.tpeers()
    greet(tpeers + pos.xpeers() + pos.zpeers())
    one, two = halves = [Scatter(net, pos, part_ref, scr_a[h], h * 64, 64) for h in range(2)]
    fold = Fold(net, pos, gu_ref, by_axis(one_u), sums_u, two_u)
    fold_q = Fold(net, pos, gq_ref, by_axis(one_q), sums_q, two_q)
    fold_g = Fold(net, pos, None, None, (sga_in, sgb_in), two_g)
    rows = OutFold(net, pos, go_ref, land)
    fold_g.second()
    ship, keep = [], []

    def send_off(i, src):
        for peer in tpeers:
            ship.append(net.go(src.at[peer["y"], peer["core"]], outr_ref.at[pos.t, i], peer))
        keep.append(net.local(src.at[pos.y, pos.core], outr_ref.at[pos.t, i]))

    send_off(2, sumd_in)

    for j in range(4):
        kv = kv_ref[j].reshape(512, 256)
        bring[j].wait()
        d_o = dot_nt(dat_ref[pl.ds(j * 2, 2)].reshape(256, D), wo_ref[...]).astype(BF)
        for c in range(2):
            k_ref[c, j] = kv[:, c * 128 : c * 128 + 64]
            v_ref[c, j] = kv[:, c * 128 + 64 : c * 128 + 128]
            cols = slice(c * 128, (c + 1) * 128)
            do = d_o[:, cols]
            do2_ref[j, c, 0:256] = do[:, 0:64]
            do2_ref[j, c, 256:512] = do[:, 64:128]
            both = (do.astype(F32) * o_ref[j, :, cols].astype(F32)).T
            delta_ref[j, c] = jnp.concatenate(
                [
                    jnp.sum(both[0:64], axis=0, keepdims=True),
                    jnp.sum(both[64:128], axis=0, keepdims=True),
                ],
                axis=1,
            )
    bring_gu.wait()
    fold.start()
    bring_part.wait()
    for dy in (2, 1, 3, 0):
        one.give(dy)
        two.give(dy)

    @pl.loop(0, 4)
    def _(i):
        cols = pl.ds(pl.multiple_of(i * 512, 512), 512)
        left = o_ref[...].reshape(1024, 256)
        g = dot_tn(left, dat_ref[:, :, cols].reshape(1024, 512)).astype(BF)
        go_ref[:, :, :, :, cols] = g.reshape(4, 2, 2, 16, 512)

    bring_n = net.local(n_in, dat_ref)
    rows.start()
    one.far()
    one.right()
    one.left()
    two.far()
    dq_ref[...] = jnp.zeros_like(dq_ref)

    swap = net.block(4)

    def pair(c, j, qb, mask):
        k, v, q, do = k_ref[c, j], v_ref[c, j], q_ref[qb, c], do2_ref[qb, c]
        p = jnp.exp(dot_nt(k, q) - lse_ref[qb, c])
        if mask is not None:
            p = jnp.where(mask, p, 0.0)
        ds = (p * (dot_nt(v, do) - delta_ref[qb, c])).astype(BF)
        dv = dot_nn(p.astype(BF), do)
        dk = dot_nn(ds, q)
        dq_ref[qb, c] += dot_tn(k, ds)
        return dk, dv

    def column(j):
        mask = causal(zhi)
        for c in range(2):
            dk, dv = pair(c, j, j, mask)
            dk_ref[c] = dk
            dv_ref[c] = dv

        def more(qb, _):
            for c in range(2):
                dk, dv = pair(c, j, qb, None)
                dk_ref[c] += dk
                dv_ref[c] += dv
            return 0

        lax.fori_loop(j + 1, 4, more, 0)
        both = jnp.concatenate([dk_ref[0], dv_ref[0], dk_ref[1], dv_ref[1]], axis=1)
        both = both.reshape(2, 256, 256)

        @pl.when(zhi == 0)
        def _():
            mine_ref[j] = both[0]
            send_ref[j] = both[1].astype(BF)

        @pl.when(zhi == 1)
        def _():
            mine_ref[j] = both[1]
            send_ref[j] = both[0].astype(BF)

        net.go(send_ref.at[j], got_ref.at[j], pos.zpart, swap + j)

    def queries(j):
        r = pl.ds(j * 256, 256)
        cos, sin = cos_ref[r], sin_ref[r]
        for c in range(2):
            dq = dq_ref[j, c].T * HEAD**-0.5
            dq = jnp.concatenate([dq[0:256], dq[256:512]], axis=1)
            dqkv_ref[r, c * 128 : (c + 1) * 128] = turn_back(dq, cos, sin).astype(BF)

    def keys(j):
        r = pl.ds(j * 256, 256)
        cos, sin = cos_ref[r], sin_ref[r]
        net.make(send_ref.at[j], got_ref.at[j], pos.zpart, swap + j).wait()
        for c in range(2):
            cols = slice(c * 128, (c + 1) * 128)
            dkv = mine_ref[j, :, cols] + got_ref[j, :, cols].astype(F32)
            dkv = jnp.where(lane_first(dkv.shape), turn_back(dkv, cos, sin), dkv)
            dqkv_ref[r, 256 + c * 128 : 384 + c * 128] = dkv.astype(BF)

    column(0)
    one.last()
    two.right()
    two.left()
    for copy in get:
        copy.wait()
    queries(0)
    column(1)
    two.last()
    rows.step()
    queries(1)
    keys(0)
    fold.step()
    column(2)
    rows.last()
    queries(2)
    keys(1)
    fold_g.finish(sumr_ref.at[0], own_g)
    send_off(0, sumr_ref.at[0])
    column(3)
    queries(3)
    fold.add()
    fold.second()
    for h, sc in enumerate(halves):
        sc.arrive()

        def block(row, at, sc=sc):
            r = pl.ds(row, 16)
            block_ref[r] = (sc.total(at) + resid_ref[r]).astype(BF)

        each16(h * 64, 64, block)

    for sc in halves:
        sc.finish()
    bring_n.wait()

    def grad(at, count):
        @pl.loop(0, 8)
        def _(i):
            cols = pl.ds(pl.multiple_of(i * 256, 256), 256)
            left = dat_ref[:, :, cols].reshape(1024, 256)
            g = dot_tn(left, dqkv_ref[:, at : at + count]).astype(BF)
            out = gq_ref.at[lax.div(i, 2), lax.rem(i, 2)]
            out[:, :, :, :, at : at + count] = g.reshape(4, 2, 2, 16, count)

    keys(2)
    grad(0, 256)
    keys(3)
    one, two = halves = [Scatter(net, pos, part_ref, scr_b[h], h * 64, 64) for h in range(2)]

    def give(dy):
        y = pos.ys(dy)
        span = pl.ds(pl.multiple_of(y * 256, 256), 256)

        @pl.loop(0, 4)
        def _(i):
            cols = pl.ds(pl.multiple_of(i * 512, 512), 512)
            part_ref[y, :, cols] = dot_nt(dqkv_ref[span], wq_ref[cols]).astype(BF)

        one.give(dy)
        two.give(dy)

    give(2)
    give(1)
    one.far()
    grad(256, 256)
    fold_q.start()
    give(3)
    one.right()
    one.left()
    give(0)
    two.far()
    fold.finish(sumr_ref.at[1])
    send_off(1, sumr_ref.at[1])
    one.last()
    two.right()
    two.left()
    fold_q.step()
    two.last()
    rows.finish(fo_ref)
    fold_q.add()
    fold_q.second()

    def half(h):
        sc = halves[h]
        sc.arrive()

        def token(row, at):
            span = pl.ds(row, 16)
            r = tok_ref[span].astype(F32)
            dtok_ref[span] = norm_back(sc.total(at), r, dmid_ref[span]).astype(BF)

        each16(h * 64, 64, token)

    half(0)
    fold_q.finish(sumq_ref)
    for peer in tpeers:
        ship.append(net.go(sumq_ref.at[peer["y"], peer["core"]], outq_ref.at[pos.t], peer))
    keep.append(net.local(sumq_ref.at[pos.y, pos.core], outq_ref.at[pos.t]))
    half(1)
    for copy in ship + keep:
        copy.wait()
    for sc in halves:
        sc.finish()


def run_tail(*args):
    sums = fold_sums(SEG)
    return pl.pallas_call(
        tail_kernel,
        out_shape=(
            shaped(128, D),
            shaped(128, D),
            shaped(16, D, dtype=F32),
            shaped(8, 16, QKV),
            shaped(8, 3, 16, SEG),
        ),
        in_specs=[VM] * 9 + [ANY] * 9,
        out_specs=(VM, VM, VM, ANY, ANY),
        scratch_shapes=[
            pltpu.VMEM((1024, QKV), BF),
            pltpu.VMEM((8, 128, D), BF),
            pltpu.VMEM((4, 256, D), BF),
            pltpu.VMEM((4, 2, 4, 2, 2, 16, SEG), BF),
            pltpu.VMEM((4, 2, 2, 16, D), BF),
            pltpu.VMEM((4, 2, 4, 2, 2, 16, QKV), BF),
            pltpu.VMEM((4, 2, 16, QKV), BF),
            pltpu.VMEM((2, 4, 2, 16, SEG), BF),
            pltpu.VMEM((1024, 128), F32),
            pltpu.VMEM((1024, 128), F32),
            pltpu.VMEM((2, 4, 512, 64), BF),
            pltpu.VMEM((2, 4, 512, 64), BF),
            pltpu.VMEM((4, 2, 512, 64), BF),
            pltpu.VMEM((4, 2, 1, 512), F32),
            pltpu.VMEM((4, 2, 64, 512), F32),
            pltpu.VMEM((2, 512, 64), F32),
            pltpu.VMEM((2, 512, 64), F32),
            pltpu.VMEM((4, 256, 256), BF),
            pltpu.VMEM((4, 256, 256), BF),
            pltpu.VMEM((4, 256, 256), F32),
        ]
        + (fold_one(SEG) + sums + fold_two(SEG))
        + (fold_one(QKV) + fold_sums(QKV) + fold_two(QKV))
        + ([pltpu.VMEM((2, 2, 16, SEG), BF)] * 2 + fold_two(SEG))
        + out_scratch()
        + scatter_scratch(64) * 4
        + sems(4 + 2 * FOLD_ONE + 3 * FOLD_TWO + 9 + 4 * SCATTER_SEMS + 28, 22),
        compiler_params=pltpu.CompilerParams(
            collective_id=4, has_side_effects=True, vmem_limit_bytes=VLIMIT
        ),
        name="tail",
    )(*args)


def rope_tables():
    half = HEAD // 2
    freq = np.exp(np.arange(half, dtype=np.float32) * np.float32(-2.0 * math.log(rope_base) / HEAD))
    spots = np.arange(2048, dtype=np.float32).reshape(4, 2, 256).transpose(1, 0, 2).reshape(2, 1024)
    angles = (spots[:, :, None] * freq.astype(np.float32)).astype(np.float32)
    angles = np.concatenate([angles] * 4, axis=2)
    return np.cos(angles).astype(np.float32), np.sin(angles).astype(np.float32)


def adam(weight, gradient, first_moment, second, step_rate, decay_weight):
    first_new = beta_one * first_moment + (1.0 - beta_one) * gradient
    second_new = beta_two * second + (1.0 - beta_two) * gradient * gradient
    first_hat = first_new / (1.0 - beta_one**STEP)
    second_hat = second_new / (1.0 - beta_two**STEP)
    weight_new = weight - step_rate * (
        first_hat / (jnp.sqrt(second_hat) + adam_eps) + decay_weight * weight
    )
    return (first_new, second_new, weight_new)


def local(
    tokens, cotangent, w_qkv, w_out, w_gate_up, w_down_t, gains,
    first_qkv, second_qkv, first_out, second_out, first_gate_up, second_gate_up,
    first_down, second_down, first_gains, second_gains,
):
    tok, cot = tokens[0], cotangent[0]
    gain = gains.astype(BF).astype(F32)
    low_qkv = w_qkv.astype(BF).astype(F32)
    low_gu = w_gate_up.astype(BF).astype(F32)
    cos, sin = (jnp.asarray(table) for table in rope_tables())
    qkv, n_in, wq, wr_blocks, wout = run_first(tok, w_qkv, w_gate_up, w_down_t, w_out, gains)
    wq = wq.reshape(D, QKV)
    o, lse, q, kv, ra, rb, wo, cotf = run_attend(
        qkv, wout, wr_blocks, cot, cos, sin
    )
    wo = wo.reshape(256, D)
    resid, d_mid, d_attn, sumd, sga, sgb, part_b, gu = run_ffn(
        o, wo, tok, cot, ra, rb, cotf
    )
    block_out, d_tokens, grad_out, sum_q, sum_r = run_tail(
        q, kv, lse, o, wo, resid, tok, d_mid, wq,
        cos, sin, d_attn, part_b, gu, n_in, sumd, sga, sgb,
    )

    sum_q = sum_q.reshape(4, 2, 16, QKV).astype(F32)
    grad_q = sum_q[..., :256].reshape(4, 2, 16, 4, HEAD).transpose(2, 1, 3, 0, 4).reshape(16, D)
    grad_kv = jnp.sum(sum_q[..., 256:], axis=0).reshape(2, 16, 2, 2, HEAD)
    grad_kv = grad_kv.transpose(1, 3, 0, 2, 4).reshape(16, 512)
    raw_qkv = jnp.concatenate([grad_q, grad_kv], axis=1)
    sum_r = sum_r.astype(F32)
    raw_gu = sum_r[:, 0:2].transpose(2, 1, 0, 3).reshape(16, 2 * FF)
    grad_down = sum_r[:, 2].transpose(1, 0, 2).reshape(16, FF)
    grad_qkv = raw_qkv * gain[:, 0:1]
    grad_gu = raw_gu * gain[:, 1:2]
    grad_gains = jnp.stack(
        [jnp.sum(low_qkv * raw_qkv, axis=1), jnp.sum(low_gu * raw_gu, axis=1)], axis=1
    )

    first_q, second_q, weight_q = adam(w_qkv, grad_qkv, first_qkv, second_qkv, rate_matrix, decay_rate)
    first_o, second_o, weight_o = adam(w_out, grad_out, first_out, second_out, rate_matrix, decay_rate)
    first_g, second_g, weight_g = adam(
        w_gate_up, grad_gu, first_gate_up, second_gate_up, rate_matrix, decay_rate
    )
    first_d, second_d, weight_d = adam(
        w_down_t, grad_down, first_down, second_down, rate_matrix, decay_rate
    )
    first_n, second_n, weight_n = adam(gains, grad_gains, first_gains, second_gains, rate_gain, 0.0)
    return (
        block_out[None], d_tokens[None],
        first_q, second_q, weight_q, first_o, second_o, weight_o,
        first_g, second_g, weight_g, first_d, second_d, weight_d,
        first_n, second_n, weight_n,
    )


def solution(mesh):
    fine = Mesh(mesh.devices.reshape(4, 2, 4, 2, 2), ("x", "zlo", "y", "zhi", "core"))
    dp, seq = ("x", "zlo"), ("y", "zhi", "core")
    act, row = P(dp, seq, None), P(dp + seq, None)
    return jax.shard_map(
        local,
        mesh=fine,
        in_specs=(act, act) + (row,) * 15,
        out_specs=(act, act) + (row,) * 15,
        check_vma=False,
    )
```
